32 devices in a mesh: rep: 8 (over y, x, core), shard: 4 (over z).
Axes of the slice: x: 2, y: 2, z: 4, core: 2. Of those that a mesh axis runs over, the one named last changes fastest.
Arguments:
- tokens: bfloat16 [16, 2048, 768], P('rep', 'shard'), may hold values from -6 to 6
- cotangent: bfloat16 [16, 2048, 768], P('rep', 'shard'), may hold values from -6 to 6
- lengths: int32 [16], P('rep'), may hold values from 512 to 2048, as said below
- w_qkv: float32 [768, 2304], P('shard', 'rep'), may hold values from -0.21875 to 0.21875
- w_out: float32 [768, 768], P('shard', 'rep'), may hold values from -6 to 6
- w_gate_up: float32 [768, 6144], P('shard', 'rep'), may hold values from -0.21875 to 0.21875
- w_down: float32 [3072, 768], P('shard', 'rep'), may hold values from -0.109375 to 0.109375
- mom_qkv: float32 [768, 2304], P('shard', 'rep'), may hold values from -28 to 28
- mom_out: float32 [768, 768], P('shard', 'rep'), may hold values from -28 to 28
- mom_gate_up: float32 [768, 6144], P('shard', 'rep'), may hold values from -28 to 28
- mom_down: float32 [3072, 768], P('shard', 'rep'), may hold values from -28 to 28
- err_qkv: float32 [8, 768, 2304], P('rep', 'shard'), may hold values from -128 to 128
- err_out: float32 [8, 768, 768], P('rep', 'shard'), may hold values from -32 to 32
- err_gate_up: float32 [8, 768, 6144], P('rep', 'shard'), may hold values from -128 to 128
- err_down: float32 [8, 3072, 768], P('rep', 'shard'), may hold values from -128 to 128
- start_qkv: float32 [4, 2304, 8], P('shard'), may hold values from -6 to 6
- start_out: float32 [4, 768, 8], P('shard'), may hold values from -6 to 6
- start_gate_up: float32 [4, 6144, 8], P('shard'), may hold values from -6 to 6
- start_down: float32 [4, 768, 8], P('shard'), may hold values from -6 to 6
- layer_norm_gains: float32 [2, 768], replicated, may hold values from 0.5 to 1.5
- layer_norm_biases: float32 [2, 768], replicated, may hold values from -4 to 4
- norm_moments: float32 [4, 768], replicated, may hold values from -80 to 80
Outputs:
- mixed_out: bfloat16 [16, 2048, 768], P('rep', 'shard')
- input_grad: float32 [16, 2048, 768], P('rep', 'shard')
- new_qkv: float32 [768, 2304], P('shard', 'rep')
- new_out: float32 [768, 768], P('shard', 'rep')
- new_gate_up: float32 [768, 6144], P('shard', 'rep')
- new_down: float32 [3072, 768], P('shard', 'rep')
- moment_qkv: float32 [768, 2304], P('shard', 'rep')
- moment_out: float32 [768, 768], P('shard', 'rep')
- moment_gate_up: float32 [768, 6144], P('shard', 'rep')
- moment_down: float32 [3072, 768], P('shard', 'rep')
- error_qkv: float32 [8, 768, 2304], P('rep', 'shard')
- error_out: float32 [8, 768, 768], P('rep', 'shard')
- error_gate_up: float32 [8, 768, 6144], P('rep', 'shard')
- error_down: float32 [8, 3072, 768], P('rep', 'shard')
- basis_qkv: float32 [768, 8], P('shard')
- basis_out: float32 [768, 8], P('shard')
- basis_gate_up: float32 [768, 8], P('shard')
- basis_down: float32 [3072, 8], P('shard')
- factor_qkv: float32 [4, 2304, 8], P('shard')
- factor_out: float32 [4, 768, 8], P('shard')
- factor_gate_up: float32 [4, 6144, 8], P('shard')
- factor_down: float32 [4, 768, 8], P('shard')
- norm_moment_new: float32 [4, 768], replicated
- norm_new: float32 [4, 768], replicated
The draws below stay inside these ranges and needn't reach their ends.
Inputs may be any that keep to these rules, and one draw needn't show every extreme that they name: `lengths`: in each group of 2 consecutive entries, one entry, which one drawn from the seed, equals 2048.
All inputs are finite; a program needn't handle non-finite values.
Results may differ from the reference program's by a relative error of at most 0.03.
Values may be sent and summed in bfloat16 or wider, within the bound.
No kernel may reach another device: no remote copies, remote signals or barrier semaphores. Data moves between devices by JAX's collectives and lax.ppermute only.
A program may use at most 320 MiB of HBM per device.

```python
import math
from functools import partial
import jax
import jax.numpy as jnp
from jax import lax

D = 768
H = 12
HD = 64
FF = 3072
SEQ = 2048
SEQ_GRP = 2
RANK = 8
GROUPS = 8
BLOCKS = 4
SEQS = 16


def draw_lengths(key, part):
    key = jax.random.fold_in(key, 11)
    group_count = SEQS // SEQ_GRP
    first_key, second_key = jax.random.split(key)
    ragged = jax.random.randint(first_key, (group_count, SEQ_GRP), SEQ // 4, SEQ + 1)
    chosen = jax.random.randint(second_key, (group_count, 1), 0, SEQ_GRP)
    full_slot = jnp.arange(SEQ_GRP, dtype=jnp.int32)[None, :] == chosen
    return jnp.where(full_slot, SEQ, ragged).reshape(SEQS).astype(jnp.int32)


def steps_of(own_key, shape, cuts, smallest, top_value):
    level = 1.0
    for axis_at, blocks in cuts:
        draws = jax.random.uniform(jax.random.fold_in(jax.random.fold_in(own_key, 6), axis_at), (blocks,), jnp.float32, smallest / len(cuts), top_value / len(cuts))
        level = level * jnp.repeat(jnp.exp(draws), shape[axis_at] // blocks).reshape((-1,) + (1,) * (len(shape) - 1 - axis_at))
    return level


def noise(stream_key, extent, scale, most, cuts=(), kind=jnp.bfloat16):
    drawn = jax.random.normal(stream_key, extent, jnp.float32) * scale
    if len(cuts) > 0:
        drawn = steps_of(stream_key, extent, cuts, -0.22, 0.18) * drawn
    return jnp.clip(drawn, min=-most, max=most).astype(kind)


def setup_inputs(seed: int = 0) -> dict:
    seeds = jax.random.split(jax.random.key(seed), 23)
    return {
        "tokens": noise(seeds[0], (SEQS, SEQ, D), 1.0, 6.0, ((0, 8), (1, 4))),
        "cotangent": noise(seeds[1], (SEQS, SEQ, D), 1.0, 6.0, ((0, 8), (1, 4))),
        "lengths": draw_lengths(jax.random.fold_in(seeds[22], 71), 0),
        "w_qkv": noise(seeds[3], (D, 3 * D), D ** -0.5, 0.21875, ((0, 4), (1, 8)), jnp.float32),
        "w_out": noise(seeds[4], (D, D), (max(1, 2 * D // SEQ)) ** -0.5, 6.0, ((0, 4), (1, 8)), jnp.float32),
        "w_gate_up": noise(seeds[5], (D, 2 * FF), D ** -0.5, 0.21875, ((0, 4), (1, 8)), jnp.float32),
        "w_down": noise(seeds[6], (FF, D), FF ** -0.5, 0.109375, ((0, 4), (1, 8)), jnp.float32),
        "mom_qkv": noise(seeds[7], (D, 3 * D), (SEQ ** 0.5 * 0.1), 28.0, ((0, 4), (1, 8)), jnp.float32),
        "mom_out": noise(seeds[8], (D, D), (SEQ ** 0.5 * 0.1), 28.0, ((0, 4), (1, 8)), jnp.float32),
        "mom_gate_up": noise(seeds[9], (D, 2 * FF), (SEQ ** 0.5 * 0.1), 28.0, ((0, 4), (1, 8)), jnp.float32),
        "mom_down": noise(seeds[10], (FF, D), (SEQ ** 0.5 * 0.1), 28.0, ((0, 4), (1, 8)), jnp.float32),
        "err_qkv": noise(seeds[11], (GROUPS, D, 3 * D), (SEQ ** 0.5 * 0.5), 128.0, ((0, 8), (1, 4)), jnp.float32),
        "err_out": noise(seeds[12], (GROUPS, D, D), (SEQ ** 0.5 * 0.12), 32.0, ((0, 8), (1, 4)), jnp.float32),
        "err_gate_up": noise(seeds[13], (GROUPS, D, 2 * FF), (SEQ ** 0.5 * 0.5), 128.0, ((0, 8), (1, 4)), jnp.float32),
        "err_down": noise(seeds[14], (GROUPS, FF, D), (SEQ ** 0.5 * 0.5), 128.0, ((0, 8), (1, 4)), jnp.float32),
        "start_qkv": noise(seeds[15], (BLOCKS, 3 * D, RANK), 1.0, 6.0, ((0, 4),), jnp.float32),
        "start_out": noise(seeds[16], (BLOCKS, D, RANK), 1.0, 6.0, ((0, 4),), jnp.float32),
        "start_gate_up": noise(seeds[17], (BLOCKS, 2 * FF, RANK), 1.0, 6.0, ((0, 4),), jnp.float32),
        "start_down": noise(seeds[18], (BLOCKS, D, RANK), 1.0, 6.0, ((0, 4),), jnp.float32),
        "layer_norm_gains": jnp.clip(1.0 + 0.1 * jax.random.normal(seeds[19], (2, D), jnp.float32), 0.5, 1.5),
        "layer_norm_biases": noise(seeds[20], (2, D), 0.3, 4.0, (), jnp.float32),
        "norm_moments": noise(seeds[21], (4, D), (SEQ ** 0.5 * 0.3), 80.0, (), jnp.float32),
    }


EPS = 1e-05
ROPE_BASE = 1000.0
MOMENTUM = 0.5
LEARN_RATES = (0.002, 0.1, 0.004, 0.002)
NORM_RATE = 0.01

@jax.custom_vjp
def low(v):
    return lax.optimization_barrier(v.astype(jnp.bfloat16)).astype(jnp.float32)

@jax.custom_vjp
def low_back(v):
    return v

def low_keep(v):
    return (low(v), None)

def low_pass(kept, grad):
    return (grad,)

def back_keep(v):
    return (v, None)

def back_low(kept, grad):
    return (low(grad),)
low.defvjp(low_keep, low_pass)
low_back.defvjp(back_keep, back_low)

def exact_dot(left, right):
    return jnp.dot(left, right, precision=lax.Precision.HIGHEST)

def layer_norm(values_in, gain, bias):
    centre = lax.optimization_barrier(jnp.mean(values_in, axis=-1, keepdims=True))
    centred = values_in - centre
    spread = lax.optimization_barrier(jnp.mean(centred * centred, axis=-1, keepdims=True))
    return centred * lax.rsqrt(spread + EPS) * gain + bias

def tables(count):
    position = jnp.arange(count, dtype=jnp.int32).astype(jnp.float32)
    inverse = jnp.exp(jnp.arange(HD // 2, dtype=jnp.int32).astype(jnp.float32) * (-2.0 * math.log(ROPE_BASE) / HD))
    angle = position[:, None] * inverse[None, :]
    return (jnp.cos(angle)[:, None, :], jnp.sin(angle)[:, None, :])

def rotary(values_in, cosine_table, sine_table):
    half_dim = values_in.shape[-1] // 2
    leading_half = values_in[..., :half_dim]
    second_half = values_in[..., half_dim:]
    return jnp.concatenate([leading_half * cosine_table - second_half * sine_table, second_half * cosine_table + leading_half * sine_table], axis=-1)

def attend(key_keep, inputs):
    query_rows, key_rows, value_rows = inputs
    scores = low_back(jnp.einsum('qd,kd->qk', query_rows, key_rows, precision=lax.Precision.HIGHEST) * HD ** (-0.5))
    scores = jnp.where(key_keep[None, :], scores, -1e+30)
    attn_probs = low(jax.nn.softmax(scores, axis=-1))
    return exact_dot(attn_probs, value_rows)

def one_sequence(token_rows, weights, layer_norm_gains, layer_norm_biases, key_keep):
    complete_query_key_value, complete_out_weight, complete_gate_up_weight, complete_down_weight = weights
    query_key_value_rows = low_back(exact_dot(token_rows, complete_query_key_value)).reshape(SEQ, 3, H, HD)
    cosine_table, sine_table = tables(SEQ)
    queries = low(rotary(query_key_value_rows[:, 0], cosine_table, sine_table)).transpose(1, 0, 2)
    keys_rot = low(rotary(query_key_value_rows[:, 1], cosine_table, sine_table)).transpose(1, 0, 2)
    values_all = low(query_key_value_rows[:, 2]).transpose(1, 0, 2)
    head_out = lax.map(jax.checkpoint(partial(attend, key_keep)), (queries, keys_rot, values_all))
    attn_mix = low_back(low(head_out)).transpose(1, 0, 2).reshape(SEQ, D)
    attention_result = low_back(exact_dot(attn_mix, complete_out_weight))
    attention_normed = layer_norm(token_rows + attention_result, layer_norm_gains[0], layer_norm_biases[0])
    gate_up_output = low_back(exact_dot(low(attention_normed), complete_gate_up_weight))
    hidden_state = low(jax.nn.silu(gate_up_output[:, :FF]) * gate_up_output[:, FF:])
    residual_branch = low_back(exact_dot(hidden_state, complete_down_weight))
    return layer_norm(attention_normed + residual_branch, layer_norm_gains[1], layer_norm_biases[1])

def orthonormal(factor):
    columns = []
    for column in range(factor.shape[1]):
        vector = factor[:, column]
        for earlier in columns:
            vector = vector - jnp.sum(earlier * vector) * earlier
        vector = vector * lax.rsqrt(jnp.sum(vector * vector) + 1e-06)
        columns.append(vector)
    return jnp.stack(columns, axis=1)

def compress(group_grads, errors, master, moment, start, step_rate):
    row_count, col_count = master.shape
    merged = group_grads + errors
    mean_grad = (lax.optimization_barrier(jnp.sum(merged, axis=0)) / GROUPS).reshape(BLOCKS, row_count // BLOCKS, col_count)
    left = jnp.einsum('jrc,jck->jrk', mean_grad, start, precision=lax.Precision.HIGHEST)
    basis = jax.vmap(orthonormal)(left)
    factor = jnp.einsum('jrc,jrk->jck', mean_grad, basis, precision=lax.Precision.HIGHEST)
    approx = jnp.einsum('jrk,jck->jrc', basis, factor, precision=lax.Precision.HIGHEST).reshape(row_count, col_count)
    error_new = merged - approx[None]
    moment_new = MOMENTUM * moment + approx
    weight_new = master - step_rate * moment_new
    return (weight_new, moment_new, error_new, basis.reshape(row_count, RANK), factor)

def reference(tokens, cotangent, lengths, w_qkv, w_out, w_gate_up, w_down, mom_qkv, mom_out, mom_gate_up, mom_down, err_qkv, err_out, err_gate_up, err_down, start_qkv, start_out, start_gate_up, start_down, layer_norm_gains, layer_norm_biases, norm_moments):
    masters = (w_qkv, w_out, w_gate_up, w_down)
    weights = tuple((low(master) for master in masters))
    token_groups = tokens.reshape(GROUPS, SEQ_GRP, SEQ, D)
    cot_groups = cotangent.reshape(GROUPS, SEQ_GRP, SEQ, D)
    length_groups = lengths.reshape(GROUPS, SEQ_GRP)

    def group_step(carry, inputs):
        token_block, cot_block, length_block = inputs
        outputs = []
        input_grads = []
        grad_sums = None
        for seq_index in range(SEQ_GRP):
            key_keep = jnp.arange(SEQ, dtype=jnp.int32) < length_block[seq_index]

            def forward(token_rows, weight_set, gain_set, bias_set):
                return one_sequence(token_rows, weight_set, gain_set, bias_set, key_keep)
            result, pull = jax.vjp(forward, token_block[seq_index].astype(jnp.float32), weights, layer_norm_gains, layer_norm_biases)
            grad_parts = pull(cot_block[seq_index].astype(jnp.float32) * key_keep[:, None].astype(jnp.float32))
            outputs.append(result)
            input_grads.append(grad_parts[0])
            weight_parts = (grad_parts[1], grad_parts[2], grad_parts[3])
            grad_sums = weight_parts if grad_sums is None else jax.tree.map(jnp.add, grad_sums, weight_parts)
        return (carry, (jnp.stack(outputs), jnp.stack(input_grads), grad_sums))
    _, (outputs, input_grads, grad_sums) = lax.scan(group_step, jnp.zeros((), jnp.float32), (token_groups, cot_groups, length_groups))
    mixed_out = outputs.reshape(SEQS, SEQ, D).astype(jnp.bfloat16)
    input_grad = input_grads.reshape(SEQS, SEQ, D)
    matrix_grads, gain_grads, bias_grads = grad_sums
    gain_mean = lax.optimization_barrier(jnp.sum(gain_grads, axis=0)) / GROUPS
    bias_mean = lax.optimization_barrier(jnp.sum(bias_grads, axis=0)) / GROUPS
    norm_grad = jnp.stack([gain_mean[0], bias_mean[0], gain_mean[1], bias_mean[1]])
    params = jnp.stack([layer_norm_gains[0], layer_norm_biases[0], layer_norm_gains[1], layer_norm_biases[1]])
    norm_moment_new = MOMENTUM * norm_moments + norm_grad
    norm_new = params - NORM_RATE * norm_moment_new
    results = [compress(grad_set, error_set, master, moment, start, step_rate) for grad_set, error_set, master, moment, start, step_rate in zip(matrix_grads, (err_qkv, err_out, err_gate_up, err_down), masters, (mom_qkv, mom_out, mom_gate_up, mom_down), (start_qkv, start_out, start_gate_up, start_down), LEARN_RATES)]
    return (mixed_out, input_grad, results[0][0], results[1][0], results[2][0], results[3][0], results[0][1], results[1][1], results[2][1], results[3][1], results[0][2], results[1][2], results[2][2], results[3][2], results[0][3], results[1][3], results[2][3], results[3][3], results[0][4], results[1][4], results[2][4], results[3][4], norm_moment_new, norm_new)
```

```python
import functools
import math

import jax
import jax.numpy as jnp
from jax import lax
from jax.experimental import pallas as pl
from jax.experimental.pallas import tpu as pltpu
from jax.sharding import PartitionSpec as P

H = 12
HD = 64
FF = 3072


EPS = 1e-05
ROPE_BASE = 1000.0
MOMENTUM = 0.5
LEARN_RATES = (0.002, 0.1, 0.004, 0.002)
NORM_RATE = 0.01
NEG_FILL = -1e30


def norm_components(values_in, gain, bias):
    centre = jnp.mean(values_in, axis=-1, keepdims=True)
    centred = values_in - centre
    spread = jnp.mean(centred * centred, axis=-1, keepdims=True)
    row_rstd = lax.rsqrt(spread + EPS)
    normed = centred * row_rstd
    return (normed * gain + bias, normed, row_rstd)


def norm_reverse_pass(grad_in, normed, row_rstd):
    return row_rstd * (
        grad_in
        - jnp.mean(grad_in, axis=-1, keepdims=True)
        - normed * jnp.mean(grad_in * normed, axis=-1, keepdims=True)
    )


def rotary(values_in, cosine_table, sine_table):
    half_dim = values_in.shape[-1] // 2
    leading_half = values_in[..., :half_dim]
    second_half = values_in[..., half_dim:]
    return jnp.concatenate(
        [
            leading_half * cosine_table - second_half * sine_table,
            second_half * cosine_table + leading_half * sine_table,
        ],
        axis=-1,
    )


def rotary_back(grad_in, cosine_table, sine_table):
    half_dim = grad_in.shape[-1] // 2
    leading_half = grad_in[..., :half_dim]
    second_half = grad_in[..., half_dim:]
    return jnp.concatenate(
        [
            leading_half * cosine_table + second_half * sine_table,
            second_half * cosine_table - leading_half * sine_table,
        ],
        axis=-1,
    )


def orthonormal(factor):
    columns = []
    for column in range(factor.shape[1]):
        vector = factor[:, column]
        for earlier in columns:
            vector = vector - jnp.sum(earlier * vector) * earlier
        vector = vector * lax.rsqrt(jnp.sum(vector * vector) + 1e-06)
        columns.append(vector)
    return jnp.stack(columns, axis=1)


def general_device(
    tokens,
    cotangent,
    lengths,
    w_qkv,
    w_out,
    w_gate_up,
    w_down,
    mom_qkv,
    mom_out,
    mom_gate_up,
    mom_down,
    err_qkv,
    err_out,
    err_gate_up,
    err_down,
    start_qkv,
    start_out,
    start_gate_up,
    start_down,
    layer_norm_gains,
    layer_norm_biases,
    norm_moments,
):
    single_float = jnp.float32
    bf16 = jnp.bfloat16
    wide_cols = (
        lax.all_gather(w_qkv.astype(bf16), "rep", axis=1, tiled=True),
        lax.all_gather(w_out.astype(bf16), "rep", axis=1, tiled=True),
        lax.all_gather(w_gate_up.astype(bf16), "rep", axis=1, tiled=True),
        lax.all_gather(w_down.astype(bf16), "rep", axis=1, tiled=True),
    )
    complete_query_key_value, complete_out_weight, complete_gate_up_weight, complete_down_weight = (
        lax.all_gather(wide_cols[0], "shard", axis=0, tiled=True),
        lax.all_gather(wide_cols[1], "shard", axis=0, tiled=True),
        lax.all_gather(wide_cols[2], "shard", axis=0, tiled=True),
        lax.all_gather(wide_cols[3], "shard", axis=0, tiled=True),
    )
    groups, local_len, model_width = tokens.shape
    shards = lax.axis_size("shard")
    seq_len = local_len * shards
    score_scale = HD ** (-0.5)
    offset = lax.axis_index("shard") * local_len
    position = offset + jnp.arange(local_len, dtype=jnp.int32)
    valid_rows = position[None, :] < lengths[:, None]
    key_keep = jnp.arange(seq_len, dtype=jnp.int32)[None, :] < lengths[:, None]
    inverse = jnp.exp(
        jnp.arange(HD // 2, dtype=jnp.int32).astype(single_float)
        * (-2.0 * math.log(ROPE_BASE) / HD)
    )
    angle = position.astype(single_float)[:, None] * inverse[None, :]
    cosine_table = jnp.cos(angle)[:, None, :]
    sine_table = jnp.sin(angle)[:, None, :]
    query_key_value_rows = jnp.einsum(
        "znk,kb->znb", tokens, complete_query_key_value, preferred_element_type=single_float
    )
    query_key_value_rows = query_key_value_rows.reshape(groups, local_len, 3, H, HD)
    q_half = (
        rotary(query_key_value_rows[:, :, 0], cosine_table, sine_table)
        .astype(bf16)
        .transpose(2, 0, 1, 3)
    )
    k_half = (
        rotary(query_key_value_rows[:, :, 1], cosine_table, sine_table)
        .astype(bf16)
        .transpose(2, 0, 1, 3)
    )
    v_half = query_key_value_rows[:, :, 2].astype(bf16).transpose(2, 0, 1, 3)
    key_all, value_all = (
        lax.all_gather(k_half, "shard", axis=2, tiled=True),
        lax.all_gather(v_half, "shard", axis=2, tiled=True),
    )

    def head_forward(inputs):
        query_h, key_h, value_h = inputs
        scores = (
            jnp.einsum("sqd,skd->sqk", query_h, key_h, preferred_element_type=single_float)
            * score_scale
        )
        scores = jnp.where(key_keep[:, None, :], scores, NEG_FILL)
        row_peak = jnp.max(scores, axis=-1, keepdims=True)
        exp_scores = jnp.exp(scores - row_peak)
        row_total = jnp.sum(exp_scores, axis=-1, keepdims=True)
        attn_probs = (exp_scores / row_total).astype(bf16)
        head_rows = jnp.einsum(
            "sqk,skd->sqd", attn_probs, value_h, preferred_element_type=single_float
        )
        return (head_rows, (row_peak + jnp.log(row_total))[..., 0])

    head_out, log_total = lax.map(head_forward, (q_half, key_all, value_all))
    mix_half = head_out.astype(bf16)
    mixture_rows = mix_half.transpose(1, 2, 0, 3).reshape(groups, local_len, model_width)
    attention_result = jnp.einsum(
        "znk,kb->znb", mixture_rows, complete_out_weight, preferred_element_type=single_float
    )
    attention_normed, attention_standardized, attention_inverse_deviation = norm_components(
        tokens.astype(single_float) + attention_result, layer_norm_gains[0], layer_norm_biases[0]
    )
    leading_half = attention_normed.astype(bf16)
    gate_up_output = jnp.einsum(
        "znk,kb->znb", leading_half, complete_gate_up_weight, preferred_element_type=single_float
    )
    gate_part = gate_up_output[..., :FF]
    up_part = gate_up_output[..., FF:]
    gate_sig = jax.nn.sigmoid(gate_part)
    hidden_state = (gate_part * gate_sig * up_part).astype(bf16)
    residual_branch = jnp.einsum(
        "ckh,hy->cky", hidden_state, complete_down_weight, preferred_element_type=single_float
    )
    feedforward_normed, feedforward_standardized, feedforward_inverse_deviation = norm_components(
        attention_normed + residual_branch, layer_norm_gains[1], layer_norm_biases[1]
    )
    mixed_out = feedforward_normed.astype(bf16)
    output_gradient = cotangent.astype(single_float) * valid_rows[..., None].astype(single_float)
    feedforward_gain = jnp.sum(output_gradient * feedforward_standardized, axis=(0, 1))
    bias_two = jnp.sum(output_gradient, axis=(0, 1))
    trailing_norm_gradient = norm_reverse_pass(
        output_gradient * layer_norm_gains[1],
        feedforward_standardized,
        feedforward_inverse_deviation,
    )
    branch_gradient = trailing_norm_gradient.astype(bf16)
    down_weight_gradient = jnp.einsum(
        "zxi,zxp->ip", hidden_state, branch_gradient, preferred_element_type=single_float
    )
    hidden_gradient = jnp.einsum(
        "gbz,wz->gbw", branch_gradient, complete_down_weight, preferred_element_type=single_float
    )
    grad_gate = hidden_gradient * up_part * gate_sig * (1.0 + gate_part * (1.0 - gate_sig))
    grad_up = hidden_gradient * gate_part * gate_sig
    gate_up_gradient = jnp.concatenate([grad_gate, grad_up], axis=-1).astype(bf16)
    gate_up_weight_gradient = jnp.einsum(
        "vcm,vcb->mb", leading_half, gate_up_gradient, preferred_element_type=single_float
    )
    leading_norm_gradient = (
        jnp.einsum(
            "thi,ci->thc",
            gate_up_gradient,
            complete_gate_up_weight,
            preferred_element_type=single_float,
        )
        + trailing_norm_gradient
    )
    attention_gain = jnp.sum(leading_norm_gradient * attention_standardized, axis=(0, 1))
    bias_one = jnp.sum(leading_norm_gradient, axis=(0, 1))
    attention_gradient = norm_reverse_pass(
        leading_norm_gradient * layer_norm_gains[0],
        attention_standardized,
        attention_inverse_deviation,
    )
    attention_gradient_half = attention_gradient.astype(bf16)
    out_weight_gradient = jnp.einsum(
        "vcm,vcb->mb", mixture_rows, attention_gradient_half, preferred_element_type=single_float
    )
    mixture_gradient = jnp.einsum(
        "thi,ci->thc",
        attention_gradient_half,
        complete_out_weight,
        preferred_element_type=single_float,
    )
    grad_mix_half = (
        mixture_gradient.astype(bf16).reshape(groups, local_len, H, HD).transpose(2, 0, 1, 3)
    )

    def head_back(inputs):
        query_h, key_h, value_h, grad_h, lse_h = inputs
        scores = (
            jnp.einsum("sqd,skd->sqk", query_h, key_h, preferred_element_type=single_float)
            * score_scale
        )
        scores = jnp.where(key_keep[:, None, :], scores, NEG_FILL)
        attn_probs = jnp.exp(scores - lse_h[..., None])
        grad_probs = jnp.einsum(
            "sqd,skd->sqk", grad_h, value_h, preferred_element_type=single_float
        )
        row_delta = jnp.sum(grad_probs * attn_probs, axis=-1, keepdims=True)
        grad_scores = (attn_probs * (grad_probs - row_delta)).astype(bf16)
        grad_query = (
            jnp.einsum("sqk,skd->sqd", grad_scores, key_h, preferred_element_type=single_float)
            * score_scale
        )
        grad_key = (
            jnp.einsum("sqk,sqd->skd", grad_scores, query_h, preferred_element_type=single_float)
            * score_scale
        )
        grad_value = jnp.einsum(
            "sqk,sqd->skd", attn_probs.astype(bf16), grad_h, preferred_element_type=single_float
        )
        return (grad_query, grad_key, grad_value)

    grad_q_heads, key_parts, value_parts = lax.map(
        head_back, (q_half, key_all, value_all, grad_mix_half, log_total)
    )
    grad_k_heads, grad_v_heads = (
        lax.psum_scatter(key_parts, "shard", scatter_dimension=2, tiled=True),
        lax.psum_scatter(value_parts, "shard", scatter_dimension=2, tiled=True),
    )
    grad_q_rows = rotary_back(grad_q_heads.transpose(1, 2, 0, 3), cosine_table, sine_table)
    grad_k_rows = rotary_back(grad_k_heads.transpose(1, 2, 0, 3), cosine_table, sine_table)
    grad_v_rows = grad_v_heads.transpose(1, 2, 0, 3)
    query_key_value_gradient = jnp.stack([grad_q_rows, grad_k_rows, grad_v_rows], axis=2)
    query_key_value_gradient = query_key_value_gradient.reshape(
        groups, local_len, 3 * model_width
    ).astype(bf16)
    query_key_value_weight_gradient = jnp.einsum(
        "vcm,vcb->mb", tokens, query_key_value_gradient, preferred_element_type=single_float
    )
    input_grad = (
        jnp.einsum(
            "thi,ci->thc",
            query_key_value_gradient,
            complete_query_key_value,
            preferred_element_type=single_float,
        )
        + attention_gradient
    )
    owned = (
        lax.psum_scatter(
            query_key_value_weight_gradient.astype(jnp.bfloat16),
            "shard",
            scatter_dimension=0,
            tiled=True,
        ).astype(jnp.float32),
        lax.psum_scatter(
            out_weight_gradient.astype(jnp.bfloat16), "shard", scatter_dimension=0, tiled=True
        ).astype(jnp.float32),
        lax.psum_scatter(
            gate_up_weight_gradient.astype(jnp.bfloat16), "shard", scatter_dimension=0, tiled=True
        ).astype(jnp.float32),
        lax.psum_scatter(
            down_weight_gradient.astype(jnp.bfloat16), "shard", scatter_dimension=0, tiled=True
        ).astype(jnp.float32),
    )
    replicas = lax.axis_size("rep")
    vector_parts = jnp.stack([attention_gain, bias_one, feedforward_gain, bias_two])
    norm_grad = lax.psum(vector_parts, ("rep", "shard")) / replicas
    params = jnp.stack(
        [layer_norm_gains[0], layer_norm_biases[0], layer_norm_gains[1], layer_norm_biases[1]]
    )
    norm_moment_new = MOMENTUM * norm_moments + norm_grad
    norm_new = params - NORM_RATE * norm_moment_new
    errors = (err_qkv, err_out, err_gate_up, err_down)
    starts = (start_qkv, start_out, start_gate_up, start_down)
    masters = (w_qkv, w_out, w_gate_up, w_down)
    moments = (mom_qkv, mom_out, mom_gate_up, mom_down)
    merged = tuple((part + error_set[0] for part, error_set in zip(owned, errors)))
    projected = tuple(
        (
            jnp.dot(block, start_set[0], precision=lax.Precision.HIGHEST)
            for block, start_set in zip(merged, starts)
        )
    )
    summed_left = lax.psum((projected[0], projected[1], projected[2], projected[3]), "rep")
    bases = tuple((orthonormal(part / replicas) for part in summed_left))
    pulled = tuple(
        (
            jnp.einsum("rc,rk->ck", block, basis, precision=lax.Precision.HIGHEST)
            for block, basis in zip(merged, bases)
        )
    )
    summed_right = (
        lax.psum(pulled[0].astype(jnp.bfloat16), "rep").astype(jnp.float32),
        lax.psum(pulled[1].astype(jnp.bfloat16), "rep").astype(jnp.float32),
        lax.psum(pulled[2].astype(jnp.bfloat16), "rep").astype(jnp.float32),
        lax.psum(pulled[3].astype(jnp.bfloat16), "rep").astype(jnp.float32),
    )
    factors = tuple((part / replicas for part in summed_right))
    rep_pos = lax.axis_index("rep")
    new_weights = []
    new_moments = []
    new_errors = []
    for block, basis, factor, master, moment, step_rate in zip(
        merged, bases, factors, masters, moments, LEARN_RATES
    ):
        approx = jnp.dot(basis, factor.T, precision=lax.Precision.HIGHEST)
        new_errors.append((block - approx)[None])
        col_count = master.shape[1]
        piece = lax.dynamic_slice_in_dim(approx, rep_pos * col_count, col_count, 1)
        moment_new = MOMENTUM * moment + piece
        new_moments.append(moment_new)
        new_weights.append(master - step_rate * moment_new)
    return (
        mixed_out,
        input_grad,
        new_weights[0],
        new_weights[1],
        new_weights[2],
        new_weights[3],
        new_moments[0],
        new_moments[1],
        new_moments[2],
        new_moments[3],
        new_errors[0],
        new_errors[1],
        new_errors[2],
        new_errors[3],
        bases[0],
        bases[1],
        bases[2],
        bases[3],
        factors[0][None],
        factors[1][None],
        factors[2][None],
        factors[3][None],
        norm_moment_new,
        norm_new,
    )


AXES = ("rep", "shard")
SHARDS = 4
REPS = 8
RANK = 8
DIM = 768
PAIRS = 6
LANES = 128
MIB = 2**20


def send(values, move):
    pairs = []
    for rep in range(REPS):
        for shard in range(SHARDS):
            to = move(rep, shard)
            if to is not None:
                pairs.append((rep * SHARDS + shard, to[0] * SHARDS + to[1]))
    return lax.ppermute(values, AXES, pairs)


def spread_move(parity):
    return lambda r, z: (r - r % 2 + z // 2, 2 * (r % 2) + (z + parity) % 2)


def gather_move(parity):
    table = {}
    for r in range(REPS):
        for z in range(SHARDS):
            table[spread_move(parity)(r, z)] = (r, z)
    return lambda r, z: table[(r, z)]


def sibling(values):
    return send(values, lambda r, z: (r ^ 1, z))


def near_x(values):
    return send(values, lambda r, z: (r ^ 2, z))


def near_y(values):
    return send(values, lambda r, z: (r ^ 4, z))


def pair_z(values):
    return send(values, lambda r, z: (r, z ^ 1))


def mirror_z(values):
    return send(values, lambda r, z: (r, 3 - z))


def to_owner(values):
    return send(values, lambda r, z: (r ^ 1, 3 - z) if r % 2 != z // 2 else None)


def turn_z(values, step):
    return send(values, lambda r, z: (r, (z + step) % SHARDS))


def after(values, *others):
    return lax.optimization_barrier((values, *others))[0]


def shard_gather(piece, shard):
    parts = jnp.stack([piece] + [turn_z(piece, step) for step in (1, 2, 3)])
    return [
        lax.dynamic_index_in_dim(parts, (shard - at) % SHARDS, 0, keepdims=False)
        for at in range(SHARDS)
    ]


def plane_near(piece):
    return near_x(piece), near_y(piece)


def plane_far(piece, near):
    half = piece.shape[0] // 2
    from_x, from_y = near
    return near_x(from_y[:half]), near_y(from_x[half:])


def exchange(piece, near, far):
    return [sibling(part) for part in (piece, *near, jnp.concatenate(far, axis=0))]


def plane_all(piece, near, far, others, rep, ahead=()):
    return stack_pieces((piece, *near, *far, *others), rep, *piece.shape, ahead)


PIECE_STEPS = ((0, None), (2, None), (4, None), (6, 0), (6, 1), (1, None), (3, None), (5, None), (7, None))


def stack_kernel(rep_ref, *refs):
    count = len(PIECE_STEPS)
    pieces = refs[:count]
    whole, staged, sems_in, sems_out = refs[-4:]
    rep = rep_ref[0]
    half = pieces[3].shape[0]
    fetches = []
    stores = []
    for slot, (step, side) in enumerate(PIECE_STEPS):
        stage = staged.at[step]
        place = whole.at[rep ^ step]
        if side is not None:
            part = pl.ds(side * half, half)
            stage = stage.at[part]
            place = place.at[part]
        fetches.append(pltpu.make_async_copy(pieces[slot], stage, sems_in.at[slot]))
        stores.append(pltpu.make_async_copy(stage, place, sems_out.at[slot]))
    for fetch in fetches:
        fetch.start()
    for fetch, store in zip(fetches, stores):
        fetch.wait()
        store.start()
    for store in stores:
        store.wait()


def stack_pieces(pieces, rep, rows, cols, ahead):
    anywhere = pl.BlockSpec(memory_space=pl.ANY)
    count = len(pieces)
    return pl.pallas_call(
        stack_kernel,
        in_specs=[pl.BlockSpec(memory_space=pltpu.SMEM)] + [anywhere] * (count + len(ahead)),
        out_specs=anywhere,
        out_shape=jax.ShapeDtypeStruct((REPS, rows, cols), pieces[0].dtype),
        scratch_shapes=[
            pltpu.VMEM((REPS, rows, cols), pieces[0].dtype),
            pltpu.SemaphoreType.DMA((count,)),
            pltpu.SemaphoreType.DMA((count,)),
        ],
        compiler_params=limit(40),
        cost_estimate=pl.CostEstimate(
            flops=0, bytes_accessed=4 * REPS * rows * cols, transcendentals=0
        ),
        name="stack_pieces",
    )(jnp.reshape(rep, (1,)), *pieces, *ahead)


def plane_sum(values):
    values = values + sibling(values)
    values = values + near_x(values)
    return values + near_y(values)


def plane_sum_half(values):
    bf16 = jnp.bfloat16
    f32 = jnp.float32
    for step in (sibling, near_x, near_y):
        rounded = values.astype(bf16)
        values = rounded.astype(f32) + step(rounded).astype(f32)
    return values


def nt(left, right):
    return lax.dot_general(
        left, right, (((1,), (1,)), ((), ())), preferred_element_type=jnp.float32
    )


def nn(left, right):
    return lax.dot_general(
        left, right, (((1,), (0,)), ((), ())), preferred_element_type=jnp.float32
    )


def cost(flops, moved, powers=0):
    return pl.CostEstimate(flops=int(flops), bytes_accessed=int(moved), transcendentals=int(powers))


def limit(mib):
    return pltpu.CompilerParams(vmem_limit_bytes=mib * MIB)


def shape(dims, dtype):
    return jax.ShapeDtypeStruct(dims, dtype)


def partner_lanes(values):
    lane = lax.broadcasted_iota(jnp.int32, values.shape, 1)
    up = pltpu.roll(values, 96, 1)
    down = pltpu.roll(values, 32, 1)
    return jnp.where(lane % HD < HD // 2, up, down)


def project_kernel(x_ref, w_ref, cos_ref, sin_ref, out_ref, *, turned, scale):
    values = nt(x_ref[...], w_ref[...])

    def turn():
        for at in range(0, values.shape[1], LANES):
            part = values[:, at : at + LANES]
            part = part * cos_ref[...] + partner_lanes(part) * sin_ref[...]
            out_ref[:, at : at + LANES] = (part * scale).astype(out_ref.dtype)

    if turned is None:
        turn()
    else:
        pl.when(pl.program_id(0) < turned)(turn)

        @pl.when(pl.program_id(0) >= turned)
        def _():
            out_ref[...] = values.astype(out_ref.dtype)


def project(rows_in, qkv_t, cos, sin, first, count, turned, scale):
    rows = rows_in.shape[0]
    tile = DIM
    fixed = lambda j: (0, 0)
    return pl.pallas_call(
        functools.partial(project_kernel, turned=turned, scale=scale),
        grid=(count,),
        in_specs=[
            pl.BlockSpec((rows, DIM), fixed),
            pl.BlockSpec((tile, DIM), lambda j: (j + first, 0)),
            pl.BlockSpec((rows, LANES), fixed),
            pl.BlockSpec((rows, LANES), fixed),
        ],
        out_specs=pl.BlockSpec((rows, tile), lambda j: (0, j)),
        out_shape=shape((rows, count * tile), jnp.bfloat16),
        compiler_params=limit(48),
        cost_estimate=cost(2 * rows * DIM * tile * count, 4 * rows * DIM + 4 * count * tile * rows),
        name="project",
    )(rows_in, qkv_t, cos, sin)


def lane_of(dims):
    return lax.broadcasted_iota(jnp.int32, dims, 1)


def head_lanes(dims, head):
    lane = lane_of(dims)
    return (lane >= HD) if head else (lane < HD)


def extra_lane(head):
    return 0 if head else HD


def key_fill(place_ref, at, count, start):
    row = lax.broadcasted_iota(jnp.int32, (count, LANES), 0) + start
    half = place_ref[6]
    position = jnp.where(row < half, place_ref[at] + row, place_ref[at + 1] + row - half)
    return jnp.where(position < place_ref[4], 0.0, NEG_FILL).astype(jnp.bfloat16)


def attend_kernel(place_ref, q_ref, ka_ref, va_ref, kb_ref, vb_ref, *refs):
    mix_ref, qx_ref, keys, values = refs[-4:]
    rows = ka_ref.shape[0]
    bf16 = jnp.bfloat16

    @pl.when(pl.program_id(1) == 0)
    def _():
        dims = (rows, LANES)
        zero = jnp.zeros(dims, bf16)
        for source, (k_ref, v_ref) in enumerate(((ka_ref, va_ref), (kb_ref, vb_ref))):
            fill = key_fill(place_ref, 2 * source, rows, 0)
            part = pl.ds(source * rows, rows)
            for head in range(2):
                inside = head_lanes(dims, head)
                other = jnp.where(lane_of(dims) == extra_lane(head), fill, zero)
                keys[head, part] = jnp.where(inside, k_ref[...], other)
                values[head, part] = jnp.where(inside, v_ref[...], zero)

    queries = q_ref[...]
    dims = queries.shape
    lane = lane_of(dims)
    total = None
    for head in range(2):
        inside = head_lanes(dims, head)
        spare = lane - extra_lane(head)
        one = jnp.where(spare == 0, 1.0, 0.0).astype(bf16)
        masked = jnp.where(inside, queries, one)
        scores = nt(masked, keys[head])
        peak = jnp.max(scores, axis=1, keepdims=True)
        powers = jnp.exp(scores - peak)
        row_sum = jnp.sum(powers, axis=1, keepdims=True)
        out = nn(powers.astype(bf16), values[head]) / row_sum
        total = out if total is None else total + out
        lse = peak + jnp.log(row_sum)
        high = lse.astype(bf16)
        middle = (lse - high.astype(jnp.float32)).astype(bf16)
        low = (lse - high.astype(jnp.float32) - middle.astype(jnp.float32)).astype(bf16)
        wide = jnp.where(spare == 1, -high, jnp.where(spare == 2, -middle, -low))
        wide = jnp.where((spare >= 1) & (spare <= 3), wide, one)
        qx_ref[:, head * LANES : (head + 1) * LANES] = jnp.where(inside, queries, wide)
    mix_ref[...] = total.astype(bf16)


def attend(place, q, kv_own, kv_other, first, count, done=()):
    rows = q.shape[0]
    block = 256
    bf16 = jnp.bfloat16
    key_spec = pl.BlockSpec((rows, LANES), lambda p, i: (0, p + first))
    value_spec = pl.BlockSpec((rows, LANES), lambda p, i: (0, p + first + PAIRS))
    return pl.pallas_call(
        attend_kernel,
        grid=(count, rows // block),
        in_specs=[
            pl.BlockSpec(memory_space=pltpu.SMEM),
            pl.BlockSpec((block, LANES), lambda p, i: (i, p + first)),
            key_spec,
            value_spec,
            key_spec,
            value_spec,
        ]
        + [pl.BlockSpec(memory_space=pl.ANY)] * len(done),
        out_specs=[
            pl.BlockSpec((block, LANES), lambda p, i: (i, p + first)),
            pl.BlockSpec((block, 2 * LANES), lambda p, i: (i, p + first)),
        ],
        out_shape=[shape((rows, DIM), bf16), shape((rows, 2 * DIM), bf16)],
        scratch_shapes=[
            pltpu.VMEM((2, 2 * rows, LANES), bf16),
            pltpu.VMEM((2, 2 * rows, LANES), bf16),
        ],
        input_output_aliases={6: 0, 7: 1} if done else {},
        compiler_params=limit(48),
        cost_estimate=cost(
            64 * count * rows * 2 * rows * HD, 32 * rows * LANES * count, 2 * count * rows * 2 * rows
        ),
        name="attend",
    )(place, q, kv_own, kv_own, kv_other, kv_other, *done)


def attend_back_kernel(place_ref, qx_ref, k_ref, v_ref, g_ref, mix_ref, *refs, at, scale):
    bf16 = jnp.bfloat16
    f32 = jnp.float32
    last = at == 0
    if last:
        dq_ref, got_k_ref, got_v_ref, cos_ref, sin_ref, out_ref, gx, g0, q0, acc = refs
    else:
        dq_ref, dk_ref, dv_ref, gx, g0, q0, acc = refs
    rows = g_ref.shape[0]
    count = k_ref.shape[0]
    step = pl.program_id(1)

    @pl.when(step == 0)
    def _():
        dims = (rows, LANES)
        lane = lane_of(dims)
        grad = g_ref[...]
        product = grad.astype(f32) * mix_ref[...].astype(f32)
        zero = jnp.zeros(dims, bf16)
        for head in range(2):
            inside = head_lanes(dims, head)
            spare = lane - extra_lane(head)
            delta = jnp.sum(jnp.where(inside, product, 0.0), axis=1, keepdims=True)
            high = delta.astype(bf16)
            middle = (delta - high.astype(f32)).astype(bf16)
            low = (delta - high.astype(f32) - middle.astype(f32)).astype(bf16)
            wide = jnp.where(spare == 1, -high, jnp.where(spare == 2, -middle, -low))
            wide = jnp.where((spare >= 1) & (spare <= 3), wide, zero)
            gx[head] = jnp.where(inside, grad, wide)
            g0[head] = jnp.where(inside, grad, zero)
            q0[head] = jnp.where(inside, qx_ref[:, head * LANES : (head + 1) * LANES], zero)
        acc[...] = jnp.zeros_like(acc)

    keys = k_ref[...]
    values = v_ref[...]
    dims = keys.shape
    lane = lane_of(dims)
    fill = key_fill(place_ref, at, count, step * count)
    keys_t = keys.astype(f32).T.astype(bf16)
    dk = None
    dv = None
    for head in range(2):
        inside = head_lanes(dims, head)
        spare = lane - extra_lane(head)
        ones = jnp.where((spare >= 1) & (spare <= 3), 1.0, 0.0).astype(bf16)
        keys_x = jnp.where(inside, keys, jnp.where(spare == 0, fill, ones))
        values_x = jnp.where(inside, values, ones)
        scores = nt(keys_x, qx_ref[:, head * LANES : (head + 1) * LANES])
        probs = jnp.exp(scores)
        dv_head = nn(probs.astype(bf16), g0[head])
        grad_probs = nt(values_x, gx[head])
        grad_scores = (probs * grad_probs).astype(bf16)
        dk_head = nn(grad_scores, q0[head])
        part = slice(head * HD, (head + 1) * HD)
        acc[part] += nn(keys_t[part], grad_scores)
        dk = dk_head if dk is None else dk + dk_head
        dv = dv_head if dv is None else dv + dv_head
    if last:
        here = pl.ds(pl.multiple_of(step * count, count), count)
        dk = dk + got_k_ref[...].astype(f32)
        dk = dk * cos_ref[here] - partner_lanes(dk) * sin_ref[here]
        out_ref[1, here] = dk.astype(bf16)
        out_ref[2, here] = (dv + got_v_ref[...].astype(f32)).astype(bf16)
    else:
        dk_ref[...] = dk.astype(bf16)
        dv_ref[...] = dv.astype(bf16)

    @pl.when(step == pl.num_programs(1) - 1)
    def _():
        dq = acc[...].T
        if last:
            dq = (dq + dq_ref[...]) * scale
            dq = dq * cos_ref[...] - partner_lanes(dq) * sin_ref[...]
            out_ref[0] = dq.astype(bf16)
        else:
            dq_ref[...] = dq


def attend_back(place, qx, kv, grad, mix, at, first, count, scale, more=()):
    rows = grad.shape[0]
    block = 512
    bf16 = jnp.bfloat16
    wide = pl.BlockSpec((rows, LANES), lambda p, j: (0, p + first))
    here = pl.BlockSpec((rows, LANES), lambda p, j: (0, p))
    keys = pl.BlockSpec((block, LANES), lambda p, j: (j, p))
    table = pl.BlockSpec((rows, LANES), lambda p, j: (0, 0))
    dims = (rows, count * LANES)
    if at == 0:
        more_specs = [here, keys, keys, table, table]
        out_specs = pl.BlockSpec((3, rows, LANES), lambda p, j: (0, 0, p))
        out_shape = shape((3, *dims), bf16)
    else:
        more_specs = []
        out_specs = [here, keys, keys]
        out_shape = [shape(dims, jnp.float32), shape(dims, bf16), shape(dims, bf16)]
    return pl.pallas_call(
        functools.partial(attend_back_kernel, at=at, scale=scale),
        grid=(count, rows // block),
        in_specs=[
            pl.BlockSpec(memory_space=pltpu.SMEM),
            pl.BlockSpec((rows, 2 * LANES), lambda p, j: (0, p + first)),
            pl.BlockSpec((block, LANES), lambda p, j: (j, p + first)),
            pl.BlockSpec((block, LANES), lambda p, j: (j, p + first + PAIRS)),
            wide,
            wide,
        ]
        + more_specs,
        out_specs=out_specs,
        out_shape=out_shape,
        scratch_shapes=[
            pltpu.VMEM((2, rows, LANES), bf16),
            pltpu.VMEM((2, rows, LANES), bf16),
            pltpu.VMEM((2, rows, LANES), bf16),
            pltpu.VMEM((LANES, rows), jnp.float32),
        ],
        compiler_params=limit(48),
        cost_estimate=cost(
            80 * count * rows * rows * HD, 40 * count * rows * LANES, 2 * count * rows * rows
        ),
        name="attend_back",
    )(place, qx, kv, kv, grad, mix, *more)


def row_mean(values):
    return jnp.sum(values, axis=1, keepdims=True) * (1.0 / DIM)


def out_norm_kernel(mix_ref, w_ref, x_ref, hat_ref, rstd_ref):
    weight = w_ref[...].reshape(DIM, DIM)
    values = x_ref[...].astype(jnp.float32) + nt(mix_ref[...], weight)
    centred = values - row_mean(values)
    rstd = lax.rsqrt(row_mean(centred * centred) + EPS)
    hat_ref[...] = centred * rstd
    rstd_ref[...] = jnp.broadcast_to(rstd, rstd_ref.shape)


def out_norm(mix, stacked, rows_in):
    rows = mix.shape[0]
    block = 256
    spec = pl.BlockSpec((block, DIM), lambda i: (i, 0))
    return pl.pallas_call(
        out_norm_kernel,
        grid=(rows // block,),
        in_specs=[spec, pl.BlockSpec((REPS, 96, DIM), lambda i: (0, 8, 0)), spec],
        out_specs=[spec, pl.BlockSpec((block, LANES), lambda i: (i, 0))],
        out_shape=[shape((rows, DIM), jnp.float32), shape((rows, LANES), jnp.float32)],
        compiler_params=limit(48),
        cost_estimate=cost(2 * rows * DIM * DIM, 8 * rows * DIM),
        name="out_norm",
    )(mix, stacked, rows_in)


FF_TILE = 256
SUB = DIM // FF_TILE
FF_PIECES = FF // DIM


def row_parts(ref):
    half = ref.shape[0] // 2
    return [pl.ds(0, half), pl.ds(half, half)]


def sub_lanes():
    return pl.ds(pl.multiple_of(pl.program_id(1) * FF_TILE, FF_TILE), FF_TILE)


def at_step(piece, sub):
    return (pl.program_id(0) == piece) & (pl.program_id(1) == sub)


def feed_forward_kernel(
    hat_ref,
    gains_ref,
    biases_ref,
    wg_ref,
    wu_ref,
    wd_ref,
    hidden_ref,
    factor_ref,
    half_ref,
    acc,
    gate_s,
    up_s,
):
    bf16 = jnp.bfloat16
    f32 = jnp.float32
    step = pl.program_id(0)

    @pl.when(step == 0)
    def _():
        normed = hat_ref[...] * gains_ref[0:1] + biases_ref[0:1]
        acc[...] = normed
        half_ref[...] = normed.astype(bf16)
        gate_s[...] = jnp.zeros_like(gate_s)
        up_s[...] = jnp.zeros_like(up_s)

    gate = gate_s[...]
    up = up_s[...]
    sig = 1.0 / (1.0 + jnp.exp(-gate))
    act = gate * sig
    hidden = (act * up).astype(bf16)
    hidden_ref[...] = hidden
    factor_ref[0] = (up * sig * (1.0 + gate - act)).astype(bf16)
    factor_ref[1] = act.astype(bf16)
    rows_in = half_ref[...]
    gate_s[...] = nn(rows_in, wg_ref[0])
    up_s[...] = nn(rows_in, wu_ref[0])
    acc[...] += nt(hidden, wd_ref[...].reshape(DIM, FF_TILE))


def feed_forward(hat, gains, biases, stacked):
    rows = hat.shape[0]
    bf16 = jnp.bfloat16
    f32 = jnp.float32
    fixed = lambda t: (0, 0)
    whole = pl.BlockSpec((rows, DIM), fixed)
    small = pl.BlockSpec((2, DIM), fixed)
    tiles = FF_PIECES * SUB

    def now(t):
        return jnp.minimum(t, tiles - 1)

    def before(t):
        return jnp.maximum(t - 1, 0)

    return pl.pallas_call(
        feed_forward_kernel,
        grid=(tiles + 1,),
        in_specs=[
            whole,
            small,
            small,
            pl.BlockSpec((1, DIM, FF_TILE), lambda t: (now(t) // SUB, 0, now(t) % SUB)),
            pl.BlockSpec((1, DIM, FF_TILE), lambda t: (now(t) // SUB + FF_PIECES, 0, now(t) % SUB)),
            pl.BlockSpec(
                (REPS, 96, FF_TILE), lambda t: (0, before(t) // SUB + 9, before(t) % SUB)
            ),
        ],
        out_specs=[
            pl.BlockSpec((rows, FF_TILE), lambda t: (0, before(t))),
            pl.BlockSpec((2, rows, FF_TILE), lambda t: (0, 0, before(t))),
            whole,
            whole,
        ],
        out_shape=[
            shape((rows, FF), bf16),
            shape((2, rows, FF), bf16),
            shape((rows, DIM), bf16),
            shape((rows, DIM), f32),
        ],
        scratch_shapes=[
            pltpu.VMEM((rows, FF_TILE), f32),
            pltpu.VMEM((rows, FF_TILE), f32),
        ],
        compiler_params=limit(60),
        cost_estimate=cost(6 * rows * DIM * FF, 6 * rows * FF + 6 * DIM * FF, rows * FF),
        name="feed_forward",
    )(hat, gains, biases, stacked, stacked, stacked)


def norm_back_kernel(
    place_ref, values_ref, gains_ref, biases_ref, cot_a_ref, cot_b_ref,
    mixed_ref, grad_ref, branch_ref, vec_ref,
):
    bf16 = jnp.bfloat16
    f32 = jnp.float32
    step = pl.program_id(0)
    second = step >= pl.num_programs(0) // 2
    values = values_ref[...]
    rows = values.shape[0]
    centred = values - row_mean(values)
    rstd = lax.rsqrt(row_mean(centred * centred) + EPS)
    hat = centred * rstd
    mixed_ref[...] = (hat * gains_ref[1:2] + biases_ref[1:2]).astype(bf16)
    row = lax.broadcasted_iota(jnp.int32, (rows, 1), 0) + step * rows
    half = place_ref[6]
    position = jnp.where(row < half, place_ref[0] + row, place_ref[1] + row - half)
    cot = jnp.where(second, cot_b_ref[...].astype(f32), cot_a_ref[...].astype(f32))
    grad = jnp.where(position < place_ref[4], cot, 0.0)

    @pl.when(step == 0)
    def _():
        vec_ref[...] = jnp.zeros_like(vec_ref)

    vec_ref[0:1] += jnp.sum(grad * hat, axis=0, keepdims=True)
    vec_ref[1:2] += jnp.sum(grad, axis=0, keepdims=True)
    grad = grad * gains_ref[1:2]
    grad = rstd * (grad - row_mean(grad) - hat * row_mean(grad * hat))
    grad_ref[...] = grad
    branch_ref[...] = grad.astype(bf16)


def norm_back(place, values, gains, biases, cot):
    rows = values.shape[0]
    block = 256
    half = rows // block // 2
    f32 = jnp.float32
    bf16 = jnp.bfloat16
    spec = pl.BlockSpec((block, DIM), lambda i: (i, 0))
    small = pl.BlockSpec((2, DIM), lambda i: (0, 0))
    return pl.pallas_call(
        norm_back_kernel,
        grid=(rows // block,),
        in_specs=[
            pl.BlockSpec(memory_space=pltpu.SMEM),
            spec,
            small,
            small,
            pl.BlockSpec((block, DIM), lambda i: (jnp.minimum(i, half - 1), 0)),
            pl.BlockSpec((block, DIM), lambda i: (jnp.maximum(i - half, 0), 0)),
        ],
        out_specs=[spec, spec, spec, small],
        out_shape=[
            shape((rows, DIM), bf16),
            shape((rows, DIM), f32),
            shape((rows, DIM), bf16),
            shape((2, DIM), f32),
        ],
        compiler_params=limit(48),
        cost_estimate=cost(30 * rows * DIM, 14 * rows * DIM),
        name="norm_back",
    )(place, values, gains, biases, *cot)


def feed_back_kernel(
    index_ref,
    grad_ref,
    branch_ref,
    factor_ref,
    wg_ref,
    wu_ref,
    wd_ref,
    left_away_ref,
    left_keep_ref,
    *refs,
):
    bf16 = jnp.bfloat16
    f32 = jnp.float32
    last = len(refs) > 6
    if last:
        hat_ref, rstd_ref, gains_ref, wo_ref, away_ref, keep_ref = refs[:6]
        attn_ref, attn_half_ref, mix_grad_ref, vec_ref, acc, both, left = refs[6:]
    else:
        away_ref, keep_ref, acc_ref, acc, both, left = refs
    half_rows = left_away_ref.shape[0]
    here = sub_lanes()

    @pl.when(at_step(0, 0))
    def _():
        acc[...] = grad_ref[...]
        left[:half_rows] = left_away_ref[...]
        left[half_rows:] = left_keep_ref[...]

    grad_hidden = nn(branch_ref[...], wd_ref[...].reshape(DIM, FF_TILE))
    for side in range(2):
        grad = (grad_hidden * factor_ref[side].astype(f32)).astype(bf16)
        both[side, :, here] = grad
        product = nn(left[...], grad).astype(bf16)
        away_ref[side] = product[:half_rows]
        keep_ref[side] = product[half_rows:]

    @pl.when(pl.program_id(1) == SUB - 1)
    def _():
        acc[...] += nt(both[0], wg_ref[0]) + nt(both[1], wu_ref[0])

    @pl.when(at_step(pl.num_programs(0) - 1, SUB - 1))
    def _():
        grad = acc[...]
        if not last:
            acc_ref[...] = grad
            return
        hat = hat_ref[...]
        vec_ref[0:1] = jnp.sum(grad * hat, axis=0, keepdims=True)
        vec_ref[1:2] = jnp.sum(grad, axis=0, keepdims=True)
        grad = grad * gains_ref[0:1]
        rstd = rstd_ref[:, 0:1]
        grad = rstd * (grad - row_mean(grad) - hat * row_mean(grad * hat))
        attn_ref[...] = grad
        half = grad.astype(bf16)
        attn_half_ref[...] = half
        mix_grad_ref[...] = nn(half, wo_ref[...].reshape(DIM, DIM)).astype(bf16)


def feed_back(index, grad, branch, factor, stacked, normed_t, first, more=()):
    rows = grad.shape[0]
    bf16 = jnp.bfloat16
    f32 = jnp.float32
    fixed = lambda j, i, s: (0, 0)
    whole = pl.BlockSpec((rows, DIM), fixed)
    small = pl.BlockSpec((2, DIM), fixed)
    pieces = FF_PIECES // 2
    count = pieces * DIM
    parts = pl.BlockSpec((2, DIM // 2, FF_TILE), lambda j, i, s: (0, 0, SUB * j + i))
    in_specs = [
        whole,
        whole,
        pl.BlockSpec((2, rows, FF_TILE), lambda j, i, s: (0, 0, SUB * (j + first) + i)),
        pl.BlockSpec((1, DIM, DIM), lambda j, i, s: (j + first, 0, 0)),
        pl.BlockSpec((1, DIM, DIM), lambda j, i, s: (j + first + FF_PIECES, 0, 0)),
        pl.BlockSpec((REPS, 96, FF_TILE), lambda j, i, s: (0, j + first + 9, i)),
        pl.BlockSpec((DIM // 2, rows), lambda j, i, s: (s[0], 0)),
        pl.BlockSpec((DIM // 2, rows), lambda j, i, s: (1 - s[0], 0)),
    ]
    out_specs = [parts, parts]
    out_shape = [shape((2, DIM // 2, count), bf16)] * 2
    if more:
        in_specs += [
            whole,
            pl.BlockSpec((rows, LANES), fixed),
            small,
            pl.BlockSpec((REPS, 96, DIM), lambda j, i, s: (0, 8, 0)),
        ]
        out_specs += [whole, whole, whole, small]
        out_shape += [
            shape((rows, DIM), f32),
            shape((rows, DIM), bf16),
            shape((rows, DIM), bf16),
            shape((2, DIM), f32),
        ]
    else:
        out_specs += [whole]
        out_shape += [shape((rows, DIM), f32)]
    return pl.pallas_call(
        feed_back_kernel,
        grid_spec=pltpu.PrefetchScalarGridSpec(
            num_scalar_prefetch=1,
            grid=(pieces, SUB),
            in_specs=in_specs,
            out_specs=out_specs,
            scratch_shapes=[
                pltpu.VMEM((rows, DIM), f32),
                pltpu.VMEM((2, rows, DIM), bf16),
                pltpu.VMEM((DIM, rows), bf16),
            ],
        ),
        out_shape=out_shape,
        compiler_params=limit(60),
        cost_estimate=cost(10 * rows * DIM * count, 4 * rows * count + 10 * DIM * count),
        name="feed_back",
    )(index, grad, branch, factor, stacked, stacked, stacked, normed_t, normed_t, *more)


def away_kernel(index_ref, left_ref, right_ref, out_ref):
    right = right_ref[0] if len(right_ref.shape) == 3 else right_ref[...]
    out_ref[...] = nn(left_ref[...], right).astype(out_ref.dtype)


def keep_kernel(index_ref, la_ref, lb_ref, right_ref, ra_ref, rb_ref, out_a_ref, out_b_ref):
    right = right_ref[0] if len(right_ref.shape) == 3 else right_ref[...]
    for left, got, out in ((la_ref, ra_ref, out_a_ref), (lb_ref, rb_ref, out_b_ref)):
        out[...] = (nn(left[...], right) + got[...].astype(jnp.float32)).astype(out.dtype)


def right_spec(right, tile):
    if right.ndim == 3:
        per = right.shape[2] // tile
        return pl.BlockSpec((1, right.shape[1], tile), lambda t, s: (t // per, 0, t % per))
    return pl.BlockSpec((right.shape[0], tile), lambda t, s: (0, t))


def away_rows(index, left_t, right, tile):
    rows = left_t.shape[1]
    half = left_t.shape[0] // 2
    count = right.size // rows
    return pl.pallas_call(
        away_kernel,
        grid_spec=pltpu.PrefetchScalarGridSpec(
            num_scalar_prefetch=1,
            grid=(count // tile,),
            in_specs=[
                pl.BlockSpec((half, rows), lambda t, s: (s[0], 0)),
                right_spec(right, tile),
            ],
            out_specs=pl.BlockSpec((half, tile), lambda t, s: (0, t)),
        ),
        out_shape=shape((half, count), jnp.bfloat16),
        compiler_params=limit(48),
        cost_estimate=cost(2 * half * rows * count, 2 * rows * count + 2 * half * count),
        name="away_rows",
    )(index, left_t, right)


def keep_rows(index, left_t, right, got, tile):
    rows = left_t.shape[1]
    block = left_t.shape[0] // 4
    count = right.size // rows
    out = pl.BlockSpec((block, tile), lambda t, s: (0, t))
    return pl.pallas_call(
        keep_kernel,
        grid_spec=pltpu.PrefetchScalarGridSpec(
            num_scalar_prefetch=1,
            grid=(count // tile,),
            in_specs=[
                pl.BlockSpec((block, rows), lambda t, s: (s[1], 0)),
                pl.BlockSpec((block, rows), lambda t, s: (s[2], 0)),
                right_spec(right, tile),
                pl.BlockSpec((block, tile), lambda t, s: (s[3], t)),
                pl.BlockSpec((block, tile), lambda t, s: (1 - s[3], t)),
            ],
            out_specs=[out, out],
        ),
        out_shape=[shape((block, count), jnp.bfloat16)] * 2,
        compiler_params=limit(48),
        cost_estimate=cost(4 * block * rows * count, 2 * rows * count + 8 * block * count),
        name="keep_rows",
    )(index, left_t, left_t, right, got, got)


def keep_columns_kernel(index_ref, left_ref, right_a_ref, right_b_ref, ra_ref, rb_ref, oa_ref, ob_ref):
    left = left_ref[...]
    for right, got, out in ((right_a_ref, ra_ref, oa_ref), (right_b_ref, rb_ref, ob_ref)):
        out[...] = (nn(left, right[...]) + got[...].astype(jnp.float32)).astype(out.dtype)


def away_columns(index, left_t, right, tile):
    height, rows = left_t.shape
    half = right.shape[1] // 2
    per = half // tile
    return pl.pallas_call(
        away_kernel,
        grid_spec=pltpu.PrefetchScalarGridSpec(
            num_scalar_prefetch=1,
            grid=(per,),
            in_specs=[
                pl.BlockSpec((height, rows), lambda t, s: (0, 0)),
                pl.BlockSpec((rows, tile), lambda t, s: (0, s[0] * per + t)),
            ],
            out_specs=pl.BlockSpec((height, tile), lambda t, s: (0, t)),
        ),
        out_shape=shape((height, half), jnp.bfloat16),
        compiler_params=limit(48),
        cost_estimate=cost(2 * height * rows * half, 2 * rows * half + 2 * height * half),
        name="away_columns",
    )(index, left_t, right)


def keep_columns(index, left_t, right, got, tile):
    height, rows = left_t.shape
    block = right.shape[1] // 4
    per = block // tile
    out = pl.BlockSpec((height, tile), lambda t, s: (0, t))
    return pl.pallas_call(
        keep_columns_kernel,
        grid_spec=pltpu.PrefetchScalarGridSpec(
            num_scalar_prefetch=1,
            grid=(per,),
            in_specs=[
                pl.BlockSpec((height, rows), lambda t, s: (0, 0)),
                pl.BlockSpec((rows, tile), lambda t, s: (0, s[1] * per + t)),
                pl.BlockSpec((rows, tile), lambda t, s: (0, s[2] * per + t)),
                pl.BlockSpec((height, tile), lambda t, s: (0, s[3] * per + t)),
                pl.BlockSpec((height, tile), lambda t, s: (0, (1 - s[3]) * per + t)),
            ],
            out_specs=[out, out],
        ),
        out_shape=[shape((height, block), jnp.bfloat16)] * 2,
        compiler_params=limit(48),
        cost_estimate=cost(4 * height * rows * block, 4 * rows * block + 8 * height * block),
        name="keep_columns",
    )(index, left_t, right, right, got, got)


def input_kernel(ga_ref, gb_ref, wa_ref, wb_ref, attn_ref, out_ref, acc):
    step = pl.program_id(0)

    @pl.when(step == 0)
    def _():
        acc[...] = attn_ref[...]

    acc[...] += nn(ga_ref[0], wa_ref[0]) + nn(gb_ref[0], wb_ref[0])

    @pl.when(step == pl.num_programs(0) - 1)
    def _():
        out_ref[...] = acc[...].astype(out_ref.dtype)


def input_rows_of(grads_a, grads_b, qkv_t, grad_attn):
    rows = grad_attn.shape[0]
    wide, narrow = grads_a.shape[2], grads_b.shape[2]
    fixed = lambda i: (0, 0)
    return pl.pallas_call(
        input_kernel,
        grid=(3,),
        in_specs=[
            pl.BlockSpec((1, rows, wide), lambda i: (i, 0, 0)),
            pl.BlockSpec((1, rows, narrow), lambda i: (i, 0, 0)),
            pl.BlockSpec((1, wide, DIM), lambda i: (i, 0, 0)),
            pl.BlockSpec((1, narrow, DIM), lambda i: (i, wide // narrow, 0)),
            pl.BlockSpec((rows, DIM), fixed),
        ],
        out_specs=pl.BlockSpec((rows, DIM), fixed),
        out_shape=shape((rows, DIM), jnp.bfloat16),
        scratch_shapes=[pltpu.VMEM((rows, DIM), jnp.float32)],
        compiler_params=limit(48),
        cost_estimate=cost(6 * rows * DIM * DIM, 14 * rows * DIM),
        name="input_rows",
    )(grads_a, grads_b, qkv_t.reshape(3, DIM, DIM), qkv_t.reshape(3, DIM, DIM), grad_attn)


def gram_schmidt_kernel(left_ref, basis_ref, *, segments):
    row = lax.broadcasted_iota(jnp.int32, (RANK, 1), 0)
    for start, width in segments:
        values = left_ref[:, start : start + width]
        for column in range(RANK):
            vector = values[column : column + 1]
            vector = vector * lax.rsqrt(jnp.sum(vector * vector, axis=1, keepdims=True) + 1e-06)
            weights = jnp.sum(values * vector, axis=1, keepdims=True)
            later = values - weights * vector
            values = jnp.where(row > column, later, jnp.where(row == column, vector, values))
        basis_ref[:, start : start + width] = values


def compress(merged, starts, masters, moments, rates, rep, rider=None):
    highest = lax.Precision.HIGHEST
    lefts = []
    places = []
    segments = []
    at = 0
    for block, start_set in zip(merged, starts):
        left = lax.dot_general(start_set[0], block, (((0,), (1,)), ((), ())), precision=highest)
        size = left.shape[1]
        padded = (size + 255) // 256 * 256
        lefts.append(jnp.pad(left, ((0, 0), (0, padded - size))))
        places.append((at, size))
        segments.append((at, padded))
        at += padded
    if rider is not None:
        lefts.append(rider)
    packed = plane_sum(jnp.concatenate(lefts, axis=1)) / REPS
    rider = packed[:, at:]
    packed = packed[:, :at]
    basis_all = pl.pallas_call(
        functools.partial(gram_schmidt_kernel, segments=tuple(segments)),
        out_shape=shape(packed.shape, jnp.float32),
        name="gram_schmidt",
    )(packed)
    bases = [basis_all[:, at : at + size] for at, size in places]
    pulled = [jnp.dot(basis, block, precision=highest) for basis, block in zip(bases, merged)]
    widths = [part.shape[1] for part in pulled]
    summed = plane_sum_half(jnp.concatenate(pulled, axis=1)) / REPS
    results = []
    at = 0
    for block, basis, size, master, moment, rate in zip(
        merged, bases, widths, masters, moments, rates
    ):
        factor = summed[:, at : at + size]
        at += size
        approx = lax.dot_general(basis, factor, (((0,), (0,)), ((), ())), precision=highest)
        col_count = master.shape[1]
        piece = lax.dynamic_slice_in_dim(factor, rep * col_count, col_count, 1)
        piece = lax.dot_general(basis, piece, (((0,), (0,)), ((), ())), precision=highest)
        moment_new = MOMENTUM * moment + piece
        results.append(
            (master - rate * moment_new, moment_new, (block - approx)[None], basis.T, factor.T[None])
        )
    return results, rider


def fast_device(
    tokens,
    cotangent,
    lengths,
    w_qkv,
    w_out,
    w_gate_up,
    w_down,
    mom_qkv,
    mom_out,
    mom_gate_up,
    mom_down,
    err_qkv,
    err_out,
    err_gate_up,
    err_down,
    start_qkv,
    start_out,
    start_gate_up,
    start_down,
    layer_norm_gains,
    layer_norm_biases,
    norm_moments,
):
    f32 = jnp.float32
    bf16 = jnp.bfloat16
    rep = lax.axis_index("rep")
    shard = lax.axis_index("shard")
    core = rep % 2
    local_len, width = tokens.shape[1:]
    scale = HD ** (-0.5)

    def spread(values, *before):
        parts = []
        for parity in (0, 1):
            sent = lax.dynamic_index_in_dim(values, (shard + parity) % 2, 0, keepdims=False)
            parts.append(send(sent, spread_move(parity)))
        return after(parts, *before)

    def bring_back(rows):
        first = send(rows[:local_len], gather_move(0))
        second = send(rows[local_len:], gather_move(1))
        even = shard % 2 == 0
        return jnp.stack([jnp.where(even, first, second), jnp.where(even, second, first)])

    side = jnp.concatenate(
        [
            w_gate_up.astype(bf16),
            w_down.astype(bf16).T,
            w_out.astype(bf16).T.reshape(24, width),
        ],
        axis=0,
    )
    gathered = lax.all_gather(side, "shard", axis=0)
    qkv_piece = jnp.concatenate(shard_gather(w_qkv.astype(bf16).T, shard), axis=1)
    qkv_near = plane_near(qkv_piece)
    rows_in = jnp.concatenate(spread(tokens), axis=0)
    qkv_far = plane_far(qkv_piece, qkv_near)
    both = jnp.stack([lengths, sibling(lengths)])
    group = shard // 2
    length = both[jnp.where(group == core, 0, 1), shard % 2]
    qkv_others = exchange(qkv_piece, qkv_near, qkv_far)
    inside = jnp.arange(local_len, dtype=jnp.int32)

    def starts_of(k):
        first = 2 * k + shard % 2
        second = 2 * k + 1 - shard % 2
        return [first * local_len, second * local_len]

    place = jnp.stack(
        starts_of(core) + starts_of(1 - core) + [length, jnp.zeros_like(length), local_len + 0 * length]
    ).astype(jnp.int32)
    qkv_t = plane_all(
        qkv_piece, qkv_near, qkv_far, qkv_others, rep, (gathered.reshape(-1, width), place)
    )
    qkv_t = qkv_t.reshape(3 * width, width)
    position = jnp.concatenate([place[0] + inside, place[1] + inside])
    inverse = jnp.exp(
        jnp.arange(HD // 2, dtype=jnp.int32).astype(f32) * (-2.0 * math.log(ROPE_BASE) / HD)
    )
    angle = position.astype(f32)[:, None] * inverse[None, :]
    cosine, sine = jnp.cos(angle), jnp.sin(angle)
    cos = jnp.concatenate([cosine] * 4, axis=1)
    sin = jnp.concatenate([-sine, sine] * 2, axis=1)

    kv = project(rows_in, qkv_t, cos, sin, 1, 2, 1, 1.0)
    kv_other = sibling(kv)
    q = project(rows_in, qkv_t, cos, sin, 0, 1, None, scale)
    out_piece = gathered[:, 288:].reshape(SHARDS, 96, 192).transpose(1, 0, 2)
    piece = jnp.concatenate(
        [
            gathered[:, :192].reshape(width, width),
            out_piece.reshape(96, width),
            gathered[:, 192:288].reshape(384, width),
        ],
        axis=0,
    )
    near = plane_near(piece)
    first = attend(place, q, kv, kv_other, 0, 2)
    second = attend(place, q, kv, kv_other, 2, 2, first)
    near = after(near, second[1])
    far = plane_far(piece, near)
    mix, qx = attend(place, q, kv, kv_other, 4, 2, second)
    others = [sibling(part) for part in (after(piece, second[1]), *near)]
    far = after(far, qx)
    others.append(sibling(jnp.concatenate(far, axis=0)))
    stacked = plane_all(piece, near, far, others, rep)
    cot_in = spread(after(cotangent, stacked))
    hat, rstd = out_norm(mix, stacked, rows_in)
    hidden, factor, normed_half, values = feed_forward(
        hat, layer_norm_gains, layer_norm_biases, stacked
    )
    mixed, grad_second, branch, vec_two = norm_back(
        place, values, layer_norm_gains, layer_norm_biases, cot_in
    )
    mixed_out = bring_back(mixed)

    other = 1 - core
    shard_own = jnp.where((shard == 0) | (shard == 3), 0, 1)
    kept = jnp.where(core == 0, shard_own, 3 - shard_own)
    index = jnp.stack([other, kept, 4 * core + 1 - kept, kept - 2 * core]).astype(jnp.int32)
    owner = core == shard // 2

    def kept_rows(values, at):
        parts = values.reshape(2, 2, -1, values.shape[2])
        return lax.dynamic_index_in_dim(parts, at, 1, keepdims=False).astype(f32)

    near = index[3]

    def core_sum(keep, got):
        mine = (kept_rows(keep, near) + kept_rows(got, near)).astype(bf16)
        theirs = (kept_rows(keep, 1 - near) + kept_rows(got, 1 - near)).astype(bf16)
        return mine, theirs

    def add(mine, pair):
        return (mine.astype(f32) + pair.astype(f32)).astype(bf16)

    branch_t = branch.T
    down_got = sibling(away_columns(index, branch_t, hidden, DIM))
    normed_t = normed_half.T
    away_1, keep_1, partial = feed_back(
        index, grad_second, branch, factor, stacked, normed_t, 0
    )
    got_1 = sibling(away_1)
    down_mine, down_theirs = keep_columns(index, branch_t, hidden, down_got, DIM)
    down_pair = pair_z(down_theirs)
    away_2, keep_2, grad_attn, grad_attn_half, grad_mix, vec_one = feed_back(
        index, after(partial, down_mine, down_theirs, mixed_out), branch, factor,
        stacked, normed_t, 2, (hat, rstd, layer_norm_gains, stacked),
    )
    got_2 = sibling(away_2)
    first_mine, first_theirs = core_sum(after(keep_1, grad_mix), got_1)
    first_pair = pair_z(first_theirs)
    mix_t = mix.T
    out_got = sibling(away_rows(index, mix_t, grad_attn_half, DIM))
    down_sum = add(down_mine, after(down_pair, grad_mix))
    down_far = to_owner(down_sum)

    def back(grads, kv_set, at, first, count, more=()):
        return attend_back(place, qx, kv_set, grads, mix, at, first, count, scale, more)

    def join(pair, single):
        return jnp.concatenate([pair[0], pair[1], single], axis=1)

    vectors = jnp.concatenate([vec_one, vec_two], axis=0)
    grads = after(grad_mix, first_mine, first_theirs, down_sum)
    dq_2, dk_2, dv_2 = back(grads, kv_other, 2, 4, 2)
    other_2 = sibling(dk_2), sibling(dv_2)
    second_mine, second_theirs = core_sum(keep_2, after(got_2, dq_2))
    out_mine, out_theirs = keep_rows(index, mix_t, grad_attn_half, after(out_got, dq_2), DIM)
    second_mine = join(second_mine, out_mine)
    second_theirs = join(second_theirs, out_theirs)
    second_pair = pair_z(second_theirs)
    vectors = after(vectors, dq_2)
    vectors_pair = pair_z(vectors)
    grads = after(grads, second_mine, second_theirs)
    dq_1, dk_1, dv_1 = back(grads, kv_other, 2, 0, 4)
    other_1 = sibling(dk_1), sibling(dv_1)
    first_sum = add(first_mine, after(first_pair, dq_1))
    first_far = to_owner(first_sum)
    down_far = after(down_far, dq_1)
    vectors = vectors + after(vectors_pair, dq_1)
    vectors_mirror = mirror_z(vectors)
    grads = after(grads, first_sum)
    grads_b = back(grads, kv, 0, 4, 2, (dq_2, *other_2, cos, sin))
    second_sum = add(second_mine, after(second_pair, grads_b))
    second_far = to_owner(second_sum)
    tokens_t = rows_in.T
    qkv_got_b = sibling(away_rows(index, tokens_t, grads_b, 256))
    vectors = vectors + after(vectors_mirror, grads_b)
    grads = after(grads, second_sum)
    grads_a = back(grads, kv, 0, 0, 4, (dq_1, *other_1, cos, sin))
    qkv_got_a = sibling(away_rows(index, tokens_t, grads_a, 512))
    qkv_mine_b, qkv_theirs_b = keep_rows(index, tokens_t, grads_b, after(qkv_got_b, grads_a), 256)
    qkv_mine_a, qkv_theirs_a = keep_rows(index, tokens_t, grads_a, qkv_got_a, 512)
    qkv_theirs = jnp.concatenate([qkv_theirs_a, qkv_theirs_b], axis=1)
    qkv_mine = jnp.concatenate([qkv_mine_a, qkv_mine_b], axis=1)
    qkv_pair = pair_z(qkv_theirs)
    input_rows = input_rows_of(grads_a, grads_b, qkv_t, after(grad_attn, qkv_theirs))
    qkv_sum = add(qkv_mine, after(qkv_pair, input_rows))
    qkv_far = to_owner(qkv_sum)
    input_grad = bring_back(after(input_rows, qkv_sum)).astype(f32)

    def owned(own, far):
        return jnp.where(owner, own, far).astype(f32)

    own_down = lax.optimization_barrier(jnp.where(owner, down_sum, down_far).T).astype(f32)
    own_first = owned(first_sum, first_far)
    own_second = owned(second_sum, second_far)
    half_ff = FF // 2
    own_gate_up = jnp.concatenate(
        [own_first[0], own_second[:, :half_ff], own_first[1], own_second[:, half_ff:FF]], axis=1
    )
    own_out = own_second[:, FF:]
    own_qkv = owned(qkv_sum, qkv_far)
    own_qkv = jnp.concatenate(
        [
            part
            for i in range(3)
            for part in (
                own_qkv[:, 512 * i : 512 * i + 512],
                own_qkv[:, 1536 + 256 * i : 1792 + 256 * i],
            )
        ],
        axis=1,
    )

    early, norm_grad = compress(
        (own_out + err_out[0], own_gate_up + err_gate_up[0], own_down + err_down[0]),
        (start_out, start_gate_up, start_down),
        (w_out, w_gate_up, w_down),
        (mom_out, mom_gate_up, mom_down),
        LEARN_RATES[1:],
        rep,
        vectors.reshape(RANK, width // 2),
    )
    norm_grad = norm_grad.reshape(4, width)
    params = jnp.stack(
        [layer_norm_gains[0], layer_norm_biases[0], layer_norm_gains[1], layer_norm_biases[1]]
    )
    norm_moment_new = MOMENTUM * norm_moments + norm_grad
    norm_new = params - NORM_RATE * norm_moment_new
    late, _ = compress(
        (after(own_qkv, *early[1][:3]) + err_qkv[0],), (start_qkv,), (w_qkv,), (mom_qkv,),
        LEARN_RATES[:1], rep,
    )
    results = late + early
    new_weights, new_moments, new_errors, bases, factors = zip(*results)
    return (
        mixed_out,
        input_grad,
        *new_weights,
        *new_moments,
        *new_errors,
        *bases,
        *factors,
        norm_moment_new,
        norm_new,
    )


def choose(mesh):
    if mesh.shape["rep"] == REPS and mesh.shape["shard"] == SHARDS:
        return fast_device
    return general_device


def solution(mesh):
    placed = (
        P("rep", "shard", None),
        P("rep", "shard", None),
        P("rep"),
        P("shard", "rep"),
        P("shard", "rep"),
        P("shard", "rep"),
        P("shard", "rep"),
        P("shard", "rep"),
        P("shard", "rep"),
        P("shard", "rep"),
        P("shard", "rep"),
        P("rep", "shard", None),
        P("rep", "shard", None),
        P("rep", "shard", None),
        P("rep", "shard", None),
        P("shard", None, None),
        P("shard", None, None),
        P("shard", None, None),
        P("shard", None, None),
        P(),
        P(),
        P(),
    )
    return jax.shard_map(
        choose(mesh),
        mesh=mesh,
        in_specs=placed,
        out_specs=(
            P("rep", "shard", None),
            P("rep", "shard", None),
            P("shard", "rep"),
            P("shard", "rep"),
            P("shard", "rep"),
            P("shard", "rep"),
            P("shard", "rep"),
            P("shard", "rep"),
            P("shard", "rep"),
            P("shard", "rep"),
            P("rep", "shard", None),
            P("rep", "shard", None),
            P("rep", "shard", None),
            P("rep", "shard", None),
            P("shard", None),
            P("shard", None),
            P("shard", None),
            P("shard", None),
            P("shard", None, None),
            P("shard", None, None),
            P("shard", None, None),
            P("shard", None, None),
            P(),
            P(),
        ),
        check_vma=False,
    )
```

```python
import functools
import math

import jax
import jax.numpy as jnp
from jax import lax
from jax.experimental import pallas as pl
from jax.experimental.pallas import tpu as pltpu
from jax.sharding import PartitionSpec as P

H = 12
HD = 64
FF = 3072


EPS = 1e-05
ROPE_BASE = 1000.0
MOMENTUM = 0.5
LEARN_RATES = (0.002, 0.1, 0.004, 0.002)
NORM_RATE = 0.01
NEG_FILL = -1e30


def norm_components(values_in, gain, bias):
    centre = jnp.mean(values_in, axis=-1, keepdims=True)
    centred = values_in - centre
    spread = jnp.mean(centred * centred, axis=-1, keepdims=True)
    row_rstd = lax.rsqrt(spread + EPS)
    normed = centred * row_rstd
    return (normed * gain + bias, normed, row_rstd)


def norm_reverse_pass(grad_in, normed, row_rstd):
    return row_rstd * (
        grad_in
        - jnp.mean(grad_in, axis=-1, keepdims=True)
        - normed * jnp.mean(grad_in * normed, axis=-1, keepdims=True)
    )


def rotary(values_in, cosine_table, sine_table):
    half_dim = values_in.shape[-1] // 2
    leading_half = values_in[..., :half_dim]
    second_half = values_in[..., half_dim:]
    return jnp.concatenate(
        [
            leading_half * cosine_table - second_half * sine_table,
            second_half * cosine_table + leading_half * sine_table,
        ],
        axis=-1,
    )


def rotary_back(grad_in, cosine_table, sine_table):
    half_dim = grad_in.shape[-1] // 2
    leading_half = grad_in[..., :half_dim]
    second_half = grad_in[..., half_dim:]
    return jnp.concatenate(
        [
            leading_half * cosine_table + second_half * sine_table,
            second_half * cosine_table - leading_half * sine_table,
        ],
        axis=-1,
    )


def orthonormal(factor):
    columns = []
    for column in range(factor.shape[1]):
        vector = factor[:, column]
        for earlier in columns:
            vector = vector - jnp.sum(earlier * vector) * earlier
        vector = vector * lax.rsqrt(jnp.sum(vector * vector) + 1e-06)
        columns.append(vector)
    return jnp.stack(columns, axis=1)


def general_device(
    tokens,
    cotangent,
    lengths,
    w_qkv,
    w_out,
    w_gate_up,
    w_down,
    mom_qkv,
    mom_out,
    mom_gate_up,
    mom_down,
    err_qkv,
    err_out,
    err_gate_up,
    err_down,
    start_qkv,
    start_out,
    start_gate_up,
    start_down,
    layer_norm_gains,
    layer_norm_biases,
    norm_moments,
):
    single_float = jnp.float32
    bf16 = jnp.bfloat16
    wide_cols = (
        lax.all_gather(w_qkv.astype(bf16), "rep", axis=1, tiled=True),
        lax.all_gather(w_out.astype(bf16), "rep", axis=1, tiled=True),
        lax.all_gather(w_gate_up.astype(bf16), "rep", axis=1, tiled=True),
        lax.all_gather(w_down.astype(bf16), "rep", axis=1, tiled=True),
    )
    complete_query_key_value, complete_out_weight, complete_gate_up_weight, complete_down_weight = (
        lax.all_gather(wide_cols[0], "shard", axis=0, tiled=True),
        lax.all_gather(wide_cols[1], "shard", axis=0, tiled=True),
        lax.all_gather(wide_cols[2], "shard", axis=0, tiled=True),
        lax.all_gather(wide_cols[3], "shard", axis=0, tiled=True),
    )
    groups, local_len, model_width = tokens.shape
    shards = lax.axis_size("shard")
    seq_len = local_len * shards
    score_scale = HD ** (-0.5)
    offset = lax.axis_index("shard") * local_len
    position = offset + jnp.arange(local_len, dtype=jnp.int32)
    valid_rows = position[None, :] < lengths[:, None]
    key_keep = jnp.arange(seq_len, dtype=jnp.int32)[None, :] < lengths[:, None]
    inverse = jnp.exp(
        jnp.arange(HD // 2, dtype=jnp.int32).astype(single_float)
        * (-2.0 * math.log(ROPE_BASE) / HD)
    )
    angle = position.astype(single_float)[:, None] * inverse[None, :]
    cosine_table = jnp.cos(angle)[:, None, :]
    sine_table = jnp.sin(angle)[:, None, :]
    query_key_value_rows = jnp.einsum(
        "znk,kb->znb", tokens, complete_query_key_value, preferred_element_type=single_float
    )
    query_key_value_rows = query_key_value_rows.reshape(groups, local_len, 3, H, HD)
    q_half = (
        rotary(query_key_value_rows[:, :, 0], cosine_table, sine_table)
        .astype(bf16)
        .transpose(2, 0, 1, 3)
    )
    k_half = (
        rotary(query_key_value_rows[:, :, 1], cosine_table, sine_table)
        .astype(bf16)
        .transpose(2, 0, 1, 3)
    )
    v_half = query_key_value_rows[:, :, 2].astype(bf16).transpose(2, 0, 1, 3)
    key_all, value_all = (
        lax.all_gather(k_half, "shard", axis=2, tiled=True),
        lax.all_gather(v_half, "shard", axis=2, tiled=True),
    )

    def head_forward(inputs):
        query_h, key_h, value_h = inputs
        scores = (
            jnp.einsum("sqd,skd->sqk", query_h, key_h, preferred_element_type=single_float)
            * score_scale
        )
        scores = jnp.where(key_keep[:, None, :], scores, NEG_FILL)
        row_peak = jnp.max(scores, axis=-1, keepdims=True)
        exp_scores = jnp.exp(scores - row_peak)
        row_total = jnp.sum(exp_scores, axis=-1, keepdims=True)
        attn_probs = (exp_scores / row_total).astype(bf16)
        head_rows = jnp.einsum(
            "sqk,skd->sqd", attn_probs, value_h, preferred_element_type=single_float
        )
        return (head_rows, (row_peak + jnp.log(row_total))[..., 0])

    head_out, log_total = lax.map(head_forward, (q_half, key_all, value_all))
    mix_half = head_out.astype(bf16)
    mixture_rows = mix_half.transpose(1, 2, 0, 3).reshape(groups, local_len, model_width)
    attention_result = jnp.einsum(
        "znk,kb->znb", mixture_rows, complete_out_weight, preferred_element_type=single_float
    )
    attention_normed, attention_standardized, attention_inverse_deviation = norm_components(
        tokens.astype(single_float) + attention_result, layer_norm_gains[0], layer_norm_biases[0]
    )
    leading_half = attention_normed.astype(bf16)
    gate_up_output = jnp.einsum(
        "znk,kb->znb", leading_half, complete_gate_up_weight, preferred_element_type=single_float
    )
    gate_part = gate_up_output[..., :FF]
    up_part = gate_up_output[..., FF:]
    gate_sig = jax.nn.sigmoid(gate_part)
    hidden_state = (gate_part * gate_sig * up_part).astype(bf16)
    residual_branch = jnp.einsum(
        "ckh,hy->cky", hidden_state, complete_down_weight, preferred_element_type=single_float
    )
    feedforward_normed, feedforward_standardized, feedforward_inverse_deviation = norm_components(
        attention_normed + residual_branch, layer_norm_gains[1], layer_norm_biases[1]
    )
    mixed_out = feedforward_normed.astype(bf16)
    output_gradient = cotangent.astype(single_float) * valid_rows[..., None].astype(single_float)
    feedforward_gain = jnp.sum(output_gradient * feedforward_standardized, axis=(0, 1))
    bias_two = jnp.sum(output_gradient, axis=(0, 1))
    trailing_norm_gradient = norm_reverse_pass(
        output_gradient * layer_norm_gains[1],
        feedforward_standardized,
        feedforward_inverse_deviation,
    )
    branch_gradient = trailing_norm_gradient.astype(bf16)
    down_weight_gradient = jnp.einsum(
        "zxi,zxp->ip", hidden_state, branch_gradient, preferred_element_type=single_float
    )
    hidden_gradient = jnp.einsum(
        "gbz,wz->gbw", branch_gradient, complete_down_weight, preferred_element_type=single_float
    )
    grad_gate = hidden_gradient * up_part * gate_sig * (1.0 + gate_part * (1.0 - gate_sig))
    grad_up = hidden_gradient * gate_part * gate_sig
    gate_up_gradient = jnp.concatenate([grad_gate, grad_up], axis=-1).astype(bf16)
    gate_up_weight_gradient = jnp.einsum(
        "vcm,vcb->mb", leading_half, gate_up_gradient, preferred_element_type=single_float
    )
    leading_norm_gradient = (
        jnp.einsum(
            "thi,ci->thc",
            gate_up_gradient,
            complete_gate_up_weight,
            preferred_element_type=single_float,
        )
        + trailing_norm_gradient
    )
    attention_gain = jnp.sum(leading_norm_gradient * attention_standardized, axis=(0, 1))
    bias_one = jnp.sum(leading_norm_gradient, axis=(0, 1))
    attention_gradient = norm_reverse_pass(
        leading_norm_gradient * layer_norm_gains[0],
        attention_standardized,
        attention_inverse_deviation,
    )
    attention_gradient_half = attention_gradient.astype(bf16)
    out_weight_gradient = jnp.einsum(
        "vcm,vcb->mb", mixture_rows, attention_gradient_half, preferred_element_type=single_float
    )
    mixture_gradient = jnp.einsum(
        "thi,ci->thc",
        attention_gradient_half,
        complete_out_weight,
        preferred_element_type=single_float,
    )
    grad_mix_half = (
        mixture_gradient.astype(bf16).reshape(groups, local_len, H, HD).transpose(2, 0, 1, 3)
    )

    def head_back(inputs):
        query_h, key_h, value_h, grad_h, lse_h = inputs
        scores = (
            jnp.einsum("sqd,skd->sqk", query_h, key_h, preferred_element_type=single_float)
            * score_scale
        )
        scores = jnp.where(key_keep[:, None, :], scores, NEG_FILL)
        attn_probs = jnp.exp(scores - lse_h[..., None])
        grad_probs = jnp.einsum(
            "sqd,skd->sqk", grad_h, value_h, preferred_element_type=single_float
        )
        row_delta = jnp.sum(grad_probs * attn_probs, axis=-1, keepdims=True)
        grad_scores = (attn_probs * (grad_probs - row_delta)).astype(bf16)
        grad_query = (
            jnp.einsum("sqk,skd->sqd", grad_scores, key_h, preferred_element_type=single_float)
            * score_scale
        )
        grad_key = (
            jnp.einsum("sqk,sqd->skd", grad_scores, query_h, preferred_element_type=single_float)
            * score_scale
        )
        grad_value = jnp.einsum(
            "sqk,sqd->skd", attn_probs.astype(bf16), grad_h, preferred_element_type=single_float
        )
        return (grad_query, grad_key, grad_value)

    grad_q_heads, key_parts, value_parts = lax.map(
        head_back, (q_half, key_all, value_all, grad_mix_half, log_total)
    )
    grad_k_heads, grad_v_heads = (
        lax.psum_scatter(key_parts, "shard", scatter_dimension=2, tiled=True),
        lax.psum_scatter(value_parts, "shard", scatter_dimension=2, tiled=True),
    )
    grad_q_rows = rotary_back(grad_q_heads.transpose(1, 2, 0, 3), cosine_table, sine_table)
    grad_k_rows = rotary_back(grad_k_heads.transpose(1, 2, 0, 3), cosine_table, sine_table)
    grad_v_rows = grad_v_heads.transpose(1, 2, 0, 3)
    query_key_value_gradient = jnp.stack([grad_q_rows, grad_k_rows, grad_v_rows], axis=2)
    query_key_value_gradient = query_key_value_gradient.reshape(
        groups, local_len, 3 * model_width
    ).astype(bf16)
    query_key_value_weight_gradient = jnp.einsum(
        "vcm,vcb->mb", tokens, query_key_value_gradient, preferred_element_type=single_float
    )
    input_grad = (
        jnp.einsum(
            "thi,ci->thc",
            query_key_value_gradient,
            complete_query_key_value,
            preferred_element_type=single_float,
        )
        + attention_gradient
    )
    owned = (
        lax.psum_scatter(
            query_key_value_weight_gradient.astype(jnp.bfloat16),
            "shard",
            scatter_dimension=0,
            tiled=True,
        ).astype(jnp.float32),
        lax.psum_scatter(
            out_weight_gradient.astype(jnp.bfloat16), "shard", scatter_dimension=0, tiled=True
        ).astype(jnp.float32),
        lax.psum_scatter(
            gate_up_weight_gradient.astype(jnp.bfloat16), "shard", scatter_dimension=0, tiled=True
        ).astype(jnp.float32),
        lax.psum_scatter(
            down_weight_gradient.astype(jnp.bfloat16), "shard", scatter_dimension=0, tiled=True
        ).astype(jnp.float32),
    )
    replicas = lax.axis_size("rep")
    vector_parts = jnp.stack([attention_gain, bias_one, feedforward_gain, bias_two])
    norm_grad = lax.psum(vector_parts, ("rep", "shard")) / replicas
    params = jnp.stack(
        [layer_norm_gains[0], layer_norm_biases[0], layer_norm_gains[1], layer_norm_biases[1]]
    )
    norm_moment_new = MOMENTUM * norm_moments + norm_grad
    norm_new = params - NORM_RATE * norm_moment_new
    errors = (err_qkv, err_out, err_gate_up, err_down)
    starts = (start_qkv, start_out, start_gate_up, start_down)
    masters = (w_qkv, w_out, w_gate_up, w_down)
    moments = (mom_qkv, mom_out, mom_gate_up, mom_down)
    merged = tuple((part + error_set[0] for part, error_set in zip(owned, errors)))
    projected = tuple(
        (
            jnp.dot(block, start_set[0], precision=lax.Precision.HIGHEST)
            for block, start_set in zip(merged, starts)
        )
    )
    summed_left = lax.psum((projected[0], projected[1], projected[2], projected[3]), "rep")
    bases = tuple((orthonormal(part / replicas) for part in summed_left))
    pulled = tuple(
        (
            jnp.einsum("rc,rk->ck", block, basis, precision=lax.Precision.HIGHEST)
            for block, basis in zip(merged, bases)
        )
    )
    summed_right = (
        lax.psum(pulled[0].astype(jnp.bfloat16), "rep").astype(jnp.float32),
        lax.psum(pulled[1].astype(jnp.bfloat16), "rep").astype(jnp.float32),
        lax.psum(pulled[2].astype(jnp.bfloat16), "rep").astype(jnp.float32),
        lax.psum(pulled[3].astype(jnp.bfloat16), "rep").astype(jnp.float32),
    )
    factors = tuple((part / replicas for part in summed_right))
    rep_pos = lax.axis_index("rep")
    new_weights = []
    new_moments = []
    new_errors = []
    for block, basis, factor, master, moment, step_rate in zip(
        merged, bases, factors, masters, moments, LEARN_RATES
    ):
        approx = jnp.dot(basis, factor.T, precision=lax.Precision.HIGHEST)
        new_errors.append((block - approx)[None])
        col_count = master.shape[1]
        piece = lax.dynamic_slice_in_dim(approx, rep_pos * col_count, col_count, 1)
        moment_new = MOMENTUM * moment + piece
        new_moments.append(moment_new)
        new_weights.append(master - step_rate * moment_new)
    return (
        mixed_out,
        input_grad,
        new_weights[0],
        new_weights[1],
        new_weights[2],
        new_weights[3],
        new_moments[0],
        new_moments[1],
        new_moments[2],
        new_moments[3],
        new_errors[0],
        new_errors[1],
        new_errors[2],
        new_errors[3],
        bases[0],
        bases[1],
        bases[2],
        bases[3],
        factors[0][None],
        factors[1][None],
        factors[2][None],
        factors[3][None],
        norm_moment_new,
        norm_new,
    )


AXES = ("rep", "shard")
SHARDS = 4
REPS = 8
RANK = 8
DIM = 768
PAIRS = 6
LANES = 128
MIB = 2**20


def send(values, move):
    pairs = []
    for rep in range(REPS):
        for shard in range(SHARDS):
            to = move(rep, shard)
            if to is not None:
                pairs.append((rep * SHARDS + shard, to[0] * SHARDS + to[1]))
    return lax.ppermute(values, AXES, pairs)


def spread_move(parity):
    return lambda r, z: (r - r % 2 + z // 2, 2 * (r % 2) + (z + parity) % 2)


def gather_move(parity):
    table = {}
    for r in range(REPS):
        for z in range(SHARDS):
            table[spread_move(parity)(r, z)] = (r, z)
    return lambda r, z: table[(r, z)]


def sibling(values):
    return send(values, lambda r, z: (r ^ 1, z))


def near_x(values):
    return send(values, lambda r, z: (r ^ 2, z))


def near_y(values):
    return send(values, lambda r, z: (r ^ 4, z))


def pair_z(values):
    return send(values, lambda r, z: (r, z ^ 1))


def mirror_z(values):
    return send(values, lambda r, z: (r, 3 - z))


def to_owner(values):
    return send(values, lambda r, z: (r ^ 1, 3 - z) if r % 2 != z // 2 else None)


def turn_z(values, step):
    return send(values, lambda r, z: (r, (z + step) % SHARDS))


def after(values, *others):
    return lax.optimization_barrier((values, *others))[0]


def shard_gather(piece, shard):
    parts = jnp.stack([piece] + [turn_z(piece, step) for step in (1, 2, 3)])
    return [
        lax.dynamic_index_in_dim(parts, (shard - at) % SHARDS, 0, keepdims=False)
        for at in range(SHARDS)
    ]


def plane_near(piece):
    return near_x(piece), near_y(piece)


def plane_far(piece, near):
    half = piece.shape[0] // 2
    from_x, from_y = near
    return near_x(from_y[:half]), near_y(from_x[half:])


def exchange(piece, near, far):
    return [sibling(part) for part in (piece, *near, jnp.concatenate(far, axis=0))]


def plane_all(piece, near, far, others, rep, ahead=()):
    return stack_pieces((piece, *near, *far, *others), rep, *piece.shape, ahead)


PIECE_STEPS = ((0, None), (2, None), (4, None), (6, 0), (6, 1), (1, None), (3, None), (5, None), (7, None))


def stack_kernel(rep_ref, *refs):
    count = len(PIECE_STEPS)
    pieces = refs[:count]
    whole, staged, sems_in, sems_out = refs[-4:]
    rep = rep_ref[0]
    half = pieces[3].shape[0]
    fetches = []
    stores = []
    for slot, (step, side) in enumerate(PIECE_STEPS):
        stage = staged.at[step]
        place = whole.at[rep ^ step]
        if side is not None:
            part = pl.ds(side * half, half)
            stage = stage.at[part]
            place = place.at[part]
        fetches.append(pltpu.make_async_copy(pieces[slot], stage, sems_in.at[slot]))
        stores.append(pltpu.make_async_copy(stage, place, sems_out.at[slot]))
    for fetch in fetches:
        fetch.start()
    for fetch, store in zip(fetches, stores):
        fetch.wait()
        store.start()
    for store in stores:
        store.wait()


def stack_pieces(pieces, rep, rows, cols, ahead):
    anywhere = pl.BlockSpec(memory_space=pl.ANY)
    count = len(pieces)
    return pl.pallas_call(
        stack_kernel,
        in_specs=[pl.BlockSpec(memory_space=pltpu.SMEM)] + [anywhere] * (count + len(ahead)),
        out_specs=anywhere,
        out_shape=jax.ShapeDtypeStruct((REPS, rows, cols), pieces[0].dtype),
        scratch_shapes=[
            pltpu.VMEM((REPS, rows, cols), pieces[0].dtype),
            pltpu.SemaphoreType.DMA((count,)),
            pltpu.SemaphoreType.DMA((count,)),
        ],
        compiler_params=limit(40),
        cost_estimate=pl.CostEstimate(
            flops=0, bytes_accessed=4 * REPS * rows * cols, transcendentals=0
        ),
        name="stack_pieces",
    )(jnp.reshape(rep, (1,)), *pieces, *ahead)


def plane_sum(values):
    values = values + sibling(values)
    values = values + near_x(values)
    return values + near_y(values)


def plane_sum_half(values):
    bf16 = jnp.bfloat16
    f32 = jnp.float32
    for step in (sibling, near_x, near_y):
        rounded = values.astype(bf16)
        values = rounded.astype(f32) + step(rounded).astype(f32)
    return values


def nt(left, right):
    return lax.dot_general(
        left, right, (((1,), (1,)), ((), ())), preferred_element_type=jnp.float32
    )


def nn(left, right):
    return lax.dot_general(
        left, right, (((1,), (0,)), ((), ())), preferred_element_type=jnp.float32
    )


def cost(flops, moved, powers=0):
    return pl.CostEstimate(flops=int(flops), bytes_accessed=int(moved), transcendentals=int(powers))


def limit(mib):
    return pltpu.CompilerParams(vmem_limit_bytes=mib * MIB)


def shape(dims, dtype):
    return jax.ShapeDtypeStruct(dims, dtype)


def partner_lanes(values):
    lane = lax.broadcasted_iota(jnp.int32, values.shape, 1)
    up = pltpu.roll(values, 96, 1)
    down = pltpu.roll(values, 32, 1)
    return jnp.where(lane % HD < HD // 2, up, down)


def project_kernel(x_ref, w_ref, cos_ref, sin_ref, out_ref, *, turned, scale):
    values = nt(x_ref[...], w_ref[...])

    def turn():
        for at in range(0, values.shape[1], LANES):
            part = values[:, at : at + LANES]
            part = part * cos_ref[...] + partner_lanes(part) * sin_ref[...]
            out_ref[:, at : at + LANES] = (part * scale).astype(out_ref.dtype)

    if turned is None:
        turn()
    else:
        pl.when(pl.program_id(0) < turned)(turn)

        @pl.when(pl.program_id(0) >= turned)
        def _():
            out_ref[...] = values.astype(out_ref.dtype)


def project(rows_in, qkv_t, cos, sin, first, count, turned, scale):
    rows = rows_in.shape[0]
    tile = DIM
    fixed = lambda j: (0, 0)
    return pl.pallas_call(
        functools.partial(project_kernel, turned=turned, scale=scale),
        grid=(count,),
        in_specs=[
            pl.BlockSpec((rows, DIM), fixed),
            pl.BlockSpec((tile, DIM), lambda j: (j + first, 0)),
            pl.BlockSpec((rows, LANES), fixed),
            pl.BlockSpec((rows, LANES), fixed),
        ],
        out_specs=pl.BlockSpec((rows, tile), lambda j: (0, j)),
        out_shape=shape((rows, count * tile), jnp.bfloat16),
        compiler_params=limit(48),
        cost_estimate=cost(2 * rows * DIM * tile * count, 4 * rows * DIM + 4 * count * tile * rows),
        name="project",
    )(rows_in, qkv_t, cos, sin)


def lane_of(dims):
    return lax.broadcasted_iota(jnp.int32, dims, 1)


def head_lanes(dims, head):
    lane = lane_of(dims)
    return (lane >= HD) if head else (lane < HD)


def extra_lane(head):
    return 0 if head else HD


def key_fill(place_ref, at, count, start):
    row = lax.broadcasted_iota(jnp.int32, (count, LANES), 0) + start
    half = place_ref[6]
    position = jnp.where(row < half, place_ref[at] + row, place_ref[at + 1] + row - half)
    return jnp.where(position < place_ref[4], 0.0, NEG_FILL).astype(jnp.bfloat16)


def attend_kernel(place_ref, q_ref, ka_ref, va_ref, kb_ref, vb_ref, *refs):
    mix_ref, qx_ref, keys, values = refs[-4:]
    rows = ka_ref.shape[0]
    bf16 = jnp.bfloat16

    @pl.when(pl.program_id(1) == 0)
    def _():
        dims = (rows, LANES)
        zero = jnp.zeros(dims, bf16)
        for source, (k_ref, v_ref) in enumerate(((ka_ref, va_ref), (kb_ref, vb_ref))):
            fill = key_fill(place_ref, 2 * source, rows, 0)
            part = pl.ds(source * rows, rows)
            for head in range(2):
                inside = head_lanes(dims, head)
                other = jnp.where(lane_of(dims) == extra_lane(head), fill, zero)
                keys[head, part] = jnp.where(inside, k_ref[...], other)
                values[head, part] = jnp.where(inside, v_ref[...], zero)

    queries = q_ref[...]
    dims = queries.shape
    lane = lane_of(dims)
    total = None
    for head in range(2):
        inside = head_lanes(dims, head)
        spare = lane - extra_lane(head)
        one = jnp.where(spare == 0, 1.0, 0.0).astype(bf16)
        masked = jnp.where(inside, queries, one)
        scores = nt(masked, keys[head])
        peak = jnp.max(scores, axis=1, keepdims=True)
        powers = jnp.exp(scores - peak)
        row_sum = jnp.sum(powers, axis=1, keepdims=True)
        out = nn(powers.astype(bf16), values[head]) / row_sum
        total = out if total is None else total + out
        lse = peak + jnp.log(row_sum)
        high = lse.astype(bf16)
        middle = (lse - high.astype(jnp.float32)).astype(bf16)
        low = (lse - high.astype(jnp.float32) - middle.astype(jnp.float32)).astype(bf16)
        wide = jnp.where(spare == 1, -high, jnp.where(spare == 2, -middle, -low))
        wide = jnp.where((spare >= 1) & (spare <= 3), wide, one)
        qx_ref[:, head * LANES : (head + 1) * LANES] = jnp.where(inside, queries, wide)
    mix_ref[...] = total.astype(bf16)


def attend(place, q, kv_own, kv_other, first, count, done=()):
    rows = q.shape[0]
    block = 256
    bf16 = jnp.bfloat16
    key_spec = pl.BlockSpec((rows, LANES), lambda p, i: (0, p + first))
    value_spec = pl.BlockSpec((rows, LANES), lambda p, i: (0, p + first + PAIRS))
    return pl.pallas_call(
        attend_kernel,
        grid=(count, rows // block),
        in_specs=[
            pl.BlockSpec(memory_space=pltpu.SMEM),
            pl.BlockSpec((block, LANES), lambda p, i: (i, p + first)),
            key_spec,
            value_spec,
            key_spec,
            value_spec,
        ]
        + [pl.BlockSpec(memory_space=pl.ANY)] * len(done),
        out_specs=[
            pl.BlockSpec((block, LANES), lambda p, i: (i, p + first)),
            pl.BlockSpec((block, 2 * LANES), lambda p, i: (i, p + first)),
        ],
        out_shape=[shape((rows, DIM), bf16), shape((rows, 2 * DIM), bf16)],
        scratch_shapes=[
            pltpu.VMEM((2, 2 * rows, LANES), bf16),
            pltpu.VMEM((2, 2 * rows, LANES), bf16),
        ],
        input_output_aliases={6: 0, 7: 1} if done else {},
        compiler_params=limit(48),
        cost_estimate=cost(
            64 * count * rows * 2 * rows * HD, 32 * rows * LANES * count, 2 * count * rows * 2 * rows
        ),
        name="attend",
    )(place, q, kv_own, kv_own, kv_other, kv_other, *done)


def attend_back_kernel(place_ref, qx_ref, k_ref, v_ref, g_ref, mix_ref, *refs, at, scale):
    bf16 = jnp.bfloat16
    f32 = jnp.float32
    last = at == 0
    if last:
        dq_ref, got_k_ref, got_v_ref, cos_ref, sin_ref, out_ref, gx, g0, q0, acc = refs
    else:
        dq_ref, dk_ref, dv_ref, gx, g0, q0, acc = refs
    rows = g_ref.shape[0]
    count = k_ref.shape[0]
    step = pl.program_id(1)

    @pl.when(step == 0)
    def _():
        dims = (rows, LANES)
        lane = lane_of(dims)
        grad = g_ref[...]
        product = grad.astype(f32) * mix_ref[...].astype(f32)
        zero = jnp.zeros(dims, bf16)
        for head in range(2):
            inside = head_lanes(dims, head)
            spare = lane - extra_lane(head)
            delta = jnp.sum(jnp.where(inside, product, 0.0), axis=1, keepdims=True)
            high = delta.astype(bf16)
            middle = (delta - high.astype(f32)).astype(bf16)
            low = (delta - high.astype(f32) - middle.astype(f32)).astype(bf16)
            wide = jnp.where(spare == 1, -high, jnp.where(spare == 2, -middle, -low))
            wide = jnp.where((spare >= 1) & (spare <= 3), wide, zero)
            gx[head] = jnp.where(inside, grad, wide)
            g0[head] = jnp.where(inside, grad, zero)
            q0[head] = jnp.where(inside, qx_ref[:, head * LANES : (head + 1) * LANES], zero)
        acc[...] = jnp.zeros_like(acc)

    keys = k_ref[...]
    values = v_ref[...]
    dims = keys.shape
    lane = lane_of(dims)
    fill = key_fill(place_ref, at, count, step * count)
    keys_t = keys.astype(f32).T.astype(bf16)
    dk = None
    dv = None
    for head in range(2):
        inside = head_lanes(dims, head)
        spare = lane - extra_lane(head)
        ones = jnp.where((spare >= 1) & (spare <= 3), 1.0, 0.0).astype(bf16)
        keys_x = jnp.where(inside, keys, jnp.where(spare == 0, fill, ones))
        values_x = jnp.where(inside, values, ones)
        scores = nt(keys_x, qx_ref[:, head * LANES : (head + 1) * LANES])
        probs = jnp.exp(scores)
        dv_head = nn(probs.astype(bf16), g0[head])
        grad_probs = nt(values_x, gx[head])
        grad_scores = (probs * grad_probs).astype(bf16)
        dk_head = nn(grad_scores, q0[head])
        part = slice(head * HD, (head + 1) * HD)
        acc[part] += nn(keys_t[part], grad_scores)
        dk = dk_head if dk is None else dk + dk_head
        dv = dv_head if dv is None else dv + dv_head
    if last:
        here = pl.ds(pl.multiple_of(step * count, count), count)
        dk = dk + got_k_ref[...].astype(f32)
        dk = dk * cos_ref[here] - partner_lanes(dk) * sin_ref[here]
        out_ref[1, here] = dk.astype(bf16)
        out_ref[2, here] = (dv + got_v_ref[...].astype(f32)).astype(bf16)
    else:
        dk_ref[...] = dk.astype(bf16)
        dv_ref[...] = dv.astype(bf16)

    @pl.when(step == pl.num_programs(1) - 1)
    def _():
        dq = acc[...].T
        if last:
            dq = (dq + dq_ref[...]) * scale
            dq = dq * cos_ref[...] - partner_lanes(dq) * sin_ref[...]
            out_ref[0] = dq.astype(bf16)
        else:
            dq_ref[...] = dq


def attend_back(place, qx, kv, grad, mix, at, first, count, scale, more=(), skip=0):
    rows = grad.shape[0]
    block = 512
    bf16 = jnp.bfloat16
    wide = pl.BlockSpec((rows, LANES), lambda p, j: (0, p + first))
    here = pl.BlockSpec((rows, LANES), lambda p, j: (0, p))
    keys = pl.BlockSpec((block, LANES), lambda p, j: (j, p))
    table = pl.BlockSpec((rows, LANES), lambda p, j: (0, 0))
    dims = (rows, count * LANES)
    if at == 0:
        ahead = pl.BlockSpec((rows, LANES), lambda p, j: (0, p + skip))
        ahead_keys = pl.BlockSpec((block, LANES), lambda p, j: (j, p + skip))
        more_specs = [ahead, ahead_keys, ahead_keys, table, table]
        out_specs = pl.BlockSpec((3, rows, LANES), lambda p, j: (0, 0, p))
        out_shape = shape((3, *dims), bf16)
    else:
        more_specs = []
        out_specs = [here, keys, keys]
        out_shape = [shape(dims, jnp.float32), shape(dims, bf16), shape(dims, bf16)]
    return pl.pallas_call(
        functools.partial(attend_back_kernel, at=at, scale=scale),
        grid=(count, rows // block),
        in_specs=[
            pl.BlockSpec(memory_space=pltpu.SMEM),
            pl.BlockSpec((rows, 2 * LANES), lambda p, j: (0, p + first)),
            pl.BlockSpec((block, LANES), lambda p, j: (j, p + first)),
            pl.BlockSpec((block, LANES), lambda p, j: (j, p + first + PAIRS)),
            wide,
            wide,
        ]
        + more_specs,
        out_specs=out_specs,
        out_shape=out_shape,
        scratch_shapes=[
            pltpu.VMEM((2, rows, LANES), bf16),
            pltpu.VMEM((2, rows, LANES), bf16),
            pltpu.VMEM((2, rows, LANES), bf16),
            pltpu.VMEM((LANES, rows), jnp.float32),
        ],
        compiler_params=limit(48),
        cost_estimate=cost(
            80 * count * rows * rows * HD, 40 * count * rows * LANES, 2 * count * rows * rows
        ),
        name="attend_back",
    )(place, qx, kv, kv, grad, mix, *more)


def row_mean(values):
    return jnp.sum(values, axis=1, keepdims=True) * (1.0 / DIM)


def out_norm_kernel(mix_ref, w_ref, x_ref, hat_ref, rstd_ref):
    weight = w_ref[...].reshape(DIM, DIM)
    values = x_ref[...].astype(jnp.float32) + nt(mix_ref[...], weight)
    centred = values - row_mean(values)
    rstd = lax.rsqrt(row_mean(centred * centred) + EPS)
    hat_ref[...] = centred * rstd
    rstd_ref[...] = jnp.broadcast_to(rstd, rstd_ref.shape)


def out_norm(mix, stacked, rows_in):
    rows = mix.shape[0]
    block = 256
    spec = pl.BlockSpec((block, DIM), lambda i: (i, 0))
    return pl.pallas_call(
        out_norm_kernel,
        grid=(rows // block,),
        in_specs=[spec, pl.BlockSpec((REPS, 96, DIM), lambda i: (0, 8, 0)), spec],
        out_specs=[spec, pl.BlockSpec((block, LANES), lambda i: (i, 0))],
        out_shape=[shape((rows, DIM), jnp.float32), shape((rows, LANES), jnp.float32)],
        compiler_params=limit(48),
        cost_estimate=cost(2 * rows * DIM * DIM, 8 * rows * DIM),
        name="out_norm",
    )(mix, stacked, rows_in)


FF_TILE = 256
SUB = DIM // FF_TILE
FF_PIECES = FF // DIM


def row_parts(ref):
    half = ref.shape[0] // 2
    return [pl.ds(0, half), pl.ds(half, half)]


def sub_lanes():
    return pl.ds(pl.multiple_of(pl.program_id(1) * FF_TILE, FF_TILE), FF_TILE)


def at_step(piece, sub):
    return (pl.program_id(0) == piece) & (pl.program_id(1) == sub)


def feed_forward_kernel(
    hat_ref,
    gains_ref,
    biases_ref,
    wg_ref,
    wu_ref,
    wd_ref,
    hidden_ref,
    factor_ref,
    half_ref,
    acc,
    gate_s,
    up_s,
):
    bf16 = jnp.bfloat16
    f32 = jnp.float32
    step = pl.program_id(0)

    @pl.when(step == 0)
    def _():
        normed = hat_ref[...] * gains_ref[0:1] + biases_ref[0:1]
        acc[...] = normed
        half_ref[...] = normed.astype(bf16)
        gate_s[...] = jnp.zeros_like(gate_s)
        up_s[...] = jnp.zeros_like(up_s)

    gate = gate_s[...]
    up = up_s[...]
    sig = 1.0 / (1.0 + jnp.exp(-gate))
    act = gate * sig
    hidden = (act * up).astype(bf16)
    hidden_ref[...] = hidden
    factor_ref[0] = (up * sig * (1.0 + gate - act)).astype(bf16)
    factor_ref[1] = act.astype(bf16)
    rows_in = half_ref[...]
    gate_s[...] = nn(rows_in, wg_ref[0])
    up_s[...] = nn(rows_in, wu_ref[0])
    acc[...] += nt(hidden, wd_ref[...].reshape(DIM, FF_TILE))


def feed_forward(hat, gains, biases, stacked):
    rows = hat.shape[0]
    bf16 = jnp.bfloat16
    f32 = jnp.float32
    fixed = lambda t: (0, 0)
    whole = pl.BlockSpec((rows, DIM), fixed)
    small = pl.BlockSpec((2, DIM), fixed)
    tiles = FF_PIECES * SUB

    def now(t):
        return jnp.minimum(t, tiles - 1)

    def before(t):
        return jnp.maximum(t - 1, 0)

    return pl.pallas_call(
        feed_forward_kernel,
        grid=(tiles + 1,),
        in_specs=[
            whole,
            small,
            small,
            pl.BlockSpec((1, DIM, FF_TILE), lambda t: (now(t) // SUB, 0, now(t) % SUB)),
            pl.BlockSpec((1, DIM, FF_TILE), lambda t: (now(t) // SUB + FF_PIECES, 0, now(t) % SUB)),
            pl.BlockSpec(
                (REPS, 96, FF_TILE), lambda t: (0, before(t) // SUB + 9, before(t) % SUB)
            ),
        ],
        out_specs=[
            pl.BlockSpec((rows, FF_TILE), lambda t: (0, before(t))),
            pl.BlockSpec((2, rows, FF_TILE), lambda t: (0, 0, before(t))),
            whole,
            whole,
        ],
        out_shape=[
            shape((rows, FF), bf16),
            shape((2, rows, FF), bf16),
            shape((rows, DIM), bf16),
            shape((rows, DIM), f32),
        ],
        scratch_shapes=[
            pltpu.VMEM((rows, FF_TILE), f32),
            pltpu.VMEM((rows, FF_TILE), f32),
        ],
        compiler_params=limit(60),
        cost_estimate=cost(6 * rows * DIM * FF, 6 * rows * FF + 6 * DIM * FF, rows * FF),
        name="feed_forward",
    )(hat, gains, biases, stacked, stacked, stacked)


def norm_back_kernel(
    place_ref, values_ref, gains_ref, biases_ref, cot_a_ref, cot_b_ref,
    mixed_ref, grad_ref, branch_ref, vec_ref,
):
    bf16 = jnp.bfloat16
    f32 = jnp.float32
    step = pl.program_id(0)
    second = step >= pl.num_programs(0) // 2
    values = values_ref[...]
    rows = values.shape[0]
    centred = values - row_mean(values)
    rstd = lax.rsqrt(row_mean(centred * centred) + EPS)
    hat = centred * rstd
    mixed_ref[...] = (hat * gains_ref[1:2] + biases_ref[1:2]).astype(bf16)
    row = lax.broadcasted_iota(jnp.int32, (rows, 1), 0) + step * rows
    half = place_ref[6]
    position = jnp.where(row < half, place_ref[0] + row, place_ref[1] + row - half)
    cot = jnp.where(second, cot_b_ref[...].astype(f32), cot_a_ref[...].astype(f32))
    grad = jnp.where(position < place_ref[4], cot, 0.0)

    @pl.when(step == 0)
    def _():
        vec_ref[...] = jnp.zeros_like(vec_ref)

    vec_ref[0:1] += jnp.sum(grad * hat, axis=0, keepdims=True)
    vec_ref[1:2] += jnp.sum(grad, axis=0, keepdims=True)
    grad = grad * gains_ref[1:2]
    grad = rstd * (grad - row_mean(grad) - hat * row_mean(grad * hat))
    grad_ref[...] = grad
    branch_ref[...] = grad.astype(bf16)


def norm_back(place, values, gains, biases, cot):
    rows = values.shape[0]
    block = 256
    half = rows // block // 2
    f32 = jnp.float32
    bf16 = jnp.bfloat16
    spec = pl.BlockSpec((block, DIM), lambda i: (i, 0))
    small = pl.BlockSpec((2, DIM), lambda i: (0, 0))
    return pl.pallas_call(
        norm_back_kernel,
        grid=(rows // block,),
        in_specs=[
            pl.BlockSpec(memory_space=pltpu.SMEM),
            spec,
            small,
            small,
            pl.BlockSpec((block, DIM), lambda i: (jnp.minimum(i, half - 1), 0)),
            pl.BlockSpec((block, DIM), lambda i: (jnp.maximum(i - half, 0), 0)),
        ],
        out_specs=[spec, spec, spec, small],
        out_shape=[
            shape((rows, DIM), bf16),
            shape((rows, DIM), f32),
            shape((rows, DIM), bf16),
            shape((2, DIM), f32),
        ],
        compiler_params=limit(48),
        cost_estimate=cost(30 * rows * DIM, 14 * rows * DIM),
        name="norm_back",
    )(place, values, gains, biases, *cot)


def feed_back_kernel(
    index_ref,
    grad_ref,
    branch_ref,
    factor_ref,
    wg_ref,
    wu_ref,
    wd_ref,
    left_away_ref,
    left_keep_ref,
    *refs,
):
    bf16 = jnp.bfloat16
    f32 = jnp.float32
    last = len(refs) > 6
    if last:
        hat_ref, rstd_ref, gains_ref, wo_ref, away_ref, keep_ref = refs[:6]
        attn_ref, attn_half_ref, mix_grad_ref, vec_ref, acc, both, left = refs[6:]
    else:
        away_ref, keep_ref, acc_ref, acc, both, left = refs
    half_rows = left_away_ref.shape[0]
    here = sub_lanes()

    @pl.when(at_step(0, 0))
    def _():
        acc[...] = grad_ref[...]
        left[:half_rows] = left_away_ref[...]
        left[half_rows:] = left_keep_ref[...]

    grad_hidden = nn(branch_ref[...], wd_ref[...].reshape(DIM, FF_TILE))
    for side in range(2):
        grad = (grad_hidden * factor_ref[side].astype(f32)).astype(bf16)
        both[side, :, here] = grad
        product = nn(left[...], grad).astype(bf16)
        away_ref[side] = product[:half_rows]
        keep_ref[side] = product[half_rows:]

    @pl.when(pl.program_id(1) == SUB - 1)
    def _():
        acc[...] += nt(both[0], wg_ref[0]) + nt(both[1], wu_ref[0])

    @pl.when(at_step(pl.num_programs(0) - 1, SUB - 1))
    def _():
        grad = acc[...]
        if not last:
            acc_ref[...] = grad
            return
        hat = hat_ref[...]
        vec_ref[0:1] = jnp.sum(grad * hat, axis=0, keepdims=True)
        vec_ref[1:2] = jnp.sum(grad, axis=0, keepdims=True)
        grad = grad * gains_ref[0:1]
        rstd = rstd_ref[:, 0:1]
        grad = rstd * (grad - row_mean(grad) - hat * row_mean(grad * hat))
        attn_ref[...] = grad
        half = grad.astype(bf16)
        attn_half_ref[...] = half
        mix_grad_ref[...] = nn(half, wo_ref[...].reshape(DIM, DIM)).astype(bf16)


def feed_back(index, grad, branch, factor, stacked, normed_t, first, more=()):
    rows = grad.shape[0]
    bf16 = jnp.bfloat16
    f32 = jnp.float32
    fixed = lambda j, i, s: (0, 0)
    whole = pl.BlockSpec((rows, DIM), fixed)
    small = pl.BlockSpec((2, DIM), fixed)
    pieces = FF_PIECES // 2
    count = pieces * DIM
    parts = pl.BlockSpec((2, DIM // 2, FF_TILE), lambda j, i, s: (0, 0, SUB * j + i))
    in_specs = [
        whole,
        whole,
        pl.BlockSpec((2, rows, FF_TILE), lambda j, i, s: (0, 0, SUB * (j + first) + i)),
        pl.BlockSpec((1, DIM, DIM), lambda j, i, s: (j + first, 0, 0)),
        pl.BlockSpec((1, DIM, DIM), lambda j, i, s: (j + first + FF_PIECES, 0, 0)),
        pl.BlockSpec((REPS, 96, FF_TILE), lambda j, i, s: (0, j + first + 9, i)),
        pl.BlockSpec((DIM // 2, rows), lambda j, i, s: (s[0], 0)),
        pl.BlockSpec((DIM // 2, rows), lambda j, i, s: (1 - s[0], 0)),
    ]
    out_specs = [parts, parts]
    out_shape = [shape((2, DIM // 2, count), bf16)] * 2
    if more:
        in_specs += [
            whole,
            pl.BlockSpec((rows, LANES), fixed),
            small,
            pl.BlockSpec((REPS, 96, DIM), lambda j, i, s: (0, 8, 0)),
        ]
        out_specs += [whole, whole, whole, small]
        out_shape += [
            shape((rows, DIM), f32),
            shape((rows, DIM), bf16),
            shape((rows, DIM), bf16),
            shape((2, DIM), f32),
        ]
    else:
        out_specs += [whole]
        out_shape += [shape((rows, DIM), f32)]
    return pl.pallas_call(
        feed_back_kernel,
        grid_spec=pltpu.PrefetchScalarGridSpec(
            num_scalar_prefetch=1,
            grid=(pieces, SUB),
            in_specs=in_specs,
            out_specs=out_specs,
            scratch_shapes=[
                pltpu.VMEM((rows, DIM), f32),
                pltpu.VMEM((2, rows, DIM), bf16),
                pltpu.VMEM((DIM, rows), bf16),
            ],
        ),
        out_shape=out_shape,
        compiler_params=limit(60),
        cost_estimate=cost(10 * rows * DIM * count, 4 * rows * count + 10 * DIM * count),
        name="feed_back",
    )(index, grad, branch, factor, stacked, stacked, stacked, normed_t, normed_t, *more)


def away_kernel(index_ref, left_ref, right_ref, out_ref):
    right = right_ref[0] if len(right_ref.shape) == 3 else right_ref[...]
    out_ref[...] = nn(left_ref[...], right).astype(out_ref.dtype)


def keep_kernel(index_ref, la_ref, lb_ref, right_ref, ra_ref, rb_ref, out_a_ref, out_b_ref):
    right = right_ref[0] if len(right_ref.shape) == 3 else right_ref[...]
    for left, got, out in ((la_ref, ra_ref, out_a_ref), (lb_ref, rb_ref, out_b_ref)):
        out[...] = (nn(left[...], right) + got[...].astype(jnp.float32)).astype(out.dtype)


def right_spec(right, tile):
    if right.ndim == 3:
        per = right.shape[2] // tile
        return pl.BlockSpec((1, right.shape[1], tile), lambda t, s: (t // per, 0, t % per))
    return pl.BlockSpec((right.shape[0], tile), lambda t, s: (0, t))


def away_rows(index, left_t, right, tile):
    rows = left_t.shape[1]
    half = left_t.shape[0] // 2
    count = right.size // rows
    return pl.pallas_call(
        away_kernel,
        grid_spec=pltpu.PrefetchScalarGridSpec(
            num_scalar_prefetch=1,
            grid=(count // tile,),
            in_specs=[
                pl.BlockSpec((half, rows), lambda t, s: (s[0], 0)),
                right_spec(right, tile),
            ],
            out_specs=pl.BlockSpec((half, tile), lambda t, s: (0, t)),
        ),
        out_shape=shape((half, count), jnp.bfloat16),
        compiler_params=limit(48),
        cost_estimate=cost(2 * half * rows * count, 2 * rows * count + 2 * half * count),
        name="away_rows",
    )(index, left_t, right)


def keep_rows(index, left_t, right, got, tile):
    rows = left_t.shape[1]
    block = left_t.shape[0] // 4
    count = right.size // rows
    out = pl.BlockSpec((block, tile), lambda t, s: (0, t))
    return pl.pallas_call(
        keep_kernel,
        grid_spec=pltpu.PrefetchScalarGridSpec(
            num_scalar_prefetch=1,
            grid=(count // tile,),
            in_specs=[
                pl.BlockSpec((block, rows), lambda t, s: (s[1], 0)),
                pl.BlockSpec((block, rows), lambda t, s: (s[2], 0)),
                right_spec(right, tile),
                pl.BlockSpec((block, tile), lambda t, s: (s[3], t)),
                pl.BlockSpec((block, tile), lambda t, s: (1 - s[3], t)),
            ],
            out_specs=[out, out],
        ),
        out_shape=[shape((block, count), jnp.bfloat16)] * 2,
        compiler_params=limit(48),
        cost_estimate=cost(4 * block * rows * count, 2 * rows * count + 8 * block * count),
        name="keep_rows",
    )(index, left_t, left_t, right, got, got)


def keep_columns_kernel(index_ref, left_ref, right_a_ref, right_b_ref, ra_ref, rb_ref, oa_ref, ob_ref):
    left = left_ref[...]
    for right, got, out in ((right_a_ref, ra_ref, oa_ref), (right_b_ref, rb_ref, ob_ref)):
        out[...] = (nn(left, right[...]) + got[...].astype(jnp.float32)).astype(out.dtype)


def away_columns(index, left_t, right, tile):
    height, rows = left_t.shape
    half = right.shape[1] // 2
    per = half // tile
    return pl.pallas_call(
        away_kernel,
        grid_spec=pltpu.PrefetchScalarGridSpec(
            num_scalar_prefetch=1,
            grid=(per,),
            in_specs=[
                pl.BlockSpec((height, rows), lambda t, s: (0, 0)),
                pl.BlockSpec((rows, tile), lambda t, s: (0, s[0] * per + t)),
            ],
            out_specs=pl.BlockSpec((height, tile), lambda t, s: (0, t)),
        ),
        out_shape=shape((height, half), jnp.bfloat16),
        compiler_params=limit(48),
        cost_estimate=cost(2 * height * rows * half, 2 * rows * half + 2 * height * half),
        name="away_columns",
    )(index, left_t, right)


def keep_columns(index, left_t, right, got, tile):
    height, rows = left_t.shape
    block = right.shape[1] // 4
    per = block // tile
    out = pl.BlockSpec((height, tile), lambda t, s: (0, t))
    return pl.pallas_call(
        keep_columns_kernel,
        grid_spec=pltpu.PrefetchScalarGridSpec(
            num_scalar_prefetch=1,
            grid=(per,),
            in_specs=[
                pl.BlockSpec((height, rows), lambda t, s: (0, 0)),
                pl.BlockSpec((rows, tile), lambda t, s: (0, s[1] * per + t)),
                pl.BlockSpec((rows, tile), lambda t, s: (0, s[2] * per + t)),
                pl.BlockSpec((height, tile), lambda t, s: (0, s[3] * per + t)),
                pl.BlockSpec((height, tile), lambda t, s: (0, (1 - s[3]) * per + t)),
            ],
            out_specs=[out, out],
        ),
        out_shape=[shape((height, block), jnp.bfloat16)] * 2,
        compiler_params=limit(48),
        cost_estimate=cost(4 * height * rows * block, 4 * rows * block + 8 * height * block),
        name="keep_columns",
    )(index, left_t, right, right, got, got)


def input_kernel(*refs):
    grads, weights, (attn_ref, out_ref, acc) = refs[:3], refs[3:6], refs[6:]
    step = pl.program_id(0)

    @pl.when(step == 0)
    def _():
        acc[...] = attn_ref[...]

    grad = jnp.concatenate([ref[0] for ref in grads], axis=1)
    weight = jnp.concatenate([ref[0] for ref in weights], axis=0)
    acc[...] += nn(grad, weight)

    @pl.when(step == pl.num_programs(0) - 1)
    def _():
        out_ref[...] = acc[...].astype(out_ref.dtype)


def input_rows_of(parts, qkv_t, grad_attn):
    rows = grad_attn.shape[0]
    wide = parts[0].shape[2]
    fixed = lambda i: (0, 0)
    weights = qkv_t.reshape(3, DIM, DIM)
    return pl.pallas_call(
        input_kernel,
        grid=(3,),
        in_specs=[pl.BlockSpec((1, rows, wide), lambda i: (i, 0, 0))] * 3
        + [
            pl.BlockSpec((1, wide, DIM), functools.partial(lambda at, i: (i, at, 0), at))
            for at in range(3)
        ]
        + [pl.BlockSpec((rows, DIM), fixed)],
        out_specs=pl.BlockSpec((rows, DIM), fixed),
        out_shape=shape((rows, DIM), jnp.bfloat16),
        scratch_shapes=[pltpu.VMEM((rows, DIM), jnp.float32)],
        compiler_params=limit(48),
        cost_estimate=cost(6 * rows * DIM * DIM, 14 * rows * DIM),
        name="input_rows",
    )(*parts, weights, weights, weights, grad_attn)


CHUNK = DIM


def halves(values):
    high = values.astype(jnp.bfloat16)
    return high, (values - high.astype(jnp.float32)).astype(jnp.bfloat16)


def exact_product(product, small, large):
    small_high, small_low = halves(small)
    large_high, large_low = halves(large)
    both = product(jnp.concatenate([small_high, small_low], axis=0), large_high)
    return both[:RANK] + both[RANK:] + product(small_high, large_low)


def merge_main_kernel(
    owner_ref, fs_ref, ff_ref, ss_ref, sf_ref, eg_ref, eo_ref, tg_ref, to_ref, mg_ref, mo_ref, p_ref
):
    f32 = jnp.float32
    step = pl.program_id(0)
    rows = mg_ref.shape[0]
    owner = owner_ref[0] == 1
    second = jnp.where(owner, ss_ref[...].astype(f32), sf_ref[...].astype(f32))

    @pl.when(step == 0)
    def _():
        p_ref[...] = jnp.zeros_like(p_ref)

    @pl.when(step < 8)
    def _():
        first = jnp.where(owner, fs_ref[0].astype(f32), ff_ref[0].astype(f32))
        merged = jnp.where(step // 2 % 2 == 0, first, second) + eg_ref[0]
        mg_ref[...] = merged
        p_ref[:, :rows] += exact_product(nt, tg_ref[...], merged)

    @pl.when(step == 8)
    def _():
        merged = second + eo_ref[0]
        mo_ref[...] = merged
        p_ref[:, 256 : 256 + rows] = exact_product(nt, to_ref[...], merged)


def merge_main(owner, first, second, err_gate_up, err_out, start_gate_up, start_out):
    rows = err_out.shape[1]
    f32 = jnp.float32
    last = 2 * FF // CHUNK - 1
    fixed = lambda i: (0, 0)
    first_spec = pl.BlockSpec((1, rows, CHUNK), lambda i: (jnp.minimum(i // 4, 1), 0, i % 2))
    second_spec = pl.BlockSpec(
        (rows, CHUNK), lambda i: (0, jnp.where(i > last, 4, 2 * (i // 4) + i % 2))
    )
    return pl.pallas_call(
        merge_main_kernel,
        grid=(last + 2,),
        in_specs=[
            pl.BlockSpec(memory_space=pltpu.SMEM),
            first_spec,
            first_spec,
            second_spec,
            second_spec,
            pl.BlockSpec((1, rows, CHUNK), lambda i: (0, 0, jnp.minimum(i, last))),
            pl.BlockSpec((1, rows, CHUNK), lambda i: (0, 0, 0)),
            pl.BlockSpec((RANK, CHUNK), lambda i: (0, jnp.minimum(i, last))),
            pl.BlockSpec((RANK, CHUNK), fixed),
        ],
        out_specs=[
            pl.BlockSpec((rows, CHUNK), lambda i: (0, jnp.minimum(i, last))),
            pl.BlockSpec((rows, CHUNK), fixed),
            pl.BlockSpec((RANK, 512), fixed),
        ],
        out_shape=[
            shape((rows, 2 * FF), f32),
            shape((rows, CHUNK), f32),
            shape((RANK, 512), f32),
        ],
        compiler_params=limit(48),
        cost_estimate=cost(60 * rows * 7 * DIM, 14 * rows * 7 * DIM),
        name="merge_main",
    )(owner, *first, *second, err_gate_up, err_out, start_gate_up, start_out)


def merge_down_kernel(owner_ref, s_ref, f_ref, e_ref, t_ref, m_ref, p_ref):
    f32 = jnp.float32
    own = jnp.where(owner_ref[0] == 1, s_ref[...].astype(f32), f_ref[...].astype(f32))
    merged = own.T + e_ref[0]
    m_ref[...] = merged
    p_ref[...] = exact_product(nt, t_ref[...], merged)


def merge_down(owner, own, err, start):
    block = 256
    f32 = jnp.float32
    column = pl.BlockSpec((DIM, block), lambda i: (0, i))
    return pl.pallas_call(
        merge_down_kernel,
        grid=(DIM // block,),
        in_specs=[
            pl.BlockSpec(memory_space=pltpu.SMEM),
            column,
            column,
            pl.BlockSpec((1, block, DIM), lambda i: (0, i, 0)),
            pl.BlockSpec((RANK, DIM), lambda i: (0, 0)),
        ],
        out_specs=[
            pl.BlockSpec((block, DIM), lambda i: (i, 0)),
            pl.BlockSpec((RANK, block), lambda i: (0, i)),
        ],
        out_shape=[shape((DIM, DIM), f32), shape((RANK, DIM), f32)],
        compiler_params=limit(48),
        cost_estimate=cost(60 * DIM * DIM, 12 * DIM * DIM),
        name="merge_down",
    )(owner, *own, err, start)


def merge_qkv_kernel(owner_ref, *refs):
    f32 = jnp.float32
    near, far, (e_ref, t_ref, m_ref, p_ref) = refs[:3], refs[3:6], refs[6:]
    rows = m_ref.shape[0]
    near = jnp.concatenate([ref[...] for ref in near], axis=1).astype(f32)
    far = jnp.concatenate([ref[...] for ref in far], axis=1).astype(f32)
    merged = jnp.where(owner_ref[0] == 1, near, far) + e_ref[0]
    m_ref[...] = merged

    @pl.when(pl.program_id(0) == 0)
    def _():
        p_ref[...] = jnp.zeros_like(p_ref)

    p_ref[:, :rows] += exact_product(nt, t_ref[...], merged)


def merge_qkv(owner, near, far, err, start):
    rows = err.shape[1]
    f32 = jnp.float32
    parts = [
        pl.BlockSpec((rows, 256), functools.partial(lambda at, i: (0, at + i), at))
        for at in (0, 0, 3)
    ]
    return pl.pallas_call(
        merge_qkv_kernel,
        grid=(3,),
        in_specs=[pl.BlockSpec(memory_space=pltpu.SMEM)]
        + parts
        + parts
        + [
            pl.BlockSpec((1, rows, CHUNK), lambda i: (0, 0, i)),
            pl.BlockSpec((RANK, CHUNK), lambda i: (0, i)),
        ],
        out_specs=[
            pl.BlockSpec((rows, CHUNK), lambda i: (0, i)),
            pl.BlockSpec((RANK, 256), lambda i: (0, 0)),
        ],
        out_shape=[shape((rows, 3 * DIM), f32), shape((RANK, 256), f32)],
        compiler_params=limit(48),
        cost_estimate=cost(60 * rows * 3 * DIM, 14 * rows * 3 * DIM),
        name="merge_qkv",
    )(owner, *near, *far, err, start)


def chunk_spec(array, first, lead=()):
    rows, count = array.shape[0], array.shape[1] // CHUNK
    zeros = tuple(0 for _ in lead)
    return pl.BlockSpec(
        (*lead, rows, CHUNK), lambda i: (*zeros, 0, jnp.clip(i - first, 0, count - 1))
    )


def chunk_starts(arrays):
    starts = [0]
    for array in arrays:
        starts.append(starts[-1] + array.shape[1] // CHUNK)
    return starts


def orthonormal_rows(values):
    row = lax.broadcasted_iota(jnp.int32, (RANK, 1), 0)
    for column in range(RANK):
        vector = values[column : column + 1]
        vector = vector * lax.rsqrt(jnp.sum(vector * vector, axis=1, keepdims=True) + 1e-06)
        weights = jnp.sum(values * vector, axis=1, keepdims=True)
        later = values - weights * vector
        values = jnp.where(row > column, later, jnp.where(row == column, vector, values))
    return values


def pull_kernel(left_ref, *refs, segments, starts):
    count = len(segments)
    merged = refs[:count]
    basis_ref, out_ref = refs[count:]
    step = pl.program_id(0)

    @pl.when(step == 0)
    def _():
        for start, width in segments:
            part = slice(start, start + (width + 255) // 256 * 256)
            basis_ref[:, part] = orthonormal_rows(left_ref[:, part] * (1.0 / REPS))

    for at, (start, width) in enumerate(segments):

        @pl.when((step >= starts[at]) & (step < starts[at + 1]))
        def _():
            basis = basis_ref[:, start : start + width]
            out_ref[...] = exact_product(nn, basis, merged[at][...]).astype(out_ref.dtype)


def pull(left, merged, segments):
    starts = chunk_starts(merged)
    total = sum(array.size for array in merged)
    fixed = pl.BlockSpec(left.shape, lambda i: (0, 0))
    return pl.pallas_call(
        functools.partial(pull_kernel, segments=segments, starts=starts),
        grid=(starts[-1],),
        in_specs=[fixed] + [chunk_spec(array, at) for array, at in zip(merged, starts)],
        out_specs=[fixed, pl.BlockSpec((RANK, CHUNK), lambda i: (0, i))],
        out_shape=[
            shape(left.shape, jnp.float32),
            shape((RANK, starts[-1] * CHUNK), jnp.bfloat16),
        ],
        compiler_params=limit(48),
        cost_estimate=cost(48 * total, 4 * total),
        name="pull",
    )(left, *merged)


def new_errors_kernel(basis_ref, factor_ref, *refs, segments, starts):
    count = len(segments)
    step = pl.program_id(0)
    for at, (start, width) in enumerate(segments):
        merged, out = refs[at], refs[count + at]

        @pl.when((step >= starts[at]) & (step < starts[at + 1]))
        def _():
            basis_high, basis_low = halves(basis_ref[:, start : start + width])
            factor_high, factor_low = halves(factor_ref[...])
            left = jnp.concatenate([basis_high, basis_low, basis_high], axis=0)
            right = jnp.concatenate([factor_high, factor_high, factor_low], axis=0)
            approx = lax.dot_general(
                left, right, (((0,), (0,)), ((), ())), preferred_element_type=jnp.float32
            )
            out[0] = merged[...] - approx


def new_errors_of(bases, factors, merged, segments):
    starts = chunk_starts(merged)
    total = sum(array.size for array in merged)
    return pl.pallas_call(
        functools.partial(new_errors_kernel, segments=segments, starts=starts),
        grid=(starts[-1],),
        in_specs=[
            pl.BlockSpec(bases.shape, lambda i: (0, 0)),
            pl.BlockSpec((RANK, CHUNK), lambda i: (0, i)),
        ]
        + [chunk_spec(array, at) for array, at in zip(merged, starts)],
        out_specs=[chunk_spec(array, at, (1,)) for array, at in zip(merged, starts)],
        out_shape=[shape((1, *array.shape), jnp.float32) for array in merged],
        compiler_params=limit(48),
        cost_estimate=cost(48 * total, 8 * total),
        name="new_errors",
    )(bases, factors, *merged)


def compress(left, merged, segments, masters, moments, rates, rep):
    highest = lax.Precision.HIGHEST
    bases, pulled = pull(left, merged, segments)
    summed = plane_sum_half(pulled) / REPS
    errors = new_errors_of(bases, summed, merged, segments)
    results = []
    at = 0
    for (start, width), block, error, master, moment, rate in zip(
        segments, merged, errors, masters, moments, rates
    ):
        basis = bases[:, start : start + width]
        size = block.shape[1]
        factor = summed[:, at : at + size]
        col_count = master.shape[1]
        piece = lax.dynamic_slice_in_dim(summed, at + rep * col_count, col_count, 1)
        piece = lax.dot_general(basis, piece, (((0,), (0,)), ((), ())), precision=highest)
        moment_new = MOMENTUM * moment + piece
        results.append(
            (master - rate * moment_new, moment_new, error, basis.T, factor.T[None])
        )
        at += size
    return results


def fast_device(
    tokens,
    cotangent,
    lengths,
    w_qkv,
    w_out,
    w_gate_up,
    w_down,
    mom_qkv,
    mom_out,
    mom_gate_up,
    mom_down,
    err_qkv,
    err_out,
    err_gate_up,
    err_down,
    start_qkv,
    start_out,
    start_gate_up,
    start_down,
    layer_norm_gains,
    layer_norm_biases,
    norm_moments,
):
    f32 = jnp.float32
    bf16 = jnp.bfloat16
    rep = lax.axis_index("rep")
    shard = lax.axis_index("shard")
    core = rep % 2
    local_len, width = tokens.shape[1:]
    scale = HD ** (-0.5)

    def spread(values, *before):
        parts = []
        for parity in (0, 1):
            sent = lax.dynamic_index_in_dim(values, (shard + parity) % 2, 0, keepdims=False)
            parts.append(send(sent, spread_move(parity)))
        return after(parts, *before)

    def bring_back(rows):
        first = send(rows[:local_len], gather_move(0))
        second = send(rows[local_len:], gather_move(1))
        even = shard % 2 == 0
        return jnp.stack([jnp.where(even, first, second), jnp.where(even, second, first)])

    side = jnp.concatenate(
        [
            w_gate_up.astype(bf16),
            w_down.astype(bf16).T,
            w_out.astype(bf16).T.reshape(24, width),
        ],
        axis=0,
    )
    gathered = lax.all_gather(side, "shard", axis=0)
    qkv_piece = jnp.concatenate(shard_gather(w_qkv.astype(bf16).T, shard), axis=1)
    qkv_near = plane_near(qkv_piece)
    rows_in = jnp.concatenate(spread(tokens), axis=0)
    qkv_far = plane_far(qkv_piece, qkv_near)
    both = jnp.stack([lengths, sibling(lengths)])
    group = shard // 2
    length = both[jnp.where(group == core, 0, 1), shard % 2]
    qkv_others = exchange(qkv_piece, qkv_near, qkv_far)
    inside = jnp.arange(local_len, dtype=jnp.int32)

    def starts_of(k):
        first = 2 * k + shard % 2
        second = 2 * k + 1 - shard % 2
        return [first * local_len, second * local_len]

    place = jnp.stack(
        starts_of(core) + starts_of(1 - core) + [length, jnp.zeros_like(length), local_len + 0 * length]
    ).astype(jnp.int32)
    qkv_t = plane_all(
        qkv_piece, qkv_near, qkv_far, qkv_others, rep, (gathered.reshape(-1, width), place)
    )
    qkv_t = qkv_t.reshape(3 * width, width)
    position = jnp.concatenate([place[0] + inside, place[1] + inside])
    inverse = jnp.exp(
        jnp.arange(HD // 2, dtype=jnp.int32).astype(f32) * (-2.0 * math.log(ROPE_BASE) / HD)
    )
    angle = position.astype(f32)[:, None] * inverse[None, :]
    cosine, sine = jnp.cos(angle), jnp.sin(angle)
    cos = jnp.concatenate([cosine] * 4, axis=1)
    sin = jnp.concatenate([-sine, sine] * 2, axis=1)

    kv = project(rows_in, qkv_t, cos, sin, 1, 2, 1, 1.0)
    kv_other = sibling(kv)
    q = project(rows_in, qkv_t, cos, sin, 0, 1, None, scale)
    out_piece = gathered[:, 288:].reshape(SHARDS, 96, 192).transpose(1, 0, 2)
    piece = jnp.concatenate(
        [
            gathered[:, :192].reshape(width, width),
            out_piece.reshape(96, width),
            gathered[:, 192:288].reshape(384, width),
        ],
        axis=0,
    )
    near = plane_near(piece)
    first = attend(place, q, kv, kv_other, 0, 2)
    second = attend(place, q, kv, kv_other, 2, 2, first)
    near = after(near, second[1])
    far = plane_far(piece, near)
    mix, qx = attend(place, q, kv, kv_other, 4, 2, second)
    others = [sibling(part) for part in (after(piece, second[1]), *near)]
    far = after(far, qx)
    others.append(sibling(jnp.concatenate(far, axis=0)))
    stacked = plane_all(piece, near, far, others, rep)
    cot_in = spread(after(cotangent, stacked))
    hat, rstd = out_norm(mix, stacked, rows_in)
    hidden, factor, normed_half, values = feed_forward(
        hat, layer_norm_gains, layer_norm_biases, stacked
    )
    mixed, grad_second, branch, vec_two = norm_back(
        place, values, layer_norm_gains, layer_norm_biases, cot_in
    )
    mixed_out = bring_back(mixed)

    other = 1 - core
    shard_own = jnp.where((shard == 0) | (shard == 3), 0, 1)
    kept = jnp.where(core == 0, shard_own, 3 - shard_own)
    index = jnp.stack([other, kept, 4 * core + 1 - kept, kept - 2 * core]).astype(jnp.int32)
    owner = core == shard // 2

    def kept_rows(values, at):
        parts = values.reshape(2, 2, -1, values.shape[2])
        return lax.dynamic_index_in_dim(parts, at, 1, keepdims=False).astype(f32)

    near = index[3]

    def core_sum(keep, got):
        mine = (kept_rows(keep, near) + kept_rows(got, near)).astype(bf16)
        theirs = (kept_rows(keep, 1 - near) + kept_rows(got, 1 - near)).astype(bf16)
        return mine, theirs

    def add(mine, pair):
        return (mine.astype(f32) + pair.astype(f32)).astype(bf16)

    branch_t = branch.T
    down_away = away_columns(index, branch_t, hidden, DIM)
    down_got = sibling(down_away)
    normed_t = normed_half.T
    away_1, keep_1, partial = feed_back(
        index, grad_second, branch, factor, stacked, normed_t, 0
    )
    got_1 = sibling(away_1)
    down_mine, down_theirs = keep_columns(index, branch_t, hidden, down_got, DIM)
    down_pair = pair_z(down_theirs)
    first_mine, first_theirs = core_sum(keep_1, got_1)
    first_pair = pair_z(first_theirs)
    away_2, keep_2, grad_attn, grad_attn_half, grad_mix, vec_one = feed_back(
        index, after(partial, down_mine, down_theirs, mixed_out), branch, factor,
        stacked, normed_t, 2, (hat, rstd, layer_norm_gains, stacked),
    )
    got_2 = sibling(away_2)
    mix_t = mix.T
    out_got = sibling(away_rows(index, mix_t, grad_attn_half, DIM))
    down_sum = add(down_mine, after(down_pair, grad_mix))
    down_far = to_owner(down_sum)

    def back(grads, kv_set, at, first, count, more=(), skip=0):
        return attend_back(place, qx, kv_set, grads, mix, at, first, count, scale, more, skip)

    def join(pair, single):
        return jnp.concatenate([pair[0], pair[1], single], axis=1)

    vectors = jnp.concatenate([vec_one, vec_two], axis=0)
    second_mine, second_theirs = core_sum(keep_2, got_2)
    out_mine, out_theirs = keep_rows(index, mix_t, grad_attn_half, out_got, DIM)
    second_mine = join(second_mine, out_mine)
    second_theirs = join(second_theirs, out_theirs)
    second_pair = pair_z(second_theirs)
    grads = after(grad_mix, down_sum, second_mine, second_theirs)
    dq_2, dk_2, dv_2 = back(grads, kv_other, 2, 4, 2)
    other_2 = sibling(dk_2), sibling(dv_2)
    first_sum = add(first_mine, after(first_pair, dq_2))
    first_far = to_owner(first_sum)
    vectors = vectors + pair_z(after(vectors, dq_2))
    grads = after(grads, first_sum)
    dq_1, dk_1, dv_1 = back(grads, kv_other, 2, 0, 4)
    other_1 = sibling(dk_1), sibling(dv_1)
    second_sum = add(second_mine, after(second_pair, dq_1))
    second_far = to_owner(second_sum)
    flag = owner.astype(jnp.int32).reshape(1)
    merged_down, left_down = merge_down(
        flag, (down_sum, after(down_far, dq_1)), err_down, start_down[0].T
    )
    tokens_t = rows_in.T

    def away_part(right):
        return away_rows(index, tokens_t, right, 256)

    def keep_part(right, got):
        return keep_rows(index, tokens_t, right, got, 256)

    grads = after(grads, second_sum)
    grads_2 = back(grads, kv, 0, 4, 2, (dq_2, *other_2, cos, sin))
    away_2 = away_part(grads_2)
    got_2 = sibling(away_2)
    vectors = vectors + mirror_z(after(vectors, grads_2))
    grads = after(grads, away_2, first_far, down_far)
    grads_0 = back(grads, kv, 0, 0, 2, (dq_1, *other_1, cos, sin))
    away_0 = away_part(grads_0)
    got_0 = sibling(away_0)
    mine_2, theirs_2 = keep_part(grads_2, after(got_2, away_0))
    mine_0, theirs_0 = keep_part(grads_0, got_0)
    qkv_mine = jnp.concatenate([mine_0, mine_2], axis=1)
    qkv_theirs = jnp.concatenate([theirs_0, theirs_2], axis=1)
    qkv_pair = pair_z(qkv_theirs)
    grads = after(grads, qkv_mine, qkv_theirs, second_far)
    grads_1 = back(grads, kv, 0, 2, 2, (dq_1, *other_1, cos, sin), 2)
    away_1 = away_part(grads_1)
    got_1 = sibling(away_1)
    qkv_sum = add(qkv_mine, after(qkv_pair, away_1))
    qkv_far = to_owner(qkv_sum)
    merged_gate_up, merged_out, left_main = merge_main(
        flag, (first_sum, first_far), (second_sum, after(second_far, qkv_sum)),
        err_gate_up, err_out, start_gate_up[0].T, start_out[0].T,
    )
    packed = jnp.concatenate([left_main, left_down, vectors.reshape(RANK, width // 2)], axis=1)
    packed = plane_sum(packed)
    mine_1, theirs_1 = keep_part(grads_1, after(got_1, left_main))
    pair_1 = pair_z(theirs_1)
    input_rows = input_rows_of(
        (grads_0, grads_1, grads_2), qkv_t, after(grad_attn, mine_1, theirs_1)
    )
    input_grad = bring_back(input_rows).astype(f32)
    sum_1 = add(mine_1, after(pair_1, input_rows))
    far_1 = to_owner(sum_1)

    norm_grad = packed[:, 1280:].reshape(4, width) / REPS
    params = jnp.stack(
        [layer_norm_gains[0], layer_norm_biases[0], layer_norm_gains[1], layer_norm_biases[1]]
    )
    norm_moment_new = MOMENTUM * norm_moments + norm_grad
    norm_new = params - NORM_RATE * norm_moment_new
    early = compress(
        packed[:, :1280],
        (merged_gate_up, merged_out, merged_down),
        ((0, 192), (256, 192), (512, 768)),
        (w_gate_up, w_out, w_down),
        (mom_gate_up, mom_out, mom_down),
        (LEARN_RATES[2], LEARN_RATES[1], LEARN_RATES[3]),
        rep,
    )
    merged_qkv, left_qkv = merge_qkv(
        flag, (qkv_sum, sum_1, qkv_sum), (qkv_far, far_1, qkv_far), err_qkv, start_qkv[0].T
    )
    late = compress(
        plane_sum(left_qkv), (merged_qkv,), ((0, 192),), (w_qkv,), (mom_qkv,),
        LEARN_RATES[:1], rep,
    )
    results = (late[0], early[1], early[0], early[2])
    new_weights, new_moments, new_errors, bases, factors = zip(*results)
    return (
        mixed_out,
        input_grad,
        *new_weights,
        *new_moments,
        *new_errors,
        *bases,
        *factors,
        norm_moment_new,
        norm_new,
    )


def choose(mesh):
    if mesh.shape["rep"] == REPS and mesh.shape["shard"] == SHARDS:
        return fast_device
    return general_device


def solution(mesh):
    placed = (
        P("rep", "shard", None),
        P("rep", "shard", None),
        P("rep"),
        P("shard", "rep"),
        P("shard", "rep"),
        P("shard", "rep"),
        P("shard", "rep"),
        P("shard", "rep"),
        P("shard", "rep"),
        P("shard", "rep"),
        P("shard", "rep"),
        P("rep", "shard", None),
        P("rep", "shard", None),
        P("rep", "shard", None),
        P("rep", "shard", None),
        P("shard", None, None),
        P("shard", None, None),
        P("shard", None, None),
        P("shard", None, None),
        P(),
        P(),
        P(),
    )
    return jax.shard_map(
        choose(mesh),
        mesh=mesh,
        in_specs=placed,
        out_specs=(
            P("rep", "shard", None),
            P("rep", "shard", None),
            P("shard", "rep"),
            P("shard", "rep"),
            P("shard", "rep"),
            P("shard", "rep"),
            P("shard", "rep"),
            P("shard", "rep"),
            P("shard", "rep"),
            P("shard", "rep"),
            P("rep", "shard", None),
            P("rep", "shard", None),
            P("rep", "shard", None),
            P("rep", "shard", None),
            P("shard", None),
            P("shard", None),
            P("shard", None),
            P("shard", None),
            P("shard", None, None),
            P("shard", None, None),
            P("shard", None, None),
            P("shard", None, None),
            P(),
            P(),
        ),
        check_vma=False,
    )
```

```python
import functools
import math

import jax
import jax.numpy as jnp
from jax import lax
from jax.experimental import pallas as pl
from jax.experimental.pallas import tpu as pltpu
from jax.sharding import PartitionSpec as P

H = 12
HD = 64
FF = 3072


EPS = 1e-05
ROPE_BASE = 1000.0
MOMENTUM = 0.5
LEARN_RATES = (0.002, 0.1, 0.004, 0.002)
NORM_RATE = 0.01
NEG_FILL = -1e30


def norm_components(values_in, gain, bias):
    centre = jnp.mean(values_in, axis=-1, keepdims=True)
    centred = values_in - centre
    spread = jnp.mean(centred * centred, axis=-1, keepdims=True)
    row_rstd = lax.rsqrt(spread + EPS)
    normed = centred * row_rstd
    return (normed * gain + bias, normed, row_rstd)


def norm_reverse_pass(grad_in, normed, row_rstd):
    return row_rstd * (
        grad_in
        - jnp.mean(grad_in, axis=-1, keepdims=True)
        - normed * jnp.mean(grad_in * normed, axis=-1, keepdims=True)
    )


def rotary(values_in, cosine_table, sine_table):
    half_dim = values_in.shape[-1] // 2
    leading_half = values_in[..., :half_dim]
    second_half = values_in[..., half_dim:]
    return jnp.concatenate(
        [
            leading_half * cosine_table - second_half * sine_table,
            second_half * cosine_table + leading_half * sine_table,
        ],
        axis=-1,
    )


def rotary_back(grad_in, cosine_table, sine_table):
    half_dim = grad_in.shape[-1] // 2
    leading_half = grad_in[..., :half_dim]
    second_half = grad_in[..., half_dim:]
    return jnp.concatenate(
        [
            leading_half * cosine_table + second_half * sine_table,
            second_half * cosine_table - leading_half * sine_table,
        ],
        axis=-1,
    )


def orthonormal(factor):
    columns = []
    for column in range(factor.shape[1]):
        vector = factor[:, column]
        for earlier in columns:
            vector = vector - jnp.sum(earlier * vector) * earlier
        vector = vector * lax.rsqrt(jnp.sum(vector * vector) + 1e-06)
        columns.append(vector)
    return jnp.stack(columns, axis=1)


def general_device(
    tokens,
    cotangent,
    lengths,
    w_qkv,
    w_out,
    w_gate_up,
    w_down,
    mom_qkv,
    mom_out,
    mom_gate_up,
    mom_down,
    err_qkv,
    err_out,
    err_gate_up,
    err_down,
    start_qkv,
    start_out,
    start_gate_up,
    start_down,
    layer_norm_gains,
    layer_norm_biases,
    norm_moments,
):
    single_float = jnp.float32
    bf16 = jnp.bfloat16
    wide_cols = (
        lax.all_gather(w_qkv.astype(bf16), "rep", axis=1, tiled=True),
        lax.all_gather(w_out.astype(bf16), "rep", axis=1, tiled=True),
        lax.all_gather(w_gate_up.astype(bf16), "rep", axis=1, tiled=True),
        lax.all_gather(w_down.astype(bf16), "rep", axis=1, tiled=True),
    )
    complete_query_key_value, complete_out_weight, complete_gate_up_weight, complete_down_weight = (
        lax.all_gather(wide_cols[0], "shard", axis=0, tiled=True),
        lax.all_gather(wide_cols[1], "shard", axis=0, tiled=True),
        lax.all_gather(wide_cols[2], "shard", axis=0, tiled=True),
        lax.all_gather(wide_cols[3], "shard", axis=0, tiled=True),
    )
    groups, local_len, model_width = tokens.shape
    shards = lax.axis_size("shard")
    seq_len = local_len * shards
    score_scale = HD ** (-0.5)
    offset = lax.axis_index("shard") * local_len
    position = offset + jnp.arange(local_len, dtype=jnp.int32)
    valid_rows = position[None, :] < lengths[:, None]
    key_keep = jnp.arange(seq_len, dtype=jnp.int32)[None, :] < lengths[:, None]
    inverse = jnp.exp(
        jnp.arange(HD // 2, dtype=jnp.int32).astype(single_float)
        * (-2.0 * math.log(ROPE_BASE) / HD)
    )
    angle = position.astype(single_float)[:, None] * inverse[None, :]
    cosine_table = jnp.cos(angle)[:, None, :]
    sine_table = jnp.sin(angle)[:, None, :]
    query_key_value_rows = jnp.einsum(
        "znk,kb->znb", tokens, complete_query_key_value, preferred_element_type=single_float
    )
    query_key_value_rows = query_key_value_rows.reshape(groups, local_len, 3, H, HD)
    q_half = (
        rotary(query_key_value_rows[:, :, 0], cosine_table, sine_table)
        .astype(bf16)
        .transpose(2, 0, 1, 3)
    )
    k_half = (
        rotary(query_key_value_rows[:, :, 1], cosine_table, sine_table)
        .astype(bf16)
        .transpose(2, 0, 1, 3)
    )
    v_half = query_key_value_rows[:, :, 2].astype(bf16).transpose(2, 0, 1, 3)
    key_all, value_all = (
        lax.all_gather(k_half, "shard", axis=2, tiled=True),
        lax.all_gather(v_half, "shard", axis=2, tiled=True),
    )

    def head_forward(inputs):
        query_h, key_h, value_h = inputs
        scores = (
            jnp.einsum("sqd,skd->sqk", query_h, key_h, preferred_element_type=single_float)
            * score_scale
        )
        scores = jnp.where(key_keep[:, None, :], scores, NEG_FILL)
        row_peak = jnp.max(scores, axis=-1, keepdims=True)
        exp_scores = jnp.exp(scores - row_peak)
        row_total = jnp.sum(exp_scores, axis=-1, keepdims=True)
        attn_probs = (exp_scores / row_total).astype(bf16)
        head_rows = jnp.einsum(
            "sqk,skd->sqd", attn_probs, value_h, preferred_element_type=single_float
        )
        return (head_rows, (row_peak + jnp.log(row_total))[..., 0])

    head_out, log_total = lax.map(head_forward, (q_half, key_all, value_all))
    mix_half = head_out.astype(bf16)
    mixture_rows = mix_half.transpose(1, 2, 0, 3).reshape(groups, local_len, model_width)
    attention_result = jnp.einsum(
        "znk,kb->znb", mixture_rows, complete_out_weight, preferred_element_type=single_float
    )
    attention_normed, attention_standardized, attention_inverse_deviation = norm_components(
        tokens.astype(single_float) + attention_result, layer_norm_gains[0], layer_norm_biases[0]
    )
    leading_half = attention_normed.astype(bf16)
    gate_up_output = jnp.einsum(
        "znk,kb->znb", leading_half, complete_gate_up_weight, preferred_element_type=single_float
    )
    gate_part = gate_up_output[..., :FF]
    up_part = gate_up_output[..., FF:]
    gate_sig = jax.nn.sigmoid(gate_part)
    hidden_state = (gate_part * gate_sig * up_part).astype(bf16)
    residual_branch = jnp.einsum(
        "ckh,hy->cky", hidden_state, complete_down_weight, preferred_element_type=single_float
    )
    feedforward_normed, feedforward_standardized, feedforward_inverse_deviation = norm_components(
        attention_normed + residual_branch, layer_norm_gains[1], layer_norm_biases[1]
    )
    mixed_out = feedforward_normed.astype(bf16)
    output_gradient = cotangent.astype(single_float) * valid_rows[..., None].astype(single_float)
    feedforward_gain = jnp.sum(output_gradient * feedforward_standardized, axis=(0, 1))
    bias_two = jnp.sum(output_gradient, axis=(0, 1))
    trailing_norm_gradient = norm_reverse_pass(
        output_gradient * layer_norm_gains[1],
        feedforward_standardized,
        feedforward_inverse_deviation,
    )
    branch_gradient = trailing_norm_gradient.astype(bf16)
    down_weight_gradient = jnp.einsum(
        "zxi,zxp->ip", hidden_state, branch_gradient, preferred_element_type=single_float
    )
    hidden_gradient = jnp.einsum(
        "gbz,wz->gbw", branch_gradient, complete_down_weight, preferred_element_type=single_float
    )
    grad_gate = hidden_gradient * up_part * gate_sig * (1.0 + gate_part * (1.0 - gate_sig))
    grad_up = hidden_gradient * gate_part * gate_sig
    gate_up_gradient = jnp.concatenate([grad_gate, grad_up], axis=-1).astype(bf16)
    gate_up_weight_gradient = jnp.einsum(
        "vcm,vcb->mb", leading_half, gate_up_gradient, preferred_element_type=single_float
    )
    leading_norm_gradient = (
        jnp.einsum(
            "thi,ci->thc",
            gate_up_gradient,
            complete_gate_up_weight,
            preferred_element_type=single_float,
        )
        + trailing_norm_gradient
    )
    attention_gain = jnp.sum(leading_norm_gradient * attention_standardized, axis=(0, 1))
    bias_one = jnp.sum(leading_norm_gradient, axis=(0, 1))
    attention_gradient = norm_reverse_pass(
        leading_norm_gradient * layer_norm_gains[0],
        attention_standardized,
        attention_inverse_deviation,
    )
    attention_gradient_half = attention_gradient.astype(bf16)
    out_weight_gradient = jnp.einsum(
        "vcm,vcb->mb", mixture_rows, attention_gradient_half, preferred_element_type=single_float
    )
    mixture_gradient = jnp.einsum(
        "thi,ci->thc",
        attention_gradient_half,
        complete_out_weight,
        preferred_element_type=single_float,
    )
    grad_mix_half = (
        mixture_gradient.astype(bf16).reshape(groups, local_len, H, HD).transpose(2, 0, 1, 3)
    )

    def head_back(inputs):
        query_h, key_h, value_h, grad_h, lse_h = inputs
        scores = (
            jnp.einsum("sqd,skd->sqk", query_h, key_h, preferred_element_type=single_float)
            * score_scale
        )
        scores = jnp.where(key_keep[:, None, :], scores, NEG_FILL)
        attn_probs = jnp.exp(scores - lse_h[..., None])
        grad_probs = jnp.einsum(
            "sqd,skd->sqk", grad_h, value_h, preferred_element_type=single_float
        )
        row_delta = jnp.sum(grad_probs * attn_probs, axis=-1, keepdims=True)
        grad_scores = (attn_probs * (grad_probs - row_delta)).astype(bf16)
        grad_query = (
            jnp.einsum("sqk,skd->sqd", grad_scores, key_h, preferred_element_type=single_float)
            * score_scale
        )
        grad_key = (
            jnp.einsum("sqk,sqd->skd", grad_scores, query_h, preferred_element_type=single_float)
            * score_scale
        )
        grad_value = jnp.einsum(
            "sqk,sqd->skd", attn_probs.astype(bf16), grad_h, preferred_element_type=single_float
        )
        return (grad_query, grad_key, grad_value)

    grad_q_heads, key_parts, value_parts = lax.map(
        head_back, (q_half, key_all, value_all, grad_mix_half, log_total)
    )
    grad_k_heads, grad_v_heads = (
        lax.psum_scatter(key_parts, "shard", scatter_dimension=2, tiled=True),
        lax.psum_scatter(value_parts, "shard", scatter_dimension=2, tiled=True),
    )
    grad_q_rows = rotary_back(grad_q_heads.transpose(1, 2, 0, 3), cosine_table, sine_table)
    grad_k_rows = rotary_back(grad_k_heads.transpose(1, 2, 0, 3), cosine_table, sine_table)
    grad_v_rows = grad_v_heads.transpose(1, 2, 0, 3)
    query_key_value_gradient = jnp.stack([grad_q_rows, grad_k_rows, grad_v_rows], axis=2)
    query_key_value_gradient = query_key_value_gradient.reshape(
        groups, local_len, 3 * model_width
    ).astype(bf16)
    query_key_value_weight_gradient = jnp.einsum(
        "vcm,vcb->mb", tokens, query_key_value_gradient, preferred_element_type=single_float
    )
    input_grad = (
        jnp.einsum(
            "thi,ci->thc",
            query_key_value_gradient,
            complete_query_key_value,
            preferred_element_type=single_float,
        )
        + attention_gradient
    )
    owned = (
        lax.psum_scatter(
            query_key_value_weight_gradient.astype(jnp.bfloat16),
            "shard",
            scatter_dimension=0,
            tiled=True,
        ).astype(jnp.float32),
        lax.psum_scatter(
            out_weight_gradient.astype(jnp.bfloat16), "shard", scatter_dimension=0, tiled=True
        ).astype(jnp.float32),
        lax.psum_scatter(
            gate_up_weight_gradient.astype(jnp.bfloat16), "shard", scatter_dimension=0, tiled=True
        ).astype(jnp.float32),
        lax.psum_scatter(
            down_weight_gradient.astype(jnp.bfloat16), "shard", scatter_dimension=0, tiled=True
        ).astype(jnp.float32),
    )
    replicas = lax.axis_size("rep")
    vector_parts = jnp.stack([attention_gain, bias_one, feedforward_gain, bias_two])
    norm_grad = lax.psum(vector_parts, ("rep", "shard")) / replicas
    params = jnp.stack(
        [layer_norm_gains[0], layer_norm_biases[0], layer_norm_gains[1], layer_norm_biases[1]]
    )
    norm_moment_new = MOMENTUM * norm_moments + norm_grad
    norm_new = params - NORM_RATE * norm_moment_new
    errors = (err_qkv, err_out, err_gate_up, err_down)
    starts = (start_qkv, start_out, start_gate_up, start_down)
    masters = (w_qkv, w_out, w_gate_up, w_down)
    moments = (mom_qkv, mom_out, mom_gate_up, mom_down)
    merged = tuple((part + error_set[0] for part, error_set in zip(owned, errors)))
    projected = tuple(
        (
            jnp.dot(block, start_set[0], precision=lax.Precision.HIGHEST)
            for block, start_set in zip(merged, starts)
        )
    )
    summed_left = lax.psum((projected[0], projected[1], projected[2], projected[3]), "rep")
    bases = tuple((orthonormal(part / replicas) for part in summed_left))
    pulled = tuple(
        (
            jnp.einsum("rc,rk->ck", block, basis, precision=lax.Precision.HIGHEST)
            for block, basis in zip(merged, bases)
        )
    )
    summed_right = (
        lax.psum(pulled[0].astype(jnp.bfloat16), "rep").astype(jnp.float32),
        lax.psum(pulled[1].astype(jnp.bfloat16), "rep").astype(jnp.float32),
        lax.psum(pulled[2].astype(jnp.bfloat16), "rep").astype(jnp.float32),
        lax.psum(pulled[3].astype(jnp.bfloat16), "rep").astype(jnp.float32),
    )
    factors = tuple((part / replicas for part in summed_right))
    rep_pos = lax.axis_index("rep")
    new_weights = []
    new_moments = []
    new_errors = []
    for block, basis, factor, master, moment, step_rate in zip(
        merged, bases, factors, masters, moments, LEARN_RATES
    ):
        approx = jnp.dot(basis, factor.T, precision=lax.Precision.HIGHEST)
        new_errors.append((block - approx)[None])
        col_count = master.shape[1]
        piece = lax.dynamic_slice_in_dim(approx, rep_pos * col_count, col_count, 1)
        moment_new = MOMENTUM * moment + piece
        new_moments.append(moment_new)
        new_weights.append(master - step_rate * moment_new)
    return (
        mixed_out,
        input_grad,
        new_weights[0],
        new_weights[1],
        new_weights[2],
        new_weights[3],
        new_moments[0],
        new_moments[1],
        new_moments[2],
        new_moments[3],
        new_errors[0],
        new_errors[1],
        new_errors[2],
        new_errors[3],
        bases[0],
        bases[1],
        bases[2],
        bases[3],
        factors[0][None],
        factors[1][None],
        factors[2][None],
        factors[3][None],
        norm_moment_new,
        norm_new,
    )


AXES = ("rep", "shard")
SHARDS = 4
REPS = 8
RANK = 8
DIM = 768
PAIRS = 6
LANES = 128
MIB = 2**20


def send(values, move):
    pairs = []
    for rep in range(REPS):
        for shard in range(SHARDS):
            to = move(rep, shard)
            if to is not None and to != (rep, shard):
                pairs.append((rep * SHARDS + shard, to[0] * SHARDS + to[1]))
    return lax.ppermute(values, AXES, pairs)


def spread_move(parity):
    return lambda r, z: (r - r % 2 + z // 2, 2 * (r % 2) + (z + parity) % 2)


def gather_move(parity):
    table = {}
    for r in range(REPS):
        for z in range(SHARDS):
            table[spread_move(parity)(r, z)] = (r, z)
    return lambda r, z: table[(r, z)]


def sibling(values):
    return send(values, lambda r, z: (r ^ 1, z))


def near_x(values):
    return send(values, lambda r, z: (r ^ 2, z))


def near_y(values):
    return send(values, lambda r, z: (r ^ 4, z))


def pair_z(values):
    return send(values, lambda r, z: (r, z ^ 1))


def mirror_z(values):
    return send(values, lambda r, z: (r, 3 - z))


def to_owner(values):
    return send(values, lambda r, z: (r ^ 1, 3 - z) if r % 2 != z // 2 else None)


def turn_z(values, step):
    return send(values, lambda r, z: (r, (z + step) % SHARDS))


def after(values, *others):
    return lax.optimization_barrier((values, *others))[0]


def shard_gather(piece, shard):
    parts = jnp.stack([piece] + [turn_z(piece, step) for step in (1, 2, 3)])
    return [
        lax.dynamic_index_in_dim(parts, (shard - at) % SHARDS, 0, keepdims=False)
        for at in range(SHARDS)
    ]


def plane_near(piece):
    return near_x(piece), near_y(piece)


def plane_far(piece, near):
    half = piece.shape[0] // 2
    from_x, from_y = near
    return near_x(from_y[:half]), near_y(from_x[half:])


def exchange(piece, near, far):
    return [sibling(part) for part in (piece, *near, jnp.concatenate(far, axis=0))]


def plane_all(piece, near, far, others, rep, ahead=()):
    return stack_pieces((piece, *near, *far, *others), rep, *piece.shape, ahead)


PIECE_STEPS = ((0, None), (2, None), (4, None), (6, 0), (6, 1), (1, None), (3, None), (5, None), (7, None))


def stack_kernel(rep_ref, *refs):
    count = len(PIECE_STEPS)
    pieces = refs[:count]
    whole, staged, sems_in, sems_out = refs[-4:]
    rep = rep_ref[0]
    half = pieces[3].shape[0]
    fetches = []
    stores = []
    for slot, (step, side) in enumerate(PIECE_STEPS):
        stage = staged.at[step]
        place = whole.at[rep ^ step]
        if side is not None:
            part = pl.ds(side * half, half)
            stage = stage.at[part]
            place = place.at[part]
        fetches.append(pltpu.make_async_copy(pieces[slot], stage, sems_in.at[slot]))
        stores.append(pltpu.make_async_copy(stage, place, sems_out.at[slot]))
    for fetch in fetches:
        fetch.start()
    for fetch, store in zip(fetches, stores):
        fetch.wait()
        store.start()
    for store in stores:
        store.wait()


def stack_pieces(pieces, rep, rows, cols, ahead):
    anywhere = pl.BlockSpec(memory_space=pl.ANY)
    count = len(pieces)
    return pl.pallas_call(
        stack_kernel,
        in_specs=[pl.BlockSpec(memory_space=pltpu.SMEM)] + [anywhere] * (count + len(ahead)),
        out_specs=anywhere,
        out_shape=jax.ShapeDtypeStruct((REPS, rows, cols), pieces[0].dtype),
        scratch_shapes=[
            pltpu.VMEM((REPS, rows, cols), pieces[0].dtype),
            pltpu.SemaphoreType.DMA((count,)),
            pltpu.SemaphoreType.DMA((count,)),
        ],
        compiler_params=limit(40),
        cost_estimate=pl.CostEstimate(
            flops=0, bytes_accessed=4 * REPS * rows * cols, transcendentals=0
        ),
        name="stack_pieces",
    )(jnp.reshape(rep, (1,)), *pieces, *ahead)


def plane_sum(values):
    values = values + sibling(values)
    values = values + near_x(values)
    return values + near_y(values)


def plane_sum_half(values):
    bf16 = jnp.bfloat16
    f32 = jnp.float32
    for step in (sibling, near_x, near_y):
        rounded = values.astype(bf16)
        values = rounded.astype(f32) + step(rounded).astype(f32)
    return values


def nt(left, right):
    return lax.dot_general(
        left, right, (((1,), (1,)), ((), ())), preferred_element_type=jnp.float32
    )


def nn(left, right):
    return lax.dot_general(
        left, right, (((1,), (0,)), ((), ())), preferred_element_type=jnp.float32
    )


def cost(flops, moved, powers=0):
    return pl.CostEstimate(flops=int(flops), bytes_accessed=int(moved), transcendentals=int(powers))


def limit(mib):
    return pltpu.CompilerParams(vmem_limit_bytes=mib * MIB)


def shape(dims, dtype):
    return jax.ShapeDtypeStruct(dims, dtype)


def partner_lanes(values):
    lane = lax.broadcasted_iota(jnp.int32, values.shape, 1)
    up = pltpu.roll(values, 96, 1)
    down = pltpu.roll(values, 32, 1)
    return jnp.where(lane % HD < HD // 2, up, down)


def project_kernel(x_ref, w_ref, cos_ref, sin_ref, *refs, turned, scale):
    out_ref = refs[-1]
    values = nt(x_ref[...], w_ref[...])

    def turn():
        for at in range(0, values.shape[1], LANES):
            part = values[:, at : at + LANES]
            part = part * cos_ref[...] + partner_lanes(part) * sin_ref[...]
            out_ref[:, at : at + LANES] = (part * scale).astype(out_ref.dtype)

    if turned is None:
        turn()
    else:
        pl.when(pl.program_id(0) < turned)(turn)

        @pl.when(pl.program_id(0) >= turned)
        def _():
            out_ref[...] = values.astype(out_ref.dtype)


def project(rows_in, qkv_t, cos, sin, first, count, turned, scale, ahead=()):
    rows = rows_in.shape[0]
    tile = DIM
    fixed = lambda j: (0, 0)
    return pl.pallas_call(
        functools.partial(project_kernel, turned=turned, scale=scale),
        grid=(count,),
        in_specs=[
            pl.BlockSpec((rows, DIM), fixed),
            pl.BlockSpec((tile, DIM), lambda j: (j + first, 0)),
            pl.BlockSpec((rows, LANES), fixed),
            pl.BlockSpec((rows, LANES), fixed),
        ]
        + [pl.BlockSpec(memory_space=pl.ANY)] * len(ahead),
        out_specs=pl.BlockSpec((rows, tile), lambda j: (0, j)),
        out_shape=shape((rows, count * tile), jnp.bfloat16),
        compiler_params=limit(48),
        cost_estimate=cost(2 * rows * DIM * tile * count, 4 * rows * DIM + 4 * count * tile * rows),
        name="project",
    )(rows_in, qkv_t, cos, sin, *ahead)


def lane_of(dims):
    return lax.broadcasted_iota(jnp.int32, dims, 1)


def head_lanes(dims, head):
    lane = lane_of(dims)
    return (lane >= HD) if head else (lane < HD)


def extra_lane(head):
    return 0 if head else HD


def key_fill(place_ref, at, count, start):
    row = lax.broadcasted_iota(jnp.int32, (count, LANES), 0) + start
    half = place_ref[6]
    position = jnp.where(row < half, place_ref[at] + row, place_ref[at + 1] + row - half)
    return jnp.where(position < place_ref[4], 0.0, NEG_FILL).astype(jnp.bfloat16)


def attend_kernel(place_ref, q_ref, ka_ref, va_ref, kb_ref, vb_ref, *refs):
    mix_ref, qx_ref, keys, values = refs[-4:]
    rows = ka_ref.shape[0]
    bf16 = jnp.bfloat16

    @pl.when(pl.program_id(1) == 0)
    def _():
        dims = (rows, LANES)
        zero = jnp.zeros(dims, bf16)
        for source, (k_ref, v_ref) in enumerate(((ka_ref, va_ref), (kb_ref, vb_ref))):
            fill = key_fill(place_ref, 2 * source, rows, 0)
            part = pl.ds(source * rows, rows)
            for head in range(2):
                inside = head_lanes(dims, head)
                other = jnp.where(lane_of(dims) == extra_lane(head), fill, zero)
                keys[head, part] = jnp.where(inside, k_ref[...], other)
                values[head, part] = jnp.where(inside, v_ref[...], zero)

    queries = q_ref[...]
    dims = queries.shape
    lane = lane_of(dims)
    total = None
    for head in range(2):
        inside = head_lanes(dims, head)
        spare = lane - extra_lane(head)
        one = jnp.where(spare == 0, 1.0, 0.0).astype(bf16)
        masked = jnp.where(inside, queries, one)
        scores = nt(masked, keys[head])
        peak = jnp.max(scores, axis=1, keepdims=True)
        powers = jnp.exp(scores - peak)
        row_sum = jnp.sum(powers, axis=1, keepdims=True)
        out = nn(powers.astype(bf16), values[head]) / row_sum
        total = out if total is None else total + out
        lse = peak + jnp.log(row_sum)
        high = lse.astype(bf16)
        middle = (lse - high.astype(jnp.float32)).astype(bf16)
        low = (lse - high.astype(jnp.float32) - middle.astype(jnp.float32)).astype(bf16)
        wide = jnp.where(spare == 1, -high, jnp.where(spare == 2, -middle, -low))
        wide = jnp.where((spare >= 1) & (spare <= 3), wide, one)
        qx_ref[:, head * LANES : (head + 1) * LANES] = jnp.where(inside, queries, wide)
    mix_ref[...] = total.astype(bf16)


def attend(place, q, kv_own, kv_other, first, count, done=()):
    rows = q.shape[0]
    block = 256
    bf16 = jnp.bfloat16
    key_spec = pl.BlockSpec((rows, LANES), lambda p, i: (0, p + first))
    value_spec = pl.BlockSpec((rows, LANES), lambda p, i: (0, p + first + PAIRS))
    return pl.pallas_call(
        attend_kernel,
        grid=(count, rows // block),
        in_specs=[
            pl.BlockSpec(memory_space=pltpu.SMEM),
            pl.BlockSpec((block, LANES), lambda p, i: (i, p + first)),
            key_spec,
            value_spec,
            key_spec,
            value_spec,
        ]
        + [pl.BlockSpec(memory_space=pl.ANY)] * len(done),
        out_specs=[
            pl.BlockSpec((block, LANES), lambda p, i: (i, p + first)),
            pl.BlockSpec((block, 2 * LANES), lambda p, i: (i, p + first)),
        ],
        out_shape=[shape((rows, DIM), bf16), shape((rows, 2 * DIM), bf16)],
        scratch_shapes=[
            pltpu.VMEM((2, 2 * rows, LANES), bf16),
            pltpu.VMEM((2, 2 * rows, LANES), bf16),
        ],
        input_output_aliases={6: 0, 7: 1} if done else {},
        compiler_params=limit(48),
        cost_estimate=cost(
            64 * count * rows * 2 * rows * HD, 32 * rows * LANES * count, 2 * count * rows * 2 * rows
        ),
        name="attend",
    )(place, q, kv_own, kv_own, kv_other, kv_other, *done)


def attend_back_kernel(place_ref, qx_ref, k_ref, v_ref, g_ref, mix_ref, *refs, at, scale):
    bf16 = jnp.bfloat16
    f32 = jnp.float32
    last = at == 0
    if last:
        dq_ref, got_k_ref, got_v_ref, cos_ref, sin_ref, out_ref, gx, g0, q0, acc = refs
    else:
        dq_ref, dk_ref, dv_ref, gx, g0, q0, acc = refs
    rows = g_ref.shape[0]
    count = k_ref.shape[0]
    step = pl.program_id(1)

    @pl.when(step == 0)
    def _():
        dims = (rows, LANES)
        lane = lane_of(dims)
        grad = g_ref[...]
        product = grad.astype(f32) * mix_ref[...].astype(f32)
        zero = jnp.zeros(dims, bf16)
        for head in range(2):
            inside = head_lanes(dims, head)
            spare = lane - extra_lane(head)
            delta = jnp.sum(jnp.where(inside, product, 0.0), axis=1, keepdims=True)
            high = delta.astype(bf16)
            middle = (delta - high.astype(f32)).astype(bf16)
            low = (delta - high.astype(f32) - middle.astype(f32)).astype(bf16)
            wide = jnp.where(spare == 1, -high, jnp.where(spare == 2, -middle, -low))
            wide = jnp.where((spare >= 1) & (spare <= 3), wide, zero)
            gx[head] = jnp.where(inside, grad, wide)
            g0[head] = jnp.where(inside, grad, zero)
            q0[head] = jnp.where(inside, qx_ref[:, head * LANES : (head + 1) * LANES], zero)
        acc[...] = jnp.zeros_like(acc)

    keys = k_ref[...]
    values = v_ref[...]
    dims = keys.shape
    lane = lane_of(dims)
    fill = key_fill(place_ref, at, count, step * count)
    keys_t = keys.astype(f32).T.astype(bf16)
    dk = None
    dv = None
    for head in range(2):
        inside = head_lanes(dims, head)
        spare = lane - extra_lane(head)
        ones = jnp.where((spare >= 1) & (spare <= 3), 1.0, 0.0).astype(bf16)
        keys_x = jnp.where(inside, keys, jnp.where(spare == 0, fill, ones))
        values_x = jnp.where(inside, values, ones)
        scores = nt(keys_x, qx_ref[:, head * LANES : (head + 1) * LANES])
        probs = jnp.exp(scores)
        dv_head = nn(probs.astype(bf16), g0[head])
        grad_probs = nt(values_x, gx[head])
        grad_scores = (probs * grad_probs).astype(bf16)
        dk_head = nn(grad_scores, q0[head])
        part = slice(head * HD, (head + 1) * HD)
        acc[part] += nn(keys_t[part], grad_scores)
        dk = dk_head if dk is None else dk + dk_head
        dv = dv_head if dv is None else dv + dv_head
    if last:
        here = pl.ds(pl.multiple_of(step * count, count), count)
        dk = dk + got_k_ref[...].astype(f32)
        dk = dk * cos_ref[here] - partner_lanes(dk) * sin_ref[here]
        out_ref[1, here] = dk.astype(bf16)
        out_ref[2, here] = (dv + got_v_ref[...].astype(f32)).astype(bf16)
    else:
        dk_ref[...] = dk.astype(bf16)
        dv_ref[...] = dv.astype(bf16)

    @pl.when(step == pl.num_programs(1) - 1)
    def _():
        dq = acc[...].T
        if last:
            dq = (dq + dq_ref[...]) * scale
            dq = dq * cos_ref[...] - partner_lanes(dq) * sin_ref[...]
            out_ref[0] = dq.astype(bf16)
        else:
            dq_ref[...] = dq


def attend_back(place, qx, kv, grad, mix, at, first, count, scale, more=(), skip=0):
    rows = grad.shape[0]
    block = 512
    bf16 = jnp.bfloat16
    wide = pl.BlockSpec((rows, LANES), lambda p, j: (0, p + first))
    here = pl.BlockSpec((rows, LANES), lambda p, j: (0, p))
    keys = pl.BlockSpec((block, LANES), lambda p, j: (j, p))
    table = pl.BlockSpec((rows, LANES), lambda p, j: (0, 0))
    dims = (rows, count * LANES)
    if at == 0:
        ahead = pl.BlockSpec((rows, LANES), lambda p, j: (0, p + skip))
        ahead_keys = pl.BlockSpec((block, LANES), lambda p, j: (j, p + skip))
        more_specs = [ahead, ahead_keys, ahead_keys, table, table]
        out_specs = pl.BlockSpec((3, rows, LANES), lambda p, j: (0, 0, p))
        out_shape = shape((3, *dims), bf16)
    else:
        more_specs = []
        out_specs = [here, keys, keys]
        out_shape = [shape(dims, jnp.float32), shape(dims, bf16), shape(dims, bf16)]
    return pl.pallas_call(
        functools.partial(attend_back_kernel, at=at, scale=scale),
        grid=(count, rows // block),
        in_specs=[
            pl.BlockSpec(memory_space=pltpu.SMEM),
            pl.BlockSpec((rows, 2 * LANES), lambda p, j: (0, p + first)),
            pl.BlockSpec((block, LANES), lambda p, j: (j, p + first)),
            pl.BlockSpec((block, LANES), lambda p, j: (j, p + first + PAIRS)),
            wide,
            wide,
        ]
        + more_specs,
        out_specs=out_specs,
        out_shape=out_shape,
        scratch_shapes=[
            pltpu.VMEM((2, rows, LANES), bf16),
            pltpu.VMEM((2, rows, LANES), bf16),
            pltpu.VMEM((2, rows, LANES), bf16),
            pltpu.VMEM((LANES, rows), jnp.float32),
        ],
        compiler_params=limit(48),
        cost_estimate=cost(
            80 * count * rows * rows * HD, 40 * count * rows * LANES, 2 * count * rows * rows
        ),
        name="attend_back",
    )(place, qx, kv, kv, grad, mix, *more)


def row_mean(values):
    return jnp.sum(values, axis=1, keepdims=True) * (1.0 / DIM)


def out_norm_kernel(mix_ref, w_ref, x_ref, hat_ref, rstd_ref):
    weight = w_ref[...].reshape(DIM, DIM)
    values = x_ref[...].astype(jnp.float32) + nt(mix_ref[...], weight)
    centred = values - row_mean(values)
    rstd = lax.rsqrt(row_mean(centred * centred) + EPS)
    hat_ref[...] = centred * rstd
    rstd_ref[...] = jnp.broadcast_to(rstd, rstd_ref.shape)


def out_norm(mix, stacked, rows_in):
    rows = mix.shape[0]
    block = 256
    spec = pl.BlockSpec((block, DIM), lambda i: (i, 0))
    return pl.pallas_call(
        out_norm_kernel,
        grid=(rows // block,),
        in_specs=[spec, pl.BlockSpec((REPS, 96, DIM), lambda i: (0, 8, 0)), spec],
        out_specs=[spec, pl.BlockSpec((block, LANES), lambda i: (i, 0))],
        out_shape=[shape((rows, DIM), jnp.float32), shape((rows, LANES), jnp.float32)],
        compiler_params=limit(48),
        cost_estimate=cost(2 * rows * DIM * DIM, 8 * rows * DIM),
        name="out_norm",
    )(mix, stacked, rows_in)


FF_TILE = 256
SUB = DIM // FF_TILE
FF_PIECES = FF // DIM


def row_parts(ref):
    half = ref.shape[0] // 2
    return [pl.ds(0, half), pl.ds(half, half)]


def sub_lanes():
    return pl.ds(pl.multiple_of(pl.program_id(1) * FF_TILE, FF_TILE), FF_TILE)


def at_step(piece, sub):
    return (pl.program_id(0) == piece) & (pl.program_id(1) == sub)


def feed_forward_kernel(
    hat_ref,
    gains_ref,
    biases_ref,
    wg_ref,
    wu_ref,
    wd_ref,
    hidden_ref,
    factor_ref,
    half_ref,
    acc,
    gate_s,
    up_s,
):
    bf16 = jnp.bfloat16
    f32 = jnp.float32
    step = pl.program_id(0)

    @pl.when(step == 0)
    def _():
        normed = hat_ref[...] * gains_ref[0:1] + biases_ref[0:1]
        acc[...] = normed
        half_ref[...] = normed.astype(bf16)
        gate_s[...] = jnp.zeros_like(gate_s)
        up_s[...] = jnp.zeros_like(up_s)

    gate = gate_s[...]
    up = up_s[...]
    sig = 1.0 / (1.0 + jnp.exp(-gate))
    act = gate * sig
    hidden = (act * up).astype(bf16)
    hidden_ref[...] = hidden
    factor_ref[0] = (up * sig * (1.0 + gate - act)).astype(bf16)
    factor_ref[1] = act.astype(bf16)
    rows_in = half_ref[...]
    gate_s[...] = nn(rows_in, wg_ref[0])
    up_s[...] = nn(rows_in, wu_ref[0])
    acc[...] += nt(hidden, wd_ref[...].reshape(DIM, FF_TILE))


def feed_forward(hat, gains, biases, stacked):
    rows = hat.shape[0]
    bf16 = jnp.bfloat16
    f32 = jnp.float32
    fixed = lambda t: (0, 0)
    whole = pl.BlockSpec((rows, DIM), fixed)
    small = pl.BlockSpec((2, DIM), fixed)
    tiles = FF_PIECES * SUB

    def now(t):
        return jnp.minimum(t, tiles - 1)

    def before(t):
        return jnp.maximum(t - 1, 0)

    return pl.pallas_call(
        feed_forward_kernel,
        grid=(tiles + 1,),
        in_specs=[
            whole,
            small,
            small,
            pl.BlockSpec((1, DIM, FF_TILE), lambda t: (now(t) // SUB, 0, now(t) % SUB)),
            pl.BlockSpec((1, DIM, FF_TILE), lambda t: (now(t) // SUB + FF_PIECES, 0, now(t) % SUB)),
            pl.BlockSpec(
                (REPS, 96, FF_TILE), lambda t: (0, before(t) // SUB + 9, before(t) % SUB)
            ),
        ],
        out_specs=[
            pl.BlockSpec((rows, FF_TILE), lambda t: (0, before(t))),
            pl.BlockSpec((2, rows, FF_TILE), lambda t: (0, 0, before(t))),
            whole,
            whole,
        ],
        out_shape=[
            shape((rows, FF), bf16),
            shape((2, rows, FF), bf16),
            shape((rows, DIM), bf16),
            shape((rows, DIM), f32),
        ],
        scratch_shapes=[
            pltpu.VMEM((rows, FF_TILE), f32),
            pltpu.VMEM((rows, FF_TILE), f32),
        ],
        compiler_params=limit(60),
        cost_estimate=cost(6 * rows * DIM * FF, 6 * rows * FF + 6 * DIM * FF, rows * FF),
        name="feed_forward",
    )(hat, gains, biases, stacked, stacked, stacked)


def norm_back_kernel(
    place_ref, values_ref, gains_ref, biases_ref, cot_a_ref, cot_b_ref,
    mixed_ref, grad_ref, branch_ref, vec_ref,
):
    bf16 = jnp.bfloat16
    f32 = jnp.float32
    step = pl.program_id(0)
    second = step >= pl.num_programs(0) // 2
    values = values_ref[...]
    rows = values.shape[0]
    centred = values - row_mean(values)
    rstd = lax.rsqrt(row_mean(centred * centred) + EPS)
    hat = centred * rstd
    mixed_ref[...] = (hat * gains_ref[1:2] + biases_ref[1:2]).astype(bf16)
    row = lax.broadcasted_iota(jnp.int32, (rows, 1), 0) + step * rows
    half = place_ref[6]
    position = jnp.where(row < half, place_ref[0] + row, place_ref[1] + row - half)
    cot = jnp.where(second, cot_b_ref[...].astype(f32), cot_a_ref[...].astype(f32))
    grad = jnp.where(position < place_ref[4], cot, 0.0)

    @pl.when(step == 0)
    def _():
        vec_ref[...] = jnp.zeros_like(vec_ref)

    vec_ref[0:1] += jnp.sum(grad * hat, axis=0, keepdims=True)
    vec_ref[1:2] += jnp.sum(grad, axis=0, keepdims=True)
    grad = grad * gains_ref[1:2]
    grad = rstd * (grad - row_mean(grad) - hat * row_mean(grad * hat))
    grad_ref[...] = grad
    branch_ref[...] = grad.astype(bf16)


def norm_back(place, values, gains, biases, cot):
    rows = values.shape[0]
    block = 256
    half = rows // block // 2
    f32 = jnp.float32
    bf16 = jnp.bfloat16
    spec = pl.BlockSpec((block, DIM), lambda i: (i, 0))
    small = pl.BlockSpec((2, DIM), lambda i: (0, 0))
    return pl.pallas_call(
        norm_back_kernel,
        grid=(rows // block,),
        in_specs=[
            pl.BlockSpec(memory_space=pltpu.SMEM),
            spec,
            small,
            small,
            pl.BlockSpec((block, DIM), lambda i: (jnp.minimum(i, half - 1), 0)),
            pl.BlockSpec((block, DIM), lambda i: (jnp.maximum(i - half, 0), 0)),
        ],
        out_specs=[spec, spec, spec, small],
        out_shape=[
            shape((rows, DIM), bf16),
            shape((rows, DIM), f32),
            shape((rows, DIM), bf16),
            shape((2, DIM), f32),
        ],
        compiler_params=limit(48),
        cost_estimate=cost(30 * rows * DIM, 14 * rows * DIM),
        name="norm_back",
    )(place, values, gains, biases, *cot)


def feed_back_kernel(
    index_ref,
    grad_ref,
    branch_ref,
    factor_ref,
    wg_ref,
    wu_ref,
    wd_ref,
    left_away_ref,
    left_keep_ref,
    *refs,
):
    bf16 = jnp.bfloat16
    f32 = jnp.float32
    last = len(refs) > 6
    if last:
        hat_ref, rstd_ref, gains_ref, wo_ref, away_ref, keep_ref = refs[:6]
        attn_ref, attn_half_ref, mix_grad_ref, vec_ref, acc, both, left = refs[6:]
    else:
        away_ref, keep_ref, acc_ref, acc, both, left = refs
    half_rows = left_away_ref.shape[0]
    here = sub_lanes()

    @pl.when(at_step(0, 0))
    def _():
        acc[...] = grad_ref[...]
        left[:half_rows] = left_away_ref[...]
        left[half_rows:] = left_keep_ref[...]

    grad_hidden = nn(branch_ref[...], wd_ref[...].reshape(DIM, FF_TILE))
    for side in range(2):
        grad = (grad_hidden * factor_ref[side].astype(f32)).astype(bf16)
        both[side, :, here] = grad
        product = nn(left[...], grad).astype(bf16)
        away_ref[side] = product[:half_rows]
        keep_ref[side] = product[half_rows:]

    @pl.when(pl.program_id(1) == SUB - 1)
    def _():
        acc[...] += nt(both[0], wg_ref[0]) + nt(both[1], wu_ref[0])

    @pl.when(at_step(pl.num_programs(0) - 1, SUB - 1))
    def _():
        grad = acc[...]
        if not last:
            acc_ref[...] = grad
            return
        hat = hat_ref[...]
        vec_ref[0:1] = jnp.sum(grad * hat, axis=0, keepdims=True)
        vec_ref[1:2] = jnp.sum(grad, axis=0, keepdims=True)
        grad = grad * gains_ref[0:1]
        rstd = rstd_ref[:, 0:1]
        grad = rstd * (grad - row_mean(grad) - hat * row_mean(grad * hat))
        attn_ref[...] = grad
        half = grad.astype(bf16)
        attn_half_ref[...] = half
        mix_grad_ref[...] = nn(half, wo_ref[...].reshape(DIM, DIM)).astype(bf16)


def feed_back(index, grad, branch, factor, stacked, normed_t, first, more=()):
    rows = grad.shape[0]
    bf16 = jnp.bfloat16
    f32 = jnp.float32
    fixed = lambda j, i, s: (0, 0)
    whole = pl.BlockSpec((rows, DIM), fixed)
    small = pl.BlockSpec((2, DIM), fixed)
    pieces = FF_PIECES // 2
    count = pieces * DIM
    parts = pl.BlockSpec((2, DIM // 2, FF_TILE), lambda j, i, s: (0, 0, SUB * j + i))
    in_specs = [
        whole,
        whole,
        pl.BlockSpec((2, rows, FF_TILE), lambda j, i, s: (0, 0, SUB * (j + first) + i)),
        pl.BlockSpec((1, DIM, DIM), lambda j, i, s: (j + first, 0, 0)),
        pl.BlockSpec((1, DIM, DIM), lambda j, i, s: (j + first + FF_PIECES, 0, 0)),
        pl.BlockSpec((REPS, 96, FF_TILE), lambda j, i, s: (0, j + first + 9, i)),
        pl.BlockSpec((DIM // 2, rows), lambda j, i, s: (s[0], 0)),
        pl.BlockSpec((DIM // 2, rows), lambda j, i, s: (1 - s[0], 0)),
    ]
    out_specs = [parts, parts]
    out_shape = [shape((2, DIM // 2, count), bf16)] * 2
    if more:
        in_specs += [
            whole,
            pl.BlockSpec((rows, LANES), fixed),
            small,
            pl.BlockSpec((REPS, 96, DIM), lambda j, i, s: (0, 8, 0)),
        ]
        out_specs += [whole, whole, whole, small]
        out_shape += [
            shape((rows, DIM), f32),
            shape((rows, DIM), bf16),
            shape((rows, DIM), bf16),
            shape((2, DIM), f32),
        ]
    else:
        out_specs += [whole]
        out_shape += [shape((rows, DIM), f32)]
    return pl.pallas_call(
        feed_back_kernel,
        grid_spec=pltpu.PrefetchScalarGridSpec(
            num_scalar_prefetch=1,
            grid=(pieces, SUB),
            in_specs=in_specs,
            out_specs=out_specs,
            scratch_shapes=[
                pltpu.VMEM((rows, DIM), f32),
                pltpu.VMEM((2, rows, DIM), bf16),
                pltpu.VMEM((DIM, rows), bf16),
            ],
        ),
        out_shape=out_shape,
        compiler_params=limit(60),
        cost_estimate=cost(10 * rows * DIM * count, 4 * rows * count + 10 * DIM * count),
        name="feed_back",
    )(index, grad, branch, factor, stacked, stacked, stacked, normed_t, normed_t, *more)


def away_kernel(index_ref, left_ref, right_ref, out_ref):
    right = right_ref[0] if len(right_ref.shape) == 3 else right_ref[...]
    out_ref[...] = nn(left_ref[...], right).astype(out_ref.dtype)


def keep_kernel(index_ref, la_ref, lb_ref, right_ref, ra_ref, rb_ref, out_a_ref, out_b_ref):
    right = right_ref[0] if len(right_ref.shape) == 3 else right_ref[...]
    for left, got, out in ((la_ref, ra_ref, out_a_ref), (lb_ref, rb_ref, out_b_ref)):
        out[...] = (nn(left[...], right) + got[...].astype(jnp.float32)).astype(out.dtype)


def right_spec(right, tile):
    if right.ndim == 3:
        per = right.shape[2] // tile
        return pl.BlockSpec((1, right.shape[1], tile), lambda t, s: (t // per, 0, t % per))
    return pl.BlockSpec((right.shape[0], tile), lambda t, s: (0, t))


def away_rows(index, left_t, right, tile):
    rows = left_t.shape[1]
    half = left_t.shape[0] // 2
    count = right.size // rows
    return pl.pallas_call(
        away_kernel,
        grid_spec=pltpu.PrefetchScalarGridSpec(
            num_scalar_prefetch=1,
            grid=(count // tile,),
            in_specs=[
                pl.BlockSpec((half, rows), lambda t, s: (s[0], 0)),
                right_spec(right, tile),
            ],
            out_specs=pl.BlockSpec((half, tile), lambda t, s: (0, t)),
        ),
        out_shape=shape((half, count), jnp.bfloat16),
        compiler_params=limit(48),
        cost_estimate=cost(2 * half * rows * count, 2 * rows * count + 2 * half * count),
        name="away_rows",
    )(index, left_t, right)


def keep_rows(index, left_t, right, got, tile):
    rows = left_t.shape[1]
    block = left_t.shape[0] // 4
    count = right.size // rows
    out = pl.BlockSpec((block, tile), lambda t, s: (0, t))
    return pl.pallas_call(
        keep_kernel,
        grid_spec=pltpu.PrefetchScalarGridSpec(
            num_scalar_prefetch=1,
            grid=(count // tile,),
            in_specs=[
                pl.BlockSpec((block, rows), lambda t, s: (s[1], 0)),
                pl.BlockSpec((block, rows), lambda t, s: (s[2], 0)),
                right_spec(right, tile),
                pl.BlockSpec((block, tile), lambda t, s: (s[3], t)),
                pl.BlockSpec((block, tile), lambda t, s: (1 - s[3], t)),
            ],
            out_specs=[out, out],
        ),
        out_shape=[shape((block, count), jnp.bfloat16)] * 2,
        compiler_params=limit(48),
        cost_estimate=cost(4 * block * rows * count, 2 * rows * count + 8 * block * count),
        name="keep_rows",
    )(index, left_t, left_t, right, got, got)


def keep_columns_kernel(index_ref, left_ref, right_a_ref, right_b_ref, ra_ref, rb_ref, oa_ref, ob_ref):
    left = left_ref[...]
    for right, got, out in ((right_a_ref, ra_ref, oa_ref), (right_b_ref, rb_ref, ob_ref)):
        out[...] = (nn(left, right[...]) + got[...].astype(jnp.float32)).astype(out.dtype)


def away_columns(index, left_t, right, tile):
    height, rows = left_t.shape
    half = right.shape[1] // 2
    per = half // tile
    return pl.pallas_call(
        away_kernel,
        grid_spec=pltpu.PrefetchScalarGridSpec(
            num_scalar_prefetch=1,
            grid=(per,),
            in_specs=[
                pl.BlockSpec((height, rows), lambda t, s: (0, 0)),
                pl.BlockSpec((rows, tile), lambda t, s: (0, s[0] * per + t)),
            ],
            out_specs=pl.BlockSpec((height, tile), lambda t, s: (0, t)),
        ),
        out_shape=shape((height, half), jnp.bfloat16),
        compiler_params=limit(48),
        cost_estimate=cost(2 * height * rows * half, 2 * rows * half + 2 * height * half),
        name="away_columns",
    )(index, left_t, right)


def keep_columns(index, left_t, right, got, tile):
    height, rows = left_t.shape
    block = right.shape[1] // 4
    per = block // tile
    out = pl.BlockSpec((height, tile), lambda t, s: (0, t))
    return pl.pallas_call(
        keep_columns_kernel,
        grid_spec=pltpu.PrefetchScalarGridSpec(
            num_scalar_prefetch=1,
            grid=(per,),
            in_specs=[
                pl.BlockSpec((height, rows), lambda t, s: (0, 0)),
                pl.BlockSpec((rows, tile), lambda t, s: (0, s[1] * per + t)),
                pl.BlockSpec((rows, tile), lambda t, s: (0, s[2] * per + t)),
                pl.BlockSpec((height, tile), lambda t, s: (0, s[3] * per + t)),
                pl.BlockSpec((height, tile), lambda t, s: (0, (1 - s[3]) * per + t)),
            ],
            out_specs=[out, out],
        ),
        out_shape=[shape((height, block), jnp.bfloat16)] * 2,
        compiler_params=limit(48),
        cost_estimate=cost(4 * height * rows * block, 4 * rows * block + 8 * height * block),
        name="keep_columns",
    )(index, left_t, right, right, got, got)


def input_kernel(*refs):
    grads, weights, (attn_ref, out_ref, acc) = refs[:3], refs[3:6], refs[6:]
    step = pl.program_id(0)

    @pl.when(step == 0)
    def _():
        acc[...] = attn_ref[...]

    grad = jnp.concatenate([ref[0] for ref in grads], axis=1)
    weight = jnp.concatenate([ref[0] for ref in weights], axis=0)
    acc[...] += nn(grad, weight)

    @pl.when(step == pl.num_programs(0) - 1)
    def _():
        out_ref[...] = acc[...].astype(out_ref.dtype)


def input_rows_of(parts, qkv_t, grad_attn):
    rows = grad_attn.shape[0]
    wide = parts[0].shape[2]
    fixed = lambda i: (0, 0)
    weights = qkv_t.reshape(3, DIM, DIM)
    return pl.pallas_call(
        input_kernel,
        grid=(3,),
        in_specs=[pl.BlockSpec((1, rows, wide), lambda i: (i, 0, 0))] * 3
        + [
            pl.BlockSpec((1, wide, DIM), functools.partial(lambda at, i: (i, at, 0), at))
            for at in range(3)
        ]
        + [pl.BlockSpec((rows, DIM), fixed)],
        out_specs=pl.BlockSpec((rows, DIM), fixed),
        out_shape=shape((rows, DIM), jnp.bfloat16),
        scratch_shapes=[pltpu.VMEM((rows, DIM), jnp.float32)],
        compiler_params=limit(48),
        cost_estimate=cost(6 * rows * DIM * DIM, 14 * rows * DIM),
        name="input_rows",
    )(*parts, weights, weights, weights, grad_attn)


CHUNK = DIM
WIDE = 2 * DIM


def halves(values):
    high = values.astype(jnp.bfloat16)
    return high, (values - high.astype(jnp.float32)).astype(jnp.bfloat16)


def exact_product(product, small, large):
    small_high, small_low = halves(small)
    large_high, large_low = halves(large)
    both = product(jnp.concatenate([small_high, small_low], axis=0), large_high)
    return both[:RANK] + both[RANK:] + product(small_high, large_low)


def merge_main_kernel(
    owner_ref, fs_ref, ff_ref, ss_ref, sf_ref, os_ref, of_ref,
    eg_ref, eo_ref, tg_ref, to_ref, mg_ref, mo_ref, p_ref,
):
    f32 = jnp.float32
    step = pl.program_id(0)
    rows = mg_ref.shape[0]
    owner = owner_ref[0] == 1
    @pl.when(step == 0)
    def _():
        p_ref[...] = jnp.zeros_like(p_ref)

    @pl.when(step < 4)
    def _():
        second = jnp.where(owner, ss_ref[...].astype(f32), sf_ref[...].astype(f32))
        first = jnp.where(owner, fs_ref[0].astype(f32), ff_ref[0].astype(f32))
        merged = jnp.where(step % 2 == 0, first, second) + eg_ref[0]
        mg_ref[...] = merged
        p_ref[:, :rows] += exact_product(nt, tg_ref[...], merged)

    @pl.when(step == 4)
    def _():
        own = jnp.where(owner, os_ref[...].astype(f32), of_ref[...].astype(f32))
        merged = own + eo_ref[0]
        mo_ref[...] = merged
        p_ref[:, 256 : 256 + rows] = exact_product(nt, to_ref[...], merged)


def merge_main(owner, first, second, err_gate_up, err_out, start_gate_up, start_out):
    rows = err_out.shape[1]
    f32 = jnp.float32
    last = 2 * FF // WIDE - 1
    fixed = lambda i: (0, 0)
    first_spec = pl.BlockSpec((1, rows, WIDE), lambda i: (jnp.minimum(i // 2, 1), 0, 0))
    second_spec = pl.BlockSpec((rows, WIDE), lambda i: (0, jnp.minimum(i // 2, 1)))
    out_spec = pl.BlockSpec((rows, CHUNK), lambda i: (0, 4))
    return pl.pallas_call(
        merge_main_kernel,
        grid=(last + 2,),
        in_specs=[
            pl.BlockSpec(memory_space=pltpu.SMEM),
            first_spec,
            first_spec,
            second_spec,
            second_spec,
            out_spec,
            out_spec,
            pl.BlockSpec((1, rows, WIDE), lambda i: (0, 0, jnp.minimum(i, last))),
            pl.BlockSpec((1, rows, CHUNK), lambda i: (0, 0, 0)),
            pl.BlockSpec((RANK, WIDE), lambda i: (0, jnp.minimum(i, last))),
            pl.BlockSpec((RANK, CHUNK), fixed),
        ],
        out_specs=[
            pl.BlockSpec((rows, WIDE), lambda i: (0, jnp.minimum(i, last))),
            pl.BlockSpec((rows, CHUNK), fixed),
            pl.BlockSpec((RANK, 512), fixed),
        ],
        out_shape=[
            shape((rows, 2 * FF), f32),
            shape((rows, CHUNK), f32),
            shape((RANK, 512), f32),
        ],
        compiler_params=limit(48),
        cost_estimate=cost(60 * rows * 7 * DIM, 14 * rows * 7 * DIM),
        name="merge_main",
    )(owner, *first, *second, *second, err_gate_up, err_out, start_gate_up, start_out)


def merge_down_kernel(owner_ref, s_ref, f_ref, e_ref, t_ref, m_ref, p_ref):
    f32 = jnp.float32
    own = jnp.where(owner_ref[0] == 1, s_ref[...].astype(f32), f_ref[...].astype(f32))
    merged = own.T + e_ref[0]
    m_ref[...] = merged
    p_ref[...] = exact_product(nt, t_ref[...], merged)


def merge_down(owner, own, err, start):
    block = 256
    f32 = jnp.float32
    column = pl.BlockSpec((DIM, block), lambda i: (0, i))
    return pl.pallas_call(
        merge_down_kernel,
        grid=(DIM // block,),
        in_specs=[
            pl.BlockSpec(memory_space=pltpu.SMEM),
            column,
            column,
            pl.BlockSpec((1, block, DIM), lambda i: (0, i, 0)),
            pl.BlockSpec((RANK, DIM), lambda i: (0, 0)),
        ],
        out_specs=[
            pl.BlockSpec((block, DIM), lambda i: (i, 0)),
            pl.BlockSpec((RANK, block), lambda i: (0, i)),
        ],
        out_shape=[shape((DIM, DIM), f32), shape((RANK, DIM), f32)],
        compiler_params=limit(48),
        cost_estimate=cost(60 * DIM * DIM, 12 * DIM * DIM),
        name="merge_down",
    )(owner, *own, err, start)


def merge_qkv_kernel(owner_ref, *refs):
    f32 = jnp.float32
    near, far, (e_ref, t_ref, m_ref, p_ref) = refs[:3], refs[3:6], refs[6:]
    rows = m_ref.shape[0]
    near = jnp.concatenate([ref[...] for ref in near], axis=1).astype(f32)
    far = jnp.concatenate([ref[...] for ref in far], axis=1).astype(f32)
    merged = jnp.where(owner_ref[0] == 1, near, far) + e_ref[0]
    m_ref[...] = merged

    @pl.when(pl.program_id(0) == 0)
    def _():
        p_ref[...] = jnp.zeros_like(p_ref)

    p_ref[:, :rows] += exact_product(nt, t_ref[...], merged)


def merge_qkv(owner, near, far, err, start):
    rows = err.shape[1]
    f32 = jnp.float32
    parts = [
        pl.BlockSpec((rows, 256), functools.partial(lambda at, i: (0, at + i), at))
        for at in (0, 0, 3)
    ]
    return pl.pallas_call(
        merge_qkv_kernel,
        grid=(3,),
        in_specs=[pl.BlockSpec(memory_space=pltpu.SMEM)]
        + parts
        + parts
        + [
            pl.BlockSpec((1, rows, CHUNK), lambda i: (0, 0, i)),
            pl.BlockSpec((RANK, CHUNK), lambda i: (0, i)),
        ],
        out_specs=[
            pl.BlockSpec((rows, CHUNK), lambda i: (0, i)),
            pl.BlockSpec((RANK, 256), lambda i: (0, 0)),
        ],
        out_shape=[shape((rows, 3 * DIM), f32), shape((RANK, 256), f32)],
        compiler_params=limit(48),
        cost_estimate=cost(60 * rows * 3 * DIM, 14 * rows * 3 * DIM),
        name="merge_qkv",
    )(owner, *near, *far, err, start)


def chunk_of(array):
    return WIDE if array.shape[1] == 2 * FF else CHUNK


def chunk_spec(rows, array, first, lead=(), ahead=0):
    chunk = chunk_of(array)
    count = array.shape[1] // chunk
    zeros = tuple(0 for _ in lead)
    return pl.BlockSpec(
        (*lead, rows, chunk),
        lambda i: (*zeros, 0, jnp.clip(i - first, 0, count - 1) + ahead // chunk),
    )


def chunk_starts(arrays):
    starts = [0]
    for array in arrays:
        starts.append(starts[-1] + array.shape[1] // chunk_of(array))
    return starts


def orthonormal_rows(values):
    row = lax.broadcasted_iota(jnp.int32, (RANK, 1), 0)
    for column in range(RANK):
        vector = values[column : column + 1]
        vector = vector * lax.rsqrt(jnp.sum(vector * vector, axis=1, keepdims=True) + 1e-06)
        weights = jnp.sum(values * vector, axis=1, keepdims=True)
        later = values - weights * vector
        values = jnp.where(row > column, later, jnp.where(row == column, vector, values))
    return values


def pull_kernel(left_ref, *refs, segments, starts):
    count = len(segments)
    merged = refs[:count]
    basis_ref, outs = refs[-count - 1], refs[-count:]
    step = pl.program_id(0)

    @pl.when(step == 0)
    def _():
        for start, width in segments:
            part = slice(start, start + (width + 255) // 256 * 256)
            basis_ref[:, part] = orthonormal_rows(left_ref[:, part] * (1.0 / REPS))

    for at, (start, width) in enumerate(segments):

        @pl.when((step >= starts[at]) & (step < starts[at + 1]))
        def _():
            basis = basis_ref[:, start : start + width]
            outs[at][...] = exact_product(nn, basis, merged[at][...]).astype(outs[at].dtype)


def pull(left, merged, segments, ahead=()):
    starts = chunk_starts(merged)
    total = sum(array.size for array in merged)
    fixed = pl.BlockSpec(left.shape, lambda i: (0, 0))
    results = pl.pallas_call(
        functools.partial(pull_kernel, segments=segments, starts=starts),
        grid=(starts[-1],),
        in_specs=[fixed]
        + [chunk_spec(array.shape[0], array, at) for array, at in zip(merged, starts)]
        + [pl.BlockSpec(memory_space=pl.ANY)] * len(ahead),
        out_specs=[fixed] + [chunk_spec(RANK, array, at) for array, at in zip(merged, starts)],
        out_shape=[shape(left.shape, jnp.float32)]
        + [shape((RANK, array.shape[1]), jnp.bfloat16) for array in merged],
        compiler_params=limit(48),
        cost_estimate=cost(48 * total, 4 * total),
        name="pull",
    )(left, *merged, *ahead)
    return results[0], jnp.concatenate(results[1:], axis=1)


def new_errors_kernel(basis_ref, *refs, segments, starts):
    count = len(segments)
    factors, refs = refs[:count], refs[count:]
    step = pl.program_id(0)
    for at, (start, width) in enumerate(segments):
        merged, out = refs[at], refs[count + at]

        @pl.when((step >= starts[at]) & (step < starts[at + 1]))
        def _():
            basis_high, basis_low = halves(basis_ref[:, start : start + width])
            factor_high, factor_low = halves(factors[at][...])
            left = jnp.concatenate([basis_high, basis_low, basis_high], axis=0)
            right = jnp.concatenate([factor_high, factor_high, factor_low], axis=0)
            approx = lax.dot_general(
                left, right, (((0,), (0,)), ((), ())), preferred_element_type=jnp.float32
            )
            out[0] = merged[...] - approx


def new_errors_of(bases, factors, merged, segments):
    starts = chunk_starts(merged)
    total = sum(array.size for array in merged)
    places = [0]
    for array in merged:
        places.append(places[-1] + array.shape[1])
    return pl.pallas_call(
        functools.partial(new_errors_kernel, segments=segments, starts=starts),
        grid=(starts[-1],),
        in_specs=[pl.BlockSpec(bases.shape, lambda i: (0, 0))]
        + [
            chunk_spec(RANK, array, at, (), place)
            for array, at, place in zip(merged, starts, places)
        ]
        + [chunk_spec(array.shape[0], array, at) for array, at in zip(merged, starts)],
        out_specs=[
            chunk_spec(array.shape[0], array, at, (1,)) for array, at in zip(merged, starts)
        ],
        out_shape=[shape((1, *array.shape), jnp.float32) for array in merged],
        compiler_params=limit(48),
        cost_estimate=cost(48 * total, 8 * total),
        name="new_errors",
    )(bases, *[factors] * len(merged), *merged)


def compress(left, merged, segments, masters, moments, rates, rep, ahead=()):
    highest = lax.Precision.HIGHEST
    bases, pulled = pull(left, merged, segments, ahead)
    summed = plane_sum_half(pulled) / REPS
    errors = new_errors_of(bases, summed, merged, segments)
    results = []
    at = 0
    for (start, width), block, error, master, moment, rate in zip(
        segments, merged, errors, masters, moments, rates
    ):
        basis = bases[:, start : start + width]
        size = block.shape[1]
        factor = summed[:, at : at + size]
        col_count = master.shape[1]
        piece = lax.dynamic_slice_in_dim(summed, at + rep * col_count, col_count, 1)
        piece = lax.dot_general(basis, piece, (((0,), (0,)), ((), ())), precision=highest)
        moment_new = MOMENTUM * moment + piece
        results.append(
            (master - rate * moment_new, moment_new, error, basis.T, factor.T[None])
        )
        at += size
    return results


def fast_device(
    tokens,
    cotangent,
    lengths,
    w_qkv,
    w_out,
    w_gate_up,
    w_down,
    mom_qkv,
    mom_out,
    mom_gate_up,
    mom_down,
    err_qkv,
    err_out,
    err_gate_up,
    err_down,
    start_qkv,
    start_out,
    start_gate_up,
    start_down,
    layer_norm_gains,
    layer_norm_biases,
    norm_moments,
):
    f32 = jnp.float32
    bf16 = jnp.bfloat16
    rep = lax.axis_index("rep")
    shard = lax.axis_index("shard")
    core = rep % 2
    local_len, width = tokens.shape[1:]
    scale = HD ** (-0.5)

    stays = core == shard // 2

    def spread(values):
        parts = []
        for parity in (0, 1):
            sent = lax.dynamic_index_in_dim(values, (shard + parity) % 2, 0, keepdims=False)
            got = send(sent, spread_move(parity))
            parts.append(jnp.where(stays, sent, got) if parity == 0 else got)
        return parts

    def bring_back(rows):
        first = send(rows[:local_len], gather_move(0))
        first = jnp.where(stays, rows[:local_len], first)
        second = send(rows[local_len:], gather_move(1))
        even = shard % 2 == 0
        return jnp.stack([jnp.where(even, first, second), jnp.where(even, second, first)])

    side = jnp.concatenate(
        [
            w_gate_up.astype(bf16),
            w_down.astype(bf16).T,
            w_out.astype(bf16).T.reshape(24, width),
        ],
        axis=0,
    )
    gathered = lax.all_gather(side, "shard", axis=0)
    qkv_piece = jnp.concatenate(shard_gather(w_qkv.astype(bf16).T, shard), axis=1)
    qkv_near = plane_near(qkv_piece)
    rows_in = jnp.concatenate(spread(tokens), axis=0)
    qkv_far = plane_far(qkv_piece, qkv_near)
    both = jnp.stack([lengths, sibling(lengths)])
    group = shard // 2
    length = both[jnp.where(group == core, 0, 1), shard % 2]
    qkv_others = exchange(qkv_piece, qkv_near, qkv_far)
    inside = jnp.arange(local_len, dtype=jnp.int32)

    def starts_of(k):
        first = 2 * k + shard % 2
        second = 2 * k + 1 - shard % 2
        return [first * local_len, second * local_len]

    place = jnp.stack(
        starts_of(core) + starts_of(1 - core) + [length, jnp.zeros_like(length), local_len + 0 * length]
    ).astype(jnp.int32)
    qkv_t = plane_all(
        qkv_piece, qkv_near, qkv_far, qkv_others, rep, (gathered.reshape(-1, width), place)
    )
    qkv_t = qkv_t.reshape(3 * width, width)
    position = jnp.concatenate([place[0] + inside, place[1] + inside])
    inverse = jnp.exp(
        jnp.arange(HD // 2, dtype=jnp.int32).astype(f32) * (-2.0 * math.log(ROPE_BASE) / HD)
    )
    angle = position.astype(f32)[:, None] * inverse[None, :]
    cosine, sine = jnp.cos(angle), jnp.sin(angle)
    cos = jnp.concatenate([cosine] * 4, axis=1)
    sin = jnp.concatenate([-sine, sine] * 2, axis=1)

    kv = project(rows_in, qkv_t, cos, sin, 1, 2, 1, 1.0)
    kv_other = sibling(kv)
    q = project(rows_in, qkv_t, cos, sin, 0, 1, None, scale)
    out_piece = gathered[:, 288:].reshape(SHARDS, 96, 192).transpose(1, 0, 2)
    piece = jnp.concatenate(
        [
            gathered[:, :192].reshape(width, width),
            out_piece.reshape(96, width),
            gathered[:, 192:288].reshape(384, width),
        ],
        axis=0,
    )
    near = plane_near(piece)
    first = attend(place, q, kv, kv_other, 0, 2)
    second = attend(place, q, kv, kv_other, 2, 2, first)
    near = after(near, second[1])
    far = plane_far(piece, near)
    mix, qx = attend(place, q, kv, kv_other, 4, 2, second)
    others = [sibling(part) for part in (after(piece, second[1]), *near)]
    far = after(far, qx)
    others.append(sibling(jnp.concatenate(far, axis=0)))
    stacked = plane_all(piece, near, far, others, rep)
    cot_in = spread(after(cotangent, stacked))
    hat, rstd = out_norm(mix, stacked, rows_in)
    hidden, factor, normed_half, values = feed_forward(
        hat, layer_norm_gains, layer_norm_biases, stacked
    )
    mixed, grad_second, branch, vec_two = norm_back(
        place, values, layer_norm_gains, layer_norm_biases, cot_in
    )
    mixed_out = bring_back(mixed)

    other = 1 - core
    shard_own = jnp.where((shard == 0) | (shard == 3), 0, 1)
    kept = jnp.where(core == 0, shard_own, 3 - shard_own)
    index = jnp.stack([other, kept, 4 * core + 1 - kept, kept - 2 * core]).astype(jnp.int32)
    owner = core == shard // 2

    def kept_rows(values, at):
        parts = values.reshape(2, 2, -1, values.shape[2])
        return lax.dynamic_index_in_dim(parts, at, 1, keepdims=False).astype(f32)

    near = index[3]

    def core_sum(keep, got):
        mine = (kept_rows(keep, near) + kept_rows(got, near)).astype(bf16)
        theirs = (kept_rows(keep, 1 - near) + kept_rows(got, 1 - near)).astype(bf16)
        return mine, theirs

    def add(mine, pair):
        return (mine.astype(f32) + pair.astype(f32)).astype(bf16)

    branch_t = branch.T
    down_away = away_columns(index, branch_t, hidden, DIM)
    down_got = sibling(down_away)
    normed_t = normed_half.T
    away_1, keep_1, partial = feed_back(
        index, grad_second, branch, factor, stacked, normed_t, 0
    )
    got_1 = sibling(away_1)
    down_mine, down_theirs = keep_columns(index, branch_t, hidden, down_got, DIM)
    down_pair = pair_z(down_theirs)
    first_mine, first_theirs = core_sum(keep_1, got_1)
    first_pair = pair_z(first_theirs)
    away_2, keep_2, grad_attn, grad_attn_half, grad_mix, vec_one = feed_back(
        index, after(partial, down_mine, down_theirs, mixed_out), branch, factor,
        stacked, normed_t, 2, (hat, rstd, layer_norm_gains, stacked),
    )
    got_2 = sibling(away_2)
    mix_t = mix.T
    out_got = sibling(away_rows(index, mix_t, grad_attn_half, DIM))

    def back(grads, kv_set, at, first, count, more=(), skip=0):
        return attend_back(place, qx, kv_set, grads, mix, at, first, count, scale, more, skip)

    def join(pair, single):
        return jnp.concatenate([pair[0], pair[1], single], axis=1)

    vectors = jnp.concatenate([vec_one, vec_two], axis=0)
    second_mine, second_theirs = core_sum(keep_2, got_2)
    out_mine, out_theirs = keep_rows(index, mix_t, grad_attn_half, out_got, DIM)
    second_mine = join(second_mine, out_mine)
    second_theirs = join(second_theirs, out_theirs)
    second_pair = pair_z(second_theirs)
    grads = after(grad_mix, second_mine, second_theirs)
    dq_2, dk_2, dv_2 = back(grads, kv_other, 2, 4, 2)
    other_2 = sibling(dk_2), sibling(dv_2)
    down_sum = add(down_mine, after(down_pair, dq_2))
    down_far = to_owner(down_sum)
    first_sum = add(first_mine, after(first_pair, dq_2))
    first_far = to_owner(first_sum)
    vectors = vectors + pair_z(after(vectors, dq_2))
    grads = after(grads, first_sum, down_sum)
    dq_1, dk_1, dv_1 = back(grads, kv_other, 2, 0, 4)
    other_1 = sibling(dk_1), sibling(dv_1)
    second_sum = add(second_mine, after(second_pair, dq_1))
    second_far = to_owner(second_sum)
    flag = owner.astype(jnp.int32).reshape(1)
    merged_down, left_down = merge_down(
        flag, (down_sum, after(down_far, dq_1)), err_down, start_down[0].T
    )
    tokens_t = rows_in.T

    def away_part(right):
        return away_rows(index, tokens_t, right, 256)

    def keep_part(right, got):
        return keep_rows(index, tokens_t, right, got, 256)

    grads = after(grads, second_sum)
    grads_2 = back(grads, kv, 0, 4, 2, (dq_2, *other_2, cos, sin))
    away_2 = away_part(grads_2)
    got_2 = sibling(away_2)
    vectors = vectors + mirror_z(after(vectors, grads_2))
    grads = after(grads, away_2, first_far, down_far)
    grads_0 = back(grads, kv, 0, 0, 2, (dq_1, *other_1, cos, sin))
    away_0 = away_part(grads_0)
    got_0 = sibling(away_0)
    mine_2, theirs_2 = keep_part(grads_2, after(got_2, away_0))
    mine_0, theirs_0 = keep_part(grads_0, got_0)
    qkv_mine = jnp.concatenate([mine_0, mine_2], axis=1)
    qkv_theirs = jnp.concatenate([theirs_0, theirs_2], axis=1)
    qkv_pair = pair_z(qkv_theirs)
    grads = after(grads, qkv_mine, qkv_theirs, second_far)
    grads_1 = back(grads, kv, 0, 2, 2, (dq_1, *other_1, cos, sin), 2)
    away_1 = away_part(grads_1)
    got_1 = sibling(away_1)
    qkv_sum = add(qkv_mine, after(qkv_pair, away_1))
    qkv_far = to_owner(qkv_sum)
    merged_gate_up, merged_out, left_main = merge_main(
        flag, (first_sum, first_far), (second_sum, after(second_far, qkv_sum)),
        err_gate_up, err_out, start_gate_up[0].T, start_out[0].T,
    )
    packed = jnp.concatenate([left_main, left_down, vectors.reshape(RANK, width // 2)], axis=1)
    packed = plane_sum(packed)
    mine_1, theirs_1 = keep_part(grads_1, after(got_1, left_main))
    pair_1 = pair_z(theirs_1)
    input_rows = input_rows_of(
        (grads_0, grads_1, grads_2), qkv_t, after(grad_attn, mine_1, theirs_1)
    )
    input_grad = bring_back(input_rows)
    sum_1 = add(mine_1, after(pair_1, input_rows))
    far_1 = to_owner(sum_1)

    norm_grad = packed[:, 1280:].reshape(4, width) / REPS
    params = jnp.stack(
        [layer_norm_gains[0], layer_norm_biases[0], layer_norm_gains[1], layer_norm_biases[1]]
    )
    norm_moment_new = MOMENTUM * norm_moments + norm_grad
    norm_new = params - NORM_RATE * norm_moment_new
    early = compress(
        packed[:, :1280],
        (merged_gate_up, merged_out, merged_down),
        ((0, 192), (256, 192), (512, 768)),
        (w_gate_up, w_out, w_down),
        (mom_gate_up, mom_out, mom_down),
        (LEARN_RATES[2], LEARN_RATES[1], LEARN_RATES[3]),
        rep,
    )
    merged_qkv, left_qkv = merge_qkv(
        flag, (qkv_sum, sum_1, qkv_sum), (qkv_far, far_1, qkv_far), err_qkv, start_qkv[0].T
    )
    late = compress(
        plane_sum(left_qkv), (merged_qkv,), ((0, 192),), (w_qkv,), (mom_qkv,),
        LEARN_RATES[:1], rep, (input_grad.reshape(-1, width),),
    )
    results = (late[0], early[1], early[0], early[2])
    new_weights, new_moments, new_errors, bases, factors = zip(*results)
    return (
        mixed_out,
        input_grad.astype(f32),
        *new_weights,
        *new_moments,
        *new_errors,
        *bases,
        *factors,
        norm_moment_new,
        norm_new,
    )


def choose(mesh):
    if mesh.shape["rep"] == REPS and mesh.shape["shard"] == SHARDS:
        return fast_device
    return general_device


def solution(mesh):
    placed = (
        P("rep", "shard", None),
        P("rep", "shard", None),
        P("rep"),
        P("shard", "rep"),
        P("shard", "rep"),
        P("shard", "rep"),
        P("shard", "rep"),
        P("shard", "rep"),
        P("shard", "rep"),
        P("shard", "rep"),
        P("shard", "rep"),
        P("rep", "shard", None),
        P("rep", "shard", None),
        P("rep", "shard", None),
        P("rep", "shard", None),
        P("shard", None, None),
        P("shard", None, None),
        P("shard", None, None),
        P("shard", None, None),
        P(),
        P(),
        P(),
    )
    return jax.shard_map(
        choose(mesh),
        mesh=mesh,
        in_specs=placed,
        out_specs=(
            P("rep", "shard", None),
            P("rep", "shard", None),
            P("shard", "rep"),
            P("shard", "rep"),
            P("shard", "rep"),
            P("shard", "rep"),
            P("shard", "rep"),
            P("shard", "rep"),
            P("shard", "rep"),
            P("shard", "rep"),
            P("rep", "shard", None),
            P("rep", "shard", None),
            P("rep", "shard", None),
            P("rep", "shard", None),
            P("shard", None),
            P("shard", None),
            P("shard", None),
            P("shard", None),
            P("shard", None, None),
            P("shard", None, None),
            P("shard", None, None),
            P("shard", None, None),
            P(),
            P(),
        ),
        check_vma=False,
    )
```

```python
import functools
import math

import jax
import jax.numpy as jnp
from jax import lax
from jax.experimental import pallas as pl
from jax.experimental.pallas import tpu as pltpu
from jax.sharding import PartitionSpec as P

H = 12
HD = 64
FF = 3072


EPS = 1e-05
ROPE_BASE = 1000.0
MOMENTUM = 0.5
LEARN_RATES = (0.002, 0.1, 0.004, 0.002)
NORM_RATE = 0.01
NEG_FILL = -1e30


def norm_components(values_in, gain, bias):
    centre = jnp.mean(values_in, axis=-1, keepdims=True)
    centred = values_in - centre
    spread = jnp.mean(centred * centred, axis=-1, keepdims=True)
    row_rstd = lax.rsqrt(spread + EPS)
    normed = centred * row_rstd
    return (normed * gain + bias, normed, row_rstd)


def norm_reverse_pass(grad_in, normed, row_rstd):
    return row_rstd * (
        grad_in
        - jnp.mean(grad_in, axis=-1, keepdims=True)
        - normed * jnp.mean(grad_in * normed, axis=-1, keepdims=True)
    )


def rotary(values_in, cosine_table, sine_table):
    half_dim = values_in.shape[-1] // 2
    leading_half = values_in[..., :half_dim]
    second_half = values_in[..., half_dim:]
    return jnp.concatenate(
        [
            leading_half * cosine_table - second_half * sine_table,
            second_half * cosine_table + leading_half * sine_table,
        ],
        axis=-1,
    )


def rotary_back(grad_in, cosine_table, sine_table):
    half_dim = grad_in.shape[-1] // 2
    leading_half = grad_in[..., :half_dim]
    second_half = grad_in[..., half_dim:]
    return jnp.concatenate(
        [
            leading_half * cosine_table + second_half * sine_table,
            second_half * cosine_table - leading_half * sine_table,
        ],
        axis=-1,
    )


def orthonormal(factor):
    columns = []
    for column in range(factor.shape[1]):
        vector = factor[:, column]
        for earlier in columns:
            vector = vector - jnp.sum(earlier * vector) * earlier
        vector = vector * lax.rsqrt(jnp.sum(vector * vector) + 1e-06)
        columns.append(vector)
    return jnp.stack(columns, axis=1)


def general_device(
    tokens,
    cotangent,
    lengths,
    w_qkv,
    w_out,
    w_gate_up,
    w_down,
    mom_qkv,
    mom_out,
    mom_gate_up,
    mom_down,
    err_qkv,
    err_out,
    err_gate_up,
    err_down,
    start_qkv,
    start_out,
    start_gate_up,
    start_down,
    layer_norm_gains,
    layer_norm_biases,
    norm_moments,
):
    single_float = jnp.float32
    bf16 = jnp.bfloat16
    wide_cols = (
        lax.all_gather(w_qkv.astype(bf16), "rep", axis=1, tiled=True),
        lax.all_gather(w_out.astype(bf16), "rep", axis=1, tiled=True),
        lax.all_gather(w_gate_up.astype(bf16), "rep", axis=1, tiled=True),
        lax.all_gather(w_down.astype(bf16), "rep", axis=1, tiled=True),
    )
    complete_query_key_value, complete_out_weight, complete_gate_up_weight, complete_down_weight = (
        lax.all_gather(wide_cols[0], "shard", axis=0, tiled=True),
        lax.all_gather(wide_cols[1], "shard", axis=0, tiled=True),
        lax.all_gather(wide_cols[2], "shard", axis=0, tiled=True),
        lax.all_gather(wide_cols[3], "shard", axis=0, tiled=True),
    )
    groups, local_len, model_width = tokens.shape
    shards = lax.axis_size("shard")
    seq_len = local_len * shards
    score_scale = HD ** (-0.5)
    offset = lax.axis_index("shard") * local_len
    position = offset + jnp.arange(local_len, dtype=jnp.int32)
    valid_rows = position[None, :] < lengths[:, None]
    key_keep = jnp.arange(seq_len, dtype=jnp.int32)[None, :] < lengths[:, None]
    inverse = jnp.exp(
        jnp.arange(HD // 2, dtype=jnp.int32).astype(single_float)
        * (-2.0 * math.log(ROPE_BASE) / HD)
    )
    angle = position.astype(single_float)[:, None] * inverse[None, :]
    cosine_table = jnp.cos(angle)[:, None, :]
    sine_table = jnp.sin(angle)[:, None, :]
    query_key_value_rows = jnp.einsum(
        "znk,kb->znb", tokens, complete_query_key_value, preferred_element_type=single_float
    )
    query_key_value_rows = query_key_value_rows.reshape(groups, local_len, 3, H, HD)
    q_half = (
        rotary(query_key_value_rows[:, :, 0], cosine_table, sine_table)
        .astype(bf16)
        .transpose(2, 0, 1, 3)
    )
    k_half = (
        rotary(query_key_value_rows[:, :, 1], cosine_table, sine_table)
        .astype(bf16)
        .transpose(2, 0, 1, 3)
    )
    v_half = query_key_value_rows[:, :, 2].astype(bf16).transpose(2, 0, 1, 3)
    key_all, value_all = (
        lax.all_gather(k_half, "shard", axis=2, tiled=True),
        lax.all_gather(v_half, "shard", axis=2, tiled=True),
    )

    def head_forward(inputs):
        query_h, key_h, value_h = inputs
        scores = (
            jnp.einsum("sqd,skd->sqk", query_h, key_h, preferred_element_type=single_float)
            * score_scale
        )
        scores = jnp.where(key_keep[:, None, :], scores, NEG_FILL)
        row_peak = jnp.max(scores, axis=-1, keepdims=True)
        exp_scores = jnp.exp(scores - row_peak)
        row_total = jnp.sum(exp_scores, axis=-1, keepdims=True)
        attn_probs = (exp_scores / row_total).astype(bf16)
        head_rows = jnp.einsum(
            "sqk,skd->sqd", attn_probs, value_h, preferred_element_type=single_float
        )
        return (head_rows, (row_peak + jnp.log(row_total))[..., 0])

    head_out, log_total = lax.map(head_forward, (q_half, key_all, value_all))
    mix_half = head_out.astype(bf16)
    mixture_rows = mix_half.transpose(1, 2, 0, 3).reshape(groups, local_len, model_width)
    attention_result = jnp.einsum(
        "znk,kb->znb", mixture_rows, complete_out_weight, preferred_element_type=single_float
    )
    attention_normed, attention_standardized, attention_inverse_deviation = norm_components(
        tokens.astype(single_float) + attention_result, layer_norm_gains[0], layer_norm_biases[0]
    )
    leading_half = attention_normed.astype(bf16)
    gate_up_output = jnp.einsum(
        "znk,kb->znb", leading_half, complete_gate_up_weight, preferred_element_type=single_float
    )
    gate_part = gate_up_output[..., :FF]
    up_part = gate_up_output[..., FF:]
    gate_sig = jax.nn.sigmoid(gate_part)
    hidden_state = (gate_part * gate_sig * up_part).astype(bf16)
    residual_branch = jnp.einsum(
        "ckh,hy->cky", hidden_state, complete_down_weight, preferred_element_type=single_float
    )
    feedforward_normed, feedforward_standardized, feedforward_inverse_deviation = norm_components(
        attention_normed + residual_branch, layer_norm_gains[1], layer_norm_biases[1]
    )
    mixed_out = feedforward_normed.astype(bf16)
    output_gradient = cotangent.astype(single_float) * valid_rows[..., None].astype(single_float)
    feedforward_gain = jnp.sum(output_gradient * feedforward_standardized, axis=(0, 1))
    bias_two = jnp.sum(output_gradient, axis=(0, 1))
    trailing_norm_gradient = norm_reverse_pass(
        output_gradient * layer_norm_gains[1],
        feedforward_standardized,
        feedforward_inverse_deviation,
    )
    branch_gradient = trailing_norm_gradient.astype(bf16)
    down_weight_gradient = jnp.einsum(
        "zxi,zxp->ip", hidden_state, branch_gradient, preferred_element_type=single_float
    )
    hidden_gradient = jnp.einsum(
        "gbz,wz->gbw", branch_gradient, complete_down_weight, preferred_element_type=single_float
    )
    grad_gate = hidden_gradient * up_part * gate_sig * (1.0 + gate_part * (1.0 - gate_sig))
    grad_up = hidden_gradient * gate_part * gate_sig
    gate_up_gradient = jnp.concatenate([grad_gate, grad_up], axis=-1).astype(bf16)
    gate_up_weight_gradient = jnp.einsum(
        "vcm,vcb->mb", leading_half, gate_up_gradient, preferred_element_type=single_float
    )
    leading_norm_gradient = (
        jnp.einsum(
            "thi,ci->thc",
            gate_up_gradient,
            complete_gate_up_weight,
            preferred_element_type=single_float,
        )
        + trailing_norm_gradient
    )
    attention_gain = jnp.sum(leading_norm_gradient * attention_standardized, axis=(0, 1))
    bias_one = jnp.sum(leading_norm_gradient, axis=(0, 1))
    attention_gradient = norm_reverse_pass(
        leading_norm_gradient * layer_norm_gains[0],
        attention_standardized,
        attention_inverse_deviation,
    )
    attention_gradient_half = attention_gradient.astype(bf16)
    out_weight_gradient = jnp.einsum(
        "vcm,vcb->mb", mixture_rows, attention_gradient_half, preferred_element_type=single_float
    )
    mixture_gradient = jnp.einsum(
        "thi,ci->thc",
        attention_gradient_half,
        complete_out_weight,
        preferred_element_type=single_float,
    )
    grad_mix_half = (
        mixture_gradient.astype(bf16).reshape(groups, local_len, H, HD).transpose(2, 0, 1, 3)
    )

    def head_back(inputs):
        query_h, key_h, value_h, grad_h, lse_h = inputs
        scores = (
            jnp.einsum("sqd,skd->sqk", query_h, key_h, preferred_element_type=single_float)
            * score_scale
        )
        scores = jnp.where(key_keep[:, None, :], scores, NEG_FILL)
        attn_probs = jnp.exp(scores - lse_h[..., None])
        grad_probs = jnp.einsum(
            "sqd,skd->sqk", grad_h, value_h, preferred_element_type=single_float
        )
        row_delta = jnp.sum(grad_probs * attn_probs, axis=-1, keepdims=True)
        grad_scores = (attn_probs * (grad_probs - row_delta)).astype(bf16)
        grad_query = (
            jnp.einsum("sqk,skd->sqd", grad_scores, key_h, preferred_element_type=single_float)
            * score_scale
        )
        grad_key = (
            jnp.einsum("sqk,sqd->skd", grad_scores, query_h, preferred_element_type=single_float)
            * score_scale
        )
        grad_value = jnp.einsum(
            "sqk,sqd->skd", attn_probs.astype(bf16), grad_h, preferred_element_type=single_float
        )
        return (grad_query, grad_key, grad_value)

    grad_q_heads, key_parts, value_parts = lax.map(
        head_back, (q_half, key_all, value_all, grad_mix_half, log_total)
    )
    grad_k_heads, grad_v_heads = (
        lax.psum_scatter(key_parts, "shard", scatter_dimension=2, tiled=True),
        lax.psum_scatter(value_parts, "shard", scatter_dimension=2, tiled=True),
    )
    grad_q_rows = rotary_back(grad_q_heads.transpose(1, 2, 0, 3), cosine_table, sine_table)
    grad_k_rows = rotary_back(grad_k_heads.transpose(1, 2, 0, 3), cosine_table, sine_table)
    grad_v_rows = grad_v_heads.transpose(1, 2, 0, 3)
    query_key_value_gradient = jnp.stack([grad_q_rows, grad_k_rows, grad_v_rows], axis=2)
    query_key_value_gradient = query_key_value_gradient.reshape(
        groups, local_len, 3 * model_width
    ).astype(bf16)
    query_key_value_weight_gradient = jnp.einsum(
        "vcm,vcb->mb", tokens, query_key_value_gradient, preferred_element_type=single_float
    )
    input_grad = (
        jnp.einsum(
            "thi,ci->thc",
            query_key_value_gradient,
            complete_query_key_value,
            preferred_element_type=single_float,
        )
        + attention_gradient
    )
    owned = (
        lax.psum_scatter(
            query_key_value_weight_gradient.astype(jnp.bfloat16),
            "shard",
            scatter_dimension=0,
            tiled=True,
        ).astype(jnp.float32),
        lax.psum_scatter(
            out_weight_gradient.astype(jnp.bfloat16), "shard", scatter_dimension=0, tiled=True
        ).astype(jnp.float32),
        lax.psum_scatter(
            gate_up_weight_gradient.astype(jnp.bfloat16), "shard", scatter_dimension=0, tiled=True
        ).astype(jnp.float32),
        lax.psum_scatter(
            down_weight_gradient.astype(jnp.bfloat16), "shard", scatter_dimension=0, tiled=True
        ).astype(jnp.float32),
    )
    replicas = lax.axis_size("rep")
    vector_parts = jnp.stack([attention_gain, bias_one, feedforward_gain, bias_two])
    norm_grad = lax.psum(vector_parts, ("rep", "shard")) / replicas
    params = jnp.stack(
        [layer_norm_gains[0], layer_norm_biases[0], layer_norm_gains[1], layer_norm_biases[1]]
    )
    norm_moment_new = MOMENTUM * norm_moments + norm_grad
    norm_new = params - NORM_RATE * norm_moment_new
    errors = (err_qkv, err_out, err_gate_up, err_down)
    starts = (start_qkv, start_out, start_gate_up, start_down)
    masters = (w_qkv, w_out, w_gate_up, w_down)
    moments = (mom_qkv, mom_out, mom_gate_up, mom_down)
    merged = tuple((part + error_set[0] for part, error_set in zip(owned, errors)))
    projected = tuple(
        (
            jnp.dot(block, start_set[0], precision=lax.Precision.HIGHEST)
            for block, start_set in zip(merged, starts)
        )
    )
    summed_left = lax.psum((projected[0], projected[1], projected[2], projected[3]), "rep")
    bases = tuple((orthonormal(part / replicas) for part in summed_left))
    pulled = tuple(
        (
            jnp.einsum("rc,rk->ck", block, basis, precision=lax.Precision.HIGHEST)
            for block, basis in zip(merged, bases)
        )
    )
    summed_right = (
        lax.psum(pulled[0].astype(jnp.bfloat16), "rep").astype(jnp.float32),
        lax.psum(pulled[1].astype(jnp.bfloat16), "rep").astype(jnp.float32),
        lax.psum(pulled[2].astype(jnp.bfloat16), "rep").astype(jnp.float32),
        lax.psum(pulled[3].astype(jnp.bfloat16), "rep").astype(jnp.float32),
    )
    factors = tuple((part / replicas for part in summed_right))
    rep_pos = lax.axis_index("rep")
    new_weights = []
    new_moments = []
    new_errors = []
    for block, basis, factor, master, moment, step_rate in zip(
        merged, bases, factors, masters, moments, LEARN_RATES
    ):
        approx = jnp.dot(basis, factor.T, precision=lax.Precision.HIGHEST)
        new_errors.append((block - approx)[None])
        col_count = master.shape[1]
        piece = lax.dynamic_slice_in_dim(approx, rep_pos * col_count, col_count, 1)
        moment_new = MOMENTUM * moment + piece
        new_moments.append(moment_new)
        new_weights.append(master - step_rate * moment_new)
    return (
        mixed_out,
        input_grad,
        new_weights[0],
        new_weights[1],
        new_weights[2],
        new_weights[3],
        new_moments[0],
        new_moments[1],
        new_moments[2],
        new_moments[3],
        new_errors[0],
        new_errors[1],
        new_errors[2],
        new_errors[3],
        bases[0],
        bases[1],
        bases[2],
        bases[3],
        factors[0][None],
        factors[1][None],
        factors[2][None],
        factors[3][None],
        norm_moment_new,
        norm_new,
    )


AXES = ("rep", "shard")
SHARDS = 4
REPS = 8
RANK = 8
DIM = 768
PAIRS = 6
LANES = 128
MIB = 2**20


def send(values, move):
    pairs = []
    for rep in range(REPS):
        for shard in range(SHARDS):
            to = move(rep, shard)
            if to is not None and to != (rep, shard):
                pairs.append((rep * SHARDS + shard, to[0] * SHARDS + to[1]))
    return lax.ppermute(values, AXES, pairs)


def spread_move(parity):
    return lambda r, z: (r - r % 2 + z // 2, 2 * (r % 2) + (z + parity) % 2)


def gather_move(parity):
    table = {}
    for r in range(REPS):
        for z in range(SHARDS):
            table[spread_move(parity)(r, z)] = (r, z)
    return lambda r, z: table[(r, z)]


def sibling(values):
    return send(values, lambda r, z: (r ^ 1, z))


def near_x(values):
    return send(values, lambda r, z: (r ^ 2, z))


def near_y(values):
    return send(values, lambda r, z: (r ^ 4, z))


def pair_z(values):
    return send(values, lambda r, z: (r, z ^ 1))


def mirror_z(values):
    return send(values, lambda r, z: (r, 3 - z))


def to_owner(values):
    return send(values, lambda r, z: (r ^ 1, 3 - z) if r % 2 != z // 2 else None)


def turn_z(values, step):
    return send(values, lambda r, z: (r, (z + step) % SHARDS))


def after(values, *others):
    return lax.optimization_barrier((values, *others))[0]


def shard_gather(piece, shard):
    parts = jnp.stack([piece] + [turn_z(piece, step) for step in (1, 2, 3)])
    return [
        lax.dynamic_index_in_dim(parts, (shard - at) % SHARDS, 0, keepdims=False)
        for at in range(SHARDS)
    ]


def plane_near(piece):
    return near_x(piece), near_y(piece)


def plane_far(piece, near):
    half = piece.shape[0] // 2
    from_x, from_y = near
    return near_x(from_y[:half]), near_y(from_x[half:])


def exchange(piece, near, far):
    near = jnp.concatenate(near, axis=0)
    return [sibling(part) for part in (piece, near, jnp.concatenate(far, axis=0))]


def plane_all(piece, near, far, others, rep, ahead=()):
    offsets = [0] * len(PIECE_STEPS)
    if len(others) == 3:
        own, both, opposite = others
        others = own, both, both, opposite
        offsets[7] = piece.shape[0]
    return stack_pieces(
        (piece, *near, *far, *others), rep, *piece.shape, ahead, tuple(offsets)
    )


PIECE_STEPS = ((0, None), (2, None), (4, None), (6, 0), (6, 1), (1, None), (3, None), (5, None), (7, None))


def stack_kernel(rep_ref, *refs, offsets):
    count = len(PIECE_STEPS)
    pieces = refs[:count]
    whole, staged, sems_in, sems_out = refs[-4:]
    rep = rep_ref[0]
    half = pieces[3].shape[0]
    fetches = []
    stores = []
    for slot, (step, side) in enumerate(PIECE_STEPS):
        stage = staged.at[step]
        place = whole.at[rep ^ step]
        if side is not None:
            part = pl.ds(side * half, half)
            stage = stage.at[part]
            place = place.at[part]
        source = pieces[slot].at[pl.ds(offsets[slot], stage.shape[0])]
        fetches.append(pltpu.make_async_copy(source, stage, sems_in.at[slot]))
        stores.append(pltpu.make_async_copy(stage, place, sems_out.at[slot]))
    for fetch in fetches:
        fetch.start()
    for fetch, store in zip(fetches, stores):
        fetch.wait()
        store.start()
    for store in stores:
        store.wait()


def stack_pieces(pieces, rep, rows, cols, ahead, offsets):
    anywhere = pl.BlockSpec(memory_space=pl.ANY)
    count = len(pieces)
    return pl.pallas_call(
        functools.partial(stack_kernel, offsets=offsets),
        in_specs=[pl.BlockSpec(memory_space=pltpu.SMEM)] + [anywhere] * (count + len(ahead)),
        out_specs=anywhere,
        out_shape=jax.ShapeDtypeStruct((REPS, rows, cols), pieces[0].dtype),
        scratch_shapes=[
            pltpu.VMEM((REPS, rows, cols), pieces[0].dtype),
            pltpu.SemaphoreType.DMA((count,)),
            pltpu.SemaphoreType.DMA((count,)),
        ],
        compiler_params=limit(40),
        cost_estimate=pl.CostEstimate(
            flops=0, bytes_accessed=4 * REPS * rows * cols, transcendentals=0
        ),
        name="stack_pieces",
    )(jnp.reshape(rep, (1,)), *pieces, *ahead)


def plane_sum(values):
    values = values + sibling(values)
    values = values + near_x(values)
    return values + near_y(values)


def plane_sum_half(values):
    bf16 = jnp.bfloat16
    f32 = jnp.float32
    for step in (sibling, near_x, near_y):
        rounded = values.astype(bf16)
        values = rounded.astype(f32) + step(rounded).astype(f32)
    return values


def nt(left, right):
    return lax.dot_general(
        left, right, (((1,), (1,)), ((), ())), preferred_element_type=jnp.float32
    )


def nn(left, right):
    return lax.dot_general(
        left, right, (((1,), (0,)), ((), ())), preferred_element_type=jnp.float32
    )


def cost(flops, moved, powers=0):
    return pl.CostEstimate(flops=int(flops), bytes_accessed=int(moved), transcendentals=int(powers))


def limit(mib):
    return pltpu.CompilerParams(vmem_limit_bytes=mib * MIB)


def shape(dims, dtype):
    return jax.ShapeDtypeStruct(dims, dtype)


def partner_lanes(values):
    lane = lax.broadcasted_iota(jnp.int32, values.shape, 1)
    up = pltpu.roll(values, 96, 1)
    down = pltpu.roll(values, 32, 1)
    return jnp.where(lane % HD < HD // 2, up, down)


def project_kernel(x_ref, w_ref, cos_ref, sin_ref, *refs, turned, scale):
    out_ref = refs[-1]
    values = nt(x_ref[...], w_ref[...])

    def turn():
        for at in range(0, values.shape[1], LANES):
            part = values[:, at : at + LANES]
            part = part * cos_ref[...] + partner_lanes(part) * sin_ref[...]
            out_ref[:, at : at + LANES] = (part * scale).astype(out_ref.dtype)

    if turned is None:
        turn()
    else:
        pl.when(pl.program_id(0) < turned)(turn)

        @pl.when(pl.program_id(0) >= turned)
        def _():
            out_ref[...] = values.astype(out_ref.dtype)


def project(rows_in, qkv_t, cos, sin, first, count, turned, scale, ahead=()):
    rows = rows_in.shape[0]
    tile = DIM
    fixed = lambda j: (0, 0)
    return pl.pallas_call(
        functools.partial(project_kernel, turned=turned, scale=scale),
        grid=(count,),
        in_specs=[
            pl.BlockSpec((rows, DIM), fixed),
            pl.BlockSpec((tile, DIM), lambda j: (j + first, 0)),
            pl.BlockSpec((rows, LANES), fixed),
            pl.BlockSpec((rows, LANES), fixed),
        ]
        + [pl.BlockSpec(memory_space=pl.ANY)] * len(ahead),
        out_specs=pl.BlockSpec((rows, tile), lambda j: (0, j)),
        out_shape=shape((rows, count * tile), jnp.bfloat16),
        compiler_params=limit(48),
        cost_estimate=cost(2 * rows * DIM * tile * count, 4 * rows * DIM + 4 * count * tile * rows),
        name="project",
    )(rows_in, qkv_t, cos, sin, *ahead)


def lane_of(dims):
    return lax.broadcasted_iota(jnp.int32, dims, 1)


def head_lanes(dims, head):
    lane = lane_of(dims)
    return (lane >= HD) if head else (lane < HD)


def extra_lane(head):
    return 0 if head else HD


def key_fill(place_ref, at, count, start):
    row = lax.broadcasted_iota(jnp.int32, (count, LANES), 0) + start
    half = place_ref[6]
    position = jnp.where(row < half, place_ref[at] + row, place_ref[at + 1] + row - half)
    return jnp.where(position < place_ref[4], 0.0, NEG_FILL).astype(jnp.bfloat16)


def attend_kernel(place_ref, q_ref, ka_ref, va_ref, kb_ref, vb_ref, *refs):
    mix_ref, qx_ref, keys, values = refs[-4:]
    rows = ka_ref.shape[0]
    bf16 = jnp.bfloat16

    @pl.when(pl.program_id(1) == 0)
    def _():
        dims = (rows, LANES)
        zero = jnp.zeros(dims, bf16)
        for source, (k_ref, v_ref) in enumerate(((ka_ref, va_ref), (kb_ref, vb_ref))):
            fill = key_fill(place_ref, 2 * source, rows, 0)
            part = pl.ds(source * rows, rows)
            for head in range(2):
                inside = head_lanes(dims, head)
                other = jnp.where(lane_of(dims) == extra_lane(head), fill, zero)
                keys[head, part] = jnp.where(inside, k_ref[...], other)
                values[head, part] = jnp.where(inside, v_ref[...], zero)

    queries = q_ref[...]
    dims = queries.shape
    lane = lane_of(dims)
    total = None
    for head in range(2):
        inside = head_lanes(dims, head)
        spare = lane - extra_lane(head)
        one = jnp.where(spare == 0, 1.0, 0.0).astype(bf16)
        masked = jnp.where(inside, queries, one)
        scores = nt(masked, keys[head])
        peak = jnp.max(scores, axis=1, keepdims=True)
        powers = jnp.exp(scores - peak)
        row_sum = jnp.sum(powers, axis=1, keepdims=True)
        out = nn(powers.astype(bf16), values[head]) / row_sum
        total = out if total is None else total + out
        lse = peak + jnp.log(row_sum)
        high = lse.astype(bf16)
        middle = (lse - high.astype(jnp.float32)).astype(bf16)
        low = (lse - high.astype(jnp.float32) - middle.astype(jnp.float32)).astype(bf16)
        wide = jnp.where(spare == 1, -high, jnp.where(spare == 2, -middle, -low))
        wide = jnp.where((spare >= 1) & (spare <= 3), wide, one)
        qx_ref[:, head * LANES : (head + 1) * LANES] = jnp.where(inside, queries, wide)
    mix_ref[...] = total.astype(bf16)


def attend(place, q, kv_own, kv_other, first, count, done=()):
    rows = q.shape[0]
    block = 256
    bf16 = jnp.bfloat16
    key_spec = pl.BlockSpec((rows, LANES), lambda p, i: (0, p + first))
    value_spec = pl.BlockSpec((rows, LANES), lambda p, i: (0, p + first + PAIRS))
    return pl.pallas_call(
        attend_kernel,
        grid=(count, rows // block),
        in_specs=[
            pl.BlockSpec(memory_space=pltpu.SMEM),
            pl.BlockSpec((block, LANES), lambda p, i: (i, p + first)),
            key_spec,
            value_spec,
            key_spec,
            value_spec,
        ]
        + [pl.BlockSpec(memory_space=pl.ANY)] * len(done),
        out_specs=[
            pl.BlockSpec((block, LANES), lambda p, i: (i, p + first)),
            pl.BlockSpec((block, 2 * LANES), lambda p, i: (i, p + first)),
        ],
        out_shape=[shape((rows, DIM), bf16), shape((rows, 2 * DIM), bf16)],
        scratch_shapes=[
            pltpu.VMEM((2, 2 * rows, LANES), bf16),
            pltpu.VMEM((2, 2 * rows, LANES), bf16),
        ],
        input_output_aliases={6: 0, 7: 1} if done else {},
        compiler_params=limit(48),
        cost_estimate=cost(
            64 * count * rows * 2 * rows * HD, 32 * rows * LANES * count, 2 * count * rows * 2 * rows
        ),
        name="attend",
    )(place, q, kv_own, kv_own, kv_other, kv_other, *done)


def attend_back_kernel(place_ref, qx_ref, k_ref, v_ref, g_ref, mix_ref, *refs, at, scale):
    bf16 = jnp.bfloat16
    f32 = jnp.float32
    last = at == 0
    if last:
        dq_ref, got_k_ref, got_v_ref, cos_ref, sin_ref, out_ref, gx, g0, q0, acc = refs
    else:
        dq_ref, dk_ref, dv_ref, gx, g0, q0, acc = refs
    rows = g_ref.shape[0]
    count = k_ref.shape[0]
    step = pl.program_id(1)

    @pl.when(step == 0)
    def _():
        dims = (rows, LANES)
        lane = lane_of(dims)
        grad = g_ref[...]
        product = grad.astype(f32) * mix_ref[...].astype(f32)
        zero = jnp.zeros(dims, bf16)
        for head in range(2):
            inside = head_lanes(dims, head)
            spare = lane - extra_lane(head)
            delta = jnp.sum(jnp.where(inside, product, 0.0), axis=1, keepdims=True)
            high = delta.astype(bf16)
            middle = (delta - high.astype(f32)).astype(bf16)
            low = (delta - high.astype(f32) - middle.astype(f32)).astype(bf16)
            wide = jnp.where(spare == 1, -high, jnp.where(spare == 2, -middle, -low))
            wide = jnp.where((spare >= 1) & (spare <= 3), wide, zero)
            gx[head] = jnp.where(inside, grad, wide)
            g0[head] = jnp.where(inside, grad, zero)
            q0[head] = jnp.where(inside, qx_ref[:, head * LANES : (head + 1) * LANES], zero)
        acc[...] = jnp.zeros_like(acc)

    keys = k_ref[...]
    values = v_ref[...]
    dims = keys.shape
    lane = lane_of(dims)
    fill = key_fill(place_ref, at, count, step * count)
    keys_t = keys.astype(f32).T.astype(bf16)
    dk = None
    dv = None
    for head in range(2):
        inside = head_lanes(dims, head)
        spare = lane - extra_lane(head)
        ones = jnp.where((spare >= 1) & (spare <= 3), 1.0, 0.0).astype(bf16)
        keys_x = jnp.where(inside, keys, jnp.where(spare == 0, fill, ones))
        values_x = jnp.where(inside, values, ones)
        scores = nt(keys_x, qx_ref[:, head * LANES : (head + 1) * LANES])
        probs = jnp.exp(scores)
        dv_head = nn(probs.astype(bf16), g0[head])
        grad_probs = nt(values_x, gx[head])
        grad_scores = (probs * grad_probs).astype(bf16)
        dk_head = nn(grad_scores, q0[head])
        part = slice(head * HD, (head + 1) * HD)
        acc[part] += nn(keys_t[part], grad_scores)
        dk = dk_head if dk is None else dk + dk_head
        dv = dv_head if dv is None else dv + dv_head
    if last:
        here = pl.ds(pl.multiple_of(step * count, count), count)
        dk = dk + got_k_ref[...].astype(f32)
        dk = dk * cos_ref[here] - partner_lanes(dk) * sin_ref[here]
        out_ref[1, here] = dk.astype(bf16)
        out_ref[2, here] = (dv + got_v_ref[...].astype(f32)).astype(bf16)
    else:
        dk_ref[...] = dk.astype(bf16)
        dv_ref[...] = dv.astype(bf16)

    @pl.when(step == pl.num_programs(1) - 1)
    def _():
        dq = acc[...].T
        if last:
            dq = (dq + dq_ref[...]) * scale
            dq = dq * cos_ref[...] - partner_lanes(dq) * sin_ref[...]
            out_ref[0] = dq.astype(bf16)
        else:
            dq_ref[...] = dq


def attend_back(place, qx, kv, grad, mix, at, first, count, scale, more=(), skip=0):
    rows = grad.shape[0]
    block = 512
    bf16 = jnp.bfloat16
    wide = pl.BlockSpec((rows, LANES), lambda p, j: (0, p + first))
    here = pl.BlockSpec((rows, LANES), lambda p, j: (0, p))
    keys = pl.BlockSpec((block, LANES), lambda p, j: (j, p))
    table = pl.BlockSpec((rows, LANES), lambda p, j: (0, 0))
    dims = (rows, count * LANES)
    if at == 0:
        ahead = pl.BlockSpec((rows, LANES), lambda p, j: (0, p + skip))
        ahead_keys = pl.BlockSpec((block, LANES), lambda p, j: (j, p + skip))
        more_specs = [ahead, ahead_keys, ahead_keys, table, table]
        out_specs = pl.BlockSpec((3, rows, LANES), lambda p, j: (0, 0, p))
        out_shape = shape((3, *dims), bf16)
    else:
        more_specs = []
        out_specs = [here, keys, keys]
        out_shape = [shape(dims, jnp.float32), shape(dims, bf16), shape(dims, bf16)]
    return pl.pallas_call(
        functools.partial(attend_back_kernel, at=at, scale=scale),
        grid=(count, rows // block),
        in_specs=[
            pl.BlockSpec(memory_space=pltpu.SMEM),
            pl.BlockSpec((rows, 2 * LANES), lambda p, j: (0, p + first)),
            pl.BlockSpec((block, LANES), lambda p, j: (j, p + first)),
            pl.BlockSpec((block, LANES), lambda p, j: (j, p + first + PAIRS)),
            wide,
            wide,
        ]
        + more_specs,
        out_specs=out_specs,
        out_shape=out_shape,
        scratch_shapes=[
            pltpu.VMEM((2, rows, LANES), bf16),
            pltpu.VMEM((2, rows, LANES), bf16),
            pltpu.VMEM((2, rows, LANES), bf16),
            pltpu.VMEM((LANES, rows), jnp.float32),
        ],
        compiler_params=limit(48),
        cost_estimate=cost(
            80 * count * rows * rows * HD, 40 * count * rows * LANES, 2 * count * rows * rows
        ),
        name="attend_back",
    )(place, qx, kv, kv, grad, mix, *more)


def row_mean(values):
    return jnp.sum(values, axis=1, keepdims=True) * (1.0 / DIM)


def out_norm_kernel(mix_ref, w_ref, x_ref, hat_ref, rstd_ref):
    weight = w_ref[...].reshape(DIM, DIM)
    values = x_ref[...].astype(jnp.float32) + nt(mix_ref[...], weight)
    centred = values - row_mean(values)
    rstd = lax.rsqrt(row_mean(centred * centred) + EPS)
    hat_ref[...] = centred * rstd
    rstd_ref[...] = jnp.broadcast_to(rstd, rstd_ref.shape)


def out_norm(mix, stacked, rows_in):
    rows = mix.shape[0]
    block = 256
    spec = pl.BlockSpec((block, DIM), lambda i: (i, 0))
    return pl.pallas_call(
        out_norm_kernel,
        grid=(rows // block,),
        in_specs=[spec, pl.BlockSpec((REPS, 96, DIM), lambda i: (0, 8, 0)), spec],
        out_specs=[spec, pl.BlockSpec((block, LANES), lambda i: (i, 0))],
        out_shape=[shape((rows, DIM), jnp.float32), shape((rows, LANES), jnp.float32)],
        compiler_params=limit(48),
        cost_estimate=cost(2 * rows * DIM * DIM, 8 * rows * DIM),
        name="out_norm",
    )(mix, stacked, rows_in)


FF_TILE = 256
SUB = DIM // FF_TILE
FF_PIECES = FF // DIM


def row_parts(ref):
    half = ref.shape[0] // 2
    return [pl.ds(0, half), pl.ds(half, half)]


def sub_lanes():
    return pl.ds(pl.multiple_of(pl.program_id(1) * FF_TILE, FF_TILE), FF_TILE)


def at_step(piece, sub):
    return (pl.program_id(0) == piece) & (pl.program_id(1) == sub)


def feed_forward_kernel(
    hat_ref,
    gains_ref,
    biases_ref,
    wg_ref,
    wu_ref,
    wd_ref,
    hidden_ref,
    factor_ref,
    half_ref,
    acc,
    gate_s,
    up_s,
):
    bf16 = jnp.bfloat16
    f32 = jnp.float32
    step = pl.program_id(0)

    @pl.when(step == 0)
    def _():
        normed = hat_ref[...] * gains_ref[0:1] + biases_ref[0:1]
        acc[...] = normed
        half_ref[...] = normed.astype(bf16)
        gate_s[...] = jnp.zeros_like(gate_s)
        up_s[...] = jnp.zeros_like(up_s)

    gate = gate_s[...]
    up = up_s[...]
    sig = 1.0 / (1.0 + jnp.exp(-gate))
    act = gate * sig
    hidden = (act * up).astype(bf16)
    hidden_ref[...] = hidden
    factor_ref[0] = (up * sig * (1.0 + gate - act)).astype(bf16)
    factor_ref[1] = act.astype(bf16)
    rows_in = half_ref[...]
    gate_s[...] = nn(rows_in, wg_ref[0])
    up_s[...] = nn(rows_in, wu_ref[0])
    acc[...] += nt(hidden, wd_ref[...].reshape(DIM, FF_TILE))


def feed_forward(hat, gains, biases, stacked):
    rows = hat.shape[0]
    bf16 = jnp.bfloat16
    f32 = jnp.float32
    fixed = lambda t: (0, 0)
    whole = pl.BlockSpec((rows, DIM), fixed)
    small = pl.BlockSpec((2, DIM), fixed)
    tiles = FF_PIECES * SUB

    def now(t):
        return jnp.minimum(t, tiles - 1)

    def before(t):
        return jnp.maximum(t - 1, 0)

    return pl.pallas_call(
        feed_forward_kernel,
        grid=(tiles + 1,),
        in_specs=[
            whole,
            small,
            small,
            pl.BlockSpec((1, DIM, FF_TILE), lambda t: (now(t) // SUB, 0, now(t) % SUB)),
            pl.BlockSpec((1, DIM, FF_TILE), lambda t: (now(t) // SUB + FF_PIECES, 0, now(t) % SUB)),
            pl.BlockSpec(
                (REPS, 96, FF_TILE), lambda t: (0, before(t) // SUB + 9, before(t) % SUB)
            ),
        ],
        out_specs=[
            pl.BlockSpec((rows, FF_TILE), lambda t: (0, before(t))),
            pl.BlockSpec((2, rows, FF_TILE), lambda t: (0, 0, before(t))),
            whole,
            whole,
        ],
        out_shape=[
            shape((rows, FF), bf16),
            shape((2, rows, FF), bf16),
            shape((rows, DIM), bf16),
            shape((rows, DIM), f32),
        ],
        scratch_shapes=[
            pltpu.VMEM((rows, FF_TILE), f32),
            pltpu.VMEM((rows, FF_TILE), f32),
        ],
        compiler_params=limit(60),
        cost_estimate=cost(6 * rows * DIM * FF, 6 * rows * FF + 6 * DIM * FF, rows * FF),
        name="feed_forward",
    )(hat, gains, biases, stacked, stacked, stacked)


def norm_back_kernel(
    place_ref, values_ref, gains_ref, biases_ref, cot_a_ref, cot_b_ref,
    mixed_ref, grad_ref, branch_ref, vec_ref,
):
    bf16 = jnp.bfloat16
    f32 = jnp.float32
    step = pl.program_id(0)
    second = step >= pl.num_programs(0) // 2
    values = values_ref[...]
    rows = values.shape[0]
    centred = values - row_mean(values)
    rstd = lax.rsqrt(row_mean(centred * centred) + EPS)
    hat = centred * rstd
    mixed_ref[...] = (hat * gains_ref[1:2] + biases_ref[1:2]).astype(bf16)
    row = lax.broadcasted_iota(jnp.int32, (rows, 1), 0) + step * rows
    half = place_ref[6]
    position = jnp.where(row < half, place_ref[0] + row, place_ref[1] + row - half)
    cot = jnp.where(second, cot_b_ref[...].astype(f32), cot_a_ref[...].astype(f32))
    grad = jnp.where(position < place_ref[4], cot, 0.0)

    @pl.when(step == 0)
    def _():
        vec_ref[...] = jnp.zeros_like(vec_ref)

    vec_ref[0:1] += jnp.sum(grad * hat, axis=0, keepdims=True)
    vec_ref[1:2] += jnp.sum(grad, axis=0, keepdims=True)
    grad = grad * gains_ref[1:2]
    grad = rstd * (grad - row_mean(grad) - hat * row_mean(grad * hat))
    grad_ref[...] = grad
    branch_ref[...] = grad.astype(bf16)


def norm_back(place, values, gains, biases, cot):
    rows = values.shape[0]
    block = 256
    half = rows // block // 2
    f32 = jnp.float32
    bf16 = jnp.bfloat16
    spec = pl.BlockSpec((block, DIM), lambda i: (i, 0))
    small = pl.BlockSpec((2, DIM), lambda i: (0, 0))
    return pl.pallas_call(
        norm_back_kernel,
        grid=(rows // block,),
        in_specs=[
            pl.BlockSpec(memory_space=pltpu.SMEM),
            spec,
            small,
            small,
            pl.BlockSpec((block, DIM), lambda i: (jnp.minimum(i, half - 1), 0)),
            pl.BlockSpec((block, DIM), lambda i: (jnp.maximum(i - half, 0), 0)),
        ],
        out_specs=[spec, spec, spec, small],
        out_shape=[
            shape((rows, DIM), bf16),
            shape((rows, DIM), f32),
            shape((rows, DIM), bf16),
            shape((2, DIM), f32),
        ],
        compiler_params=limit(48),
        cost_estimate=cost(30 * rows * DIM, 14 * rows * DIM),
        name="norm_back",
    )(place, values, gains, biases, *cot)


def feed_back_kernel(
    index_ref,
    grad_ref,
    branch_ref,
    factor_ref,
    wg_ref,
    wu_ref,
    wd_ref,
    left_away_ref,
    left_keep_ref,
    *refs,
):
    bf16 = jnp.bfloat16
    f32 = jnp.float32
    last = len(refs) > 6
    if last:
        hat_ref, rstd_ref, gains_ref, wo_ref, away_ref, keep_ref = refs[:6]
        attn_ref, attn_half_ref, mix_grad_ref, vec_ref, acc, both, left = refs[6:]
    else:
        away_ref, keep_ref, acc_ref, acc, both, left = refs
    half_rows = left_away_ref.shape[0]
    here = sub_lanes()

    @pl.when(at_step(0, 0))
    def _():
        acc[...] = grad_ref[...]
        left[:half_rows] = left_away_ref[...]
        left[half_rows:] = left_keep_ref[...]

    grad_hidden = nn(branch_ref[...], wd_ref[...].reshape(DIM, FF_TILE))
    for side in range(2):
        grad = (grad_hidden * factor_ref[side].astype(f32)).astype(bf16)
        both[side, :, here] = grad
        product = nn(left[...], grad).astype(bf16)
        away_ref[side] = product[:half_rows]
        keep_ref[side] = product[half_rows:]

    @pl.when(pl.program_id(1) == SUB - 1)
    def _():
        acc[...] += nt(both[0], wg_ref[0]) + nt(both[1], wu_ref[0])

    @pl.when(at_step(pl.num_programs(0) - 1, SUB - 1))
    def _():
        grad = acc[...]
        if not last:
            acc_ref[...] = grad
            return
        hat = hat_ref[...]
        vec_ref[0:1] = jnp.sum(grad * hat, axis=0, keepdims=True)
        vec_ref[1:2] = jnp.sum(grad, axis=0, keepdims=True)
        grad = grad * gains_ref[0:1]
        rstd = rstd_ref[:, 0:1]
        grad = rstd * (grad - row_mean(grad) - hat * row_mean(grad * hat))
        attn_ref[...] = grad
        half = grad.astype(bf16)
        attn_half_ref[...] = half
        mix_grad_ref[...] = nn(half, wo_ref[...].reshape(DIM, DIM)).astype(bf16)


def feed_back(index, grad, branch, factor, stacked, normed_t, first, more=()):
    rows = grad.shape[0]
    bf16 = jnp.bfloat16
    f32 = jnp.float32
    fixed = lambda j, i, s: (0, 0)
    whole = pl.BlockSpec((rows, DIM), fixed)
    small = pl.BlockSpec((2, DIM), fixed)
    pieces = FF_PIECES // 2
    count = pieces * DIM
    parts = pl.BlockSpec((2, DIM // 2, FF_TILE), lambda j, i, s: (0, 0, SUB * j + i))
    in_specs = [
        whole,
        whole,
        pl.BlockSpec((2, rows, FF_TILE), lambda j, i, s: (0, 0, SUB * (j + first) + i)),
        pl.BlockSpec((1, DIM, DIM), lambda j, i, s: (j + first, 0, 0)),
        pl.BlockSpec((1, DIM, DIM), lambda j, i, s: (j + first + FF_PIECES, 0, 0)),
        pl.BlockSpec((REPS, 96, FF_TILE), lambda j, i, s: (0, j + first + 9, i)),
        pl.BlockSpec((DIM // 2, rows), lambda j, i, s: (s[0], 0)),
        pl.BlockSpec((DIM // 2, rows), lambda j, i, s: (1 - s[0], 0)),
    ]
    out_specs = [parts, parts]
    out_shape = [shape((2, DIM // 2, count), bf16)] * 2
    if more:
        in_specs += [
            whole,
            pl.BlockSpec((rows, LANES), fixed),
            small,
            pl.BlockSpec((REPS, 96, DIM), lambda j, i, s: (0, 8, 0)),
        ]
        out_specs += [whole, whole, whole, small]
        out_shape += [
            shape((rows, DIM), f32),
            shape((rows, DIM), bf16),
            shape((rows, DIM), bf16),
            shape((2, DIM), f32),
        ]
    else:
        out_specs += [whole]
        out_shape += [shape((rows, DIM), f32)]
    return pl.pallas_call(
        feed_back_kernel,
        grid_spec=pltpu.PrefetchScalarGridSpec(
            num_scalar_prefetch=1,
            grid=(pieces, SUB),
            in_specs=in_specs,
            out_specs=out_specs,
            scratch_shapes=[
                pltpu.VMEM((rows, DIM), f32),
                pltpu.VMEM((2, rows, DIM), bf16),
                pltpu.VMEM((DIM, rows), bf16),
            ],
        ),
        out_shape=out_shape,
        compiler_params=limit(60),
        cost_estimate=cost(10 * rows * DIM * count, 4 * rows * count + 10 * DIM * count),
        name="feed_back",
    )(index, grad, branch, factor, stacked, stacked, stacked, normed_t, normed_t, *more)


def away_kernel(index_ref, left_ref, right_ref, out_ref):
    right = right_ref[0] if len(right_ref.shape) == 3 else right_ref[...]
    out_ref[...] = nn(left_ref[...], right).astype(out_ref.dtype)


def keep_kernel(index_ref, la_ref, lb_ref, right_ref, ra_ref, rb_ref, out_a_ref, out_b_ref):
    right = right_ref[0] if len(right_ref.shape) == 3 else right_ref[...]
    for left, got, out in ((la_ref, ra_ref, out_a_ref), (lb_ref, rb_ref, out_b_ref)):
        out[...] = (nn(left[...], right) + got[...].astype(jnp.float32)).astype(out.dtype)


def right_spec(right, tile):
    if right.ndim == 3:
        per = right.shape[2] // tile
        return pl.BlockSpec((1, right.shape[1], tile), lambda t, s: (t // per, 0, t % per))
    return pl.BlockSpec((right.shape[0], tile), lambda t, s: (0, t))


def away_rows(index, left_t, right, tile):
    rows = left_t.shape[1]
    half = left_t.shape[0] // 2
    count = right.size // rows
    return pl.pallas_call(
        away_kernel,
        grid_spec=pltpu.PrefetchScalarGridSpec(
            num_scalar_prefetch=1,
            grid=(count // tile,),
            in_specs=[
                pl.BlockSpec((half, rows), lambda t, s: (s[0], 0)),
                right_spec(right, tile),
            ],
            out_specs=pl.BlockSpec((half, tile), lambda t, s: (0, t)),
        ),
        out_shape=shape((half, count), jnp.bfloat16),
        compiler_params=limit(48),
        cost_estimate=cost(2 * half * rows * count, 2 * rows * count + 2 * half * count),
        name="away_rows",
    )(index, left_t, right)


def keep_rows(index, left_t, right, got, tile):
    rows = left_t.shape[1]
    block = left_t.shape[0] // 4
    count = right.size // rows
    out = pl.BlockSpec((block, tile), lambda t, s: (0, t))
    return pl.pallas_call(
        keep_kernel,
        grid_spec=pltpu.PrefetchScalarGridSpec(
            num_scalar_prefetch=1,
            grid=(count // tile,),
            in_specs=[
                pl.BlockSpec((block, rows), lambda t, s: (s[1], 0)),
                pl.BlockSpec((block, rows), lambda t, s: (s[2], 0)),
                right_spec(right, tile),
                pl.BlockSpec((block, tile), lambda t, s: (s[3], t)),
                pl.BlockSpec((block, tile), lambda t, s: (1 - s[3], t)),
            ],
            out_specs=[out, out],
        ),
        out_shape=[shape((block, count), jnp.bfloat16)] * 2,
        compiler_params=limit(48),
        cost_estimate=cost(4 * block * rows * count, 2 * rows * count + 8 * block * count),
        name="keep_rows",
    )(index, left_t, left_t, right, got, got)


def keep_columns_kernel(index_ref, left_ref, right_a_ref, right_b_ref, ra_ref, rb_ref, oa_ref, ob_ref):
    left = left_ref[...]
    for right, got, out in ((right_a_ref, ra_ref, oa_ref), (right_b_ref, rb_ref, ob_ref)):
        out[...] = (nn(left, right[...]) + got[...].astype(jnp.float32)).astype(out.dtype)


def away_columns(index, left_t, right, tile):
    height, rows = left_t.shape
    half = right.shape[1] // 2
    per = half // tile
    return pl.pallas_call(
        away_kernel,
        grid_spec=pltpu.PrefetchScalarGridSpec(
            num_scalar_prefetch=1,
            grid=(per,),
            in_specs=[
                pl.BlockSpec((height, rows), lambda t, s: (0, 0)),
                pl.BlockSpec((rows, tile), lambda t, s: (0, s[0] * per + t)),
            ],
            out_specs=pl.BlockSpec((height, tile), lambda t, s: (0, t)),
        ),
        out_shape=shape((height, half), jnp.bfloat16),
        compiler_params=limit(48),
        cost_estimate=cost(2 * height * rows * half, 2 * rows * half + 2 * height * half),
        name="away_columns",
    )(index, left_t, right)


def keep_columns(index, left_t, right, got, tile):
    height, rows = left_t.shape
    block = right.shape[1] // 4
    per = block // tile
    out = pl.BlockSpec((height, tile), lambda t, s: (0, t))
    return pl.pallas_call(
        keep_columns_kernel,
        grid_spec=pltpu.PrefetchScalarGridSpec(
            num_scalar_prefetch=1,
            grid=(per,),
            in_specs=[
                pl.BlockSpec((height, rows), lambda t, s: (0, 0)),
                pl.BlockSpec((rows, tile), lambda t, s: (0, s[1] * per + t)),
                pl.BlockSpec((rows, tile), lambda t, s: (0, s[2] * per + t)),
                pl.BlockSpec((height, tile), lambda t, s: (0, s[3] * per + t)),
                pl.BlockSpec((height, tile), lambda t, s: (0, (1 - s[3]) * per + t)),
            ],
            out_specs=[out, out],
        ),
        out_shape=[shape((height, block), jnp.bfloat16)] * 2,
        compiler_params=limit(48),
        cost_estimate=cost(4 * height * rows * block, 4 * rows * block + 8 * height * block),
        name="keep_columns",
    )(index, left_t, right, right, got, got)


def input_kernel(*refs):
    grads, weights, (attn_ref, out_ref, acc) = refs[:3], refs[3:6], refs[6:]
    step = pl.program_id(0)

    @pl.when(step == 0)
    def _():
        acc[...] = attn_ref[...]

    grad = jnp.concatenate([ref[0] for ref in grads], axis=1)
    weight = jnp.concatenate([ref[0] for ref in weights], axis=0)
    acc[...] += nn(grad, weight)

    @pl.when(step == pl.num_programs(0) - 1)
    def _():
        out_ref[...] = acc[...].astype(out_ref.dtype)


def input_rows_of(parts, qkv_t, grad_attn):
    rows = grad_attn.shape[0]
    wide = parts[0].shape[2]
    fixed = lambda i: (0, 0)
    weights = qkv_t.reshape(3, DIM, DIM)
    return pl.pallas_call(
        input_kernel,
        grid=(3,),
        in_specs=[pl.BlockSpec((1, rows, wide), lambda i: (i, 0, 0))] * 3
        + [
            pl.BlockSpec((1, wide, DIM), functools.partial(lambda at, i: (i, at, 0), at))
            for at in range(3)
        ]
        + [pl.BlockSpec((rows, DIM), fixed)],
        out_specs=pl.BlockSpec((rows, DIM), fixed),
        out_shape=shape((rows, DIM), jnp.bfloat16),
        scratch_shapes=[pltpu.VMEM((rows, DIM), jnp.float32)],
        compiler_params=limit(48),
        cost_estimate=cost(6 * rows * DIM * DIM, 14 * rows * DIM),
        name="input_rows",
    )(*parts, weights, weights, weights, grad_attn)


CHUNK = DIM
WIDE = 2 * DIM


def halves(values):
    high = values.astype(jnp.bfloat16)
    return high, (values - high.astype(jnp.float32)).astype(jnp.bfloat16)


def exact_product(product, small, large):
    small_high, small_low = halves(small)
    large_high, large_low = halves(large)
    both = product(jnp.concatenate([small_high, small_low], axis=0), large_high)
    return both[:RANK] + both[RANK:] + product(small_high, large_low)


def merge_main_kernel(
    owner_ref, fs_ref, ff_ref, ss_ref, sf_ref, os_ref, of_ref,
    eg_ref, eo_ref, tg_ref, to_ref, mg_ref, mo_ref, p_ref,
):
    f32 = jnp.float32
    step = pl.program_id(0)
    rows = mg_ref.shape[0]
    owner = owner_ref[0] == 1
    @pl.when(step == 0)
    def _():
        p_ref[...] = jnp.zeros_like(p_ref)

    @pl.when(step < 4)
    def _():
        second = jnp.where(owner, ss_ref[...].astype(f32), sf_ref[...].astype(f32))
        first = jnp.where(owner, fs_ref[0].astype(f32), ff_ref[0].astype(f32))
        merged = jnp.where(step % 2 == 0, first, second) + eg_ref[0]
        mg_ref[...] = merged
        p_ref[:, :rows] += exact_product(nt, tg_ref[...], merged)

    @pl.when(step == 4)
    def _():
        own = jnp.where(owner, os_ref[...].astype(f32), of_ref[...].astype(f32))
        merged = own + eo_ref[0]
        mo_ref[...] = merged
        p_ref[:, 256 : 256 + rows] = exact_product(nt, to_ref[...], merged)


def merge_main(owner, first, second, err_gate_up, err_out, start_gate_up, start_out):
    rows = err_out.shape[1]
    f32 = jnp.float32
    last = 2 * FF // WIDE - 1
    fixed = lambda i: (0, 0)
    first_spec = pl.BlockSpec((1, rows, WIDE), lambda i: (jnp.minimum(i // 2, 1), 0, 0))
    second_spec = pl.BlockSpec((rows, WIDE), lambda i: (0, jnp.minimum(i // 2, 1)))
    out_spec = pl.BlockSpec((rows, CHUNK), lambda i: (0, 4))
    return pl.pallas_call(
        merge_main_kernel,
        grid=(last + 2,),
        in_specs=[
            pl.BlockSpec(memory_space=pltpu.SMEM),
            first_spec,
            first_spec,
            second_spec,
            second_spec,
            out_spec,
            out_spec,
            pl.BlockSpec((1, rows, WIDE), lambda i: (0, 0, jnp.minimum(i, last))),
            pl.BlockSpec((1, rows, CHUNK), lambda i: (0, 0, 0)),
            pl.BlockSpec((RANK, WIDE), lambda i: (0, jnp.minimum(i, last))),
            pl.BlockSpec((RANK, CHUNK), fixed),
        ],
        out_specs=[
            pl.BlockSpec((rows, WIDE), lambda i: (0, jnp.minimum(i, last))),
            pl.BlockSpec((rows, CHUNK), fixed),
            pl.BlockSpec((RANK, 512), fixed),
        ],
        out_shape=[
            shape((rows, 2 * FF), f32),
            shape((rows, CHUNK), f32),
            shape((RANK, 512), f32),
        ],
        compiler_params=limit(48),
        cost_estimate=cost(60 * rows * 7 * DIM, 14 * rows * 7 * DIM),
        name="merge_main",
    )(owner, *first, *second, *second, err_gate_up, err_out, start_gate_up, start_out)


def merge_down_kernel(owner_ref, s_ref, f_ref, e_ref, t_ref, m_ref, p_ref):
    f32 = jnp.float32
    own = jnp.where(owner_ref[0] == 1, s_ref[...].astype(f32), f_ref[...].astype(f32))
    merged = own.T + e_ref[0]
    m_ref[...] = merged
    p_ref[...] = exact_product(nt, t_ref[...], merged)


def merge_down(owner, own, err, start):
    block = 256
    f32 = jnp.float32
    column = pl.BlockSpec((DIM, block), lambda i: (0, i))
    return pl.pallas_call(
        merge_down_kernel,
        grid=(DIM // block,),
        in_specs=[
            pl.BlockSpec(memory_space=pltpu.SMEM),
            column,
            column,
            pl.BlockSpec((1, block, DIM), lambda i: (0, i, 0)),
            pl.BlockSpec((RANK, DIM), lambda i: (0, 0)),
        ],
        out_specs=[
            pl.BlockSpec((block, DIM), lambda i: (i, 0)),
            pl.BlockSpec((RANK, block), lambda i: (0, i)),
        ],
        out_shape=[shape((DIM, DIM), f32), shape((RANK, DIM), f32)],
        compiler_params=limit(48),
        cost_estimate=cost(60 * DIM * DIM, 12 * DIM * DIM),
        name="merge_down",
    )(owner, *own, err, start)


def merge_qkv_kernel(owner_ref, *refs):
    f32 = jnp.float32
    near, far, (e_ref, t_ref, m_ref, p_ref) = refs[:3], refs[3:6], refs[6:]
    rows = m_ref.shape[0]
    near = jnp.concatenate([ref[...] for ref in near], axis=1).astype(f32)
    far = jnp.concatenate([ref[...] for ref in far], axis=1).astype(f32)
    merged = jnp.where(owner_ref[0] == 1, near, far) + e_ref[0]
    m_ref[...] = merged

    @pl.when(pl.program_id(0) == 0)
    def _():
        p_ref[...] = jnp.zeros_like(p_ref)

    p_ref[:, :rows] += exact_product(nt, t_ref[...], merged)


def merge_qkv(owner, near, far, err, start):
    rows = err.shape[1]
    f32 = jnp.float32
    parts = [
        pl.BlockSpec((rows, 256), functools.partial(lambda at, i: (0, at + i), at))
        for at in (0, 0, 3)
    ]
    return pl.pallas_call(
        merge_qkv_kernel,
        grid=(3,),
        in_specs=[pl.BlockSpec(memory_space=pltpu.SMEM)]
        + parts
        + parts
        + [
            pl.BlockSpec((1, rows, CHUNK), lambda i: (0, 0, i)),
            pl.BlockSpec((RANK, CHUNK), lambda i: (0, i)),
        ],
        out_specs=[
            pl.BlockSpec((rows, CHUNK), lambda i: (0, i)),
            pl.BlockSpec((RANK, 256), lambda i: (0, 0)),
        ],
        out_shape=[shape((rows, 3 * DIM), f32), shape((RANK, 256), f32)],
        compiler_params=limit(48),
        cost_estimate=cost(60 * rows * 3 * DIM, 14 * rows * 3 * DIM),
        name="merge_qkv",
    )(owner, *near, *far, err, start)


def chunk_of(array):
    return WIDE if array.shape[1] == 2 * FF else CHUNK


def chunk_spec(rows, array, first, lead=(), ahead=0):
    chunk = chunk_of(array)
    count = array.shape[1] // chunk
    zeros = tuple(0 for _ in lead)
    return pl.BlockSpec(
        (*lead, rows, chunk),
        lambda i: (*zeros, 0, jnp.clip(i - first, 0, count - 1) + ahead // chunk),
    )


def chunk_starts(arrays):
    starts = [0]
    for array in arrays:
        starts.append(starts[-1] + array.shape[1] // chunk_of(array))
    return starts


def orthonormal_rows(values):
    row = lax.broadcasted_iota(jnp.int32, (RANK, 1), 0)
    for column in range(RANK):
        vector = values[column : column + 1]
        vector = vector * lax.rsqrt(jnp.sum(vector * vector, axis=1, keepdims=True) + 1e-06)
        weights = jnp.sum(values * vector, axis=1, keepdims=True)
        later = values - weights * vector
        values = jnp.where(row > column, later, jnp.where(row == column, vector, values))
    return values


def pull_kernel(left_ref, *refs, segments, starts):
    count = len(segments)
    merged = refs[:count]
    basis_ref, outs = refs[-count - 1], refs[-count:]
    step = pl.program_id(0)

    @pl.when(step == 0)
    def _():
        for start, width in segments:
            part = slice(start, start + (width + 255) // 256 * 256)
            basis_ref[:, part] = orthonormal_rows(left_ref[:, part] * (1.0 / REPS))

    for at, (start, width) in enumerate(segments):

        @pl.when((step >= starts[at]) & (step < starts[at + 1]))
        def _():
            basis = basis_ref[:, start : start + width]
            outs[at][...] = exact_product(nn, basis, merged[at][...]).astype(outs[at].dtype)


def pull(left, merged, segments, ahead=()):
    starts = chunk_starts(merged)
    total = sum(array.size for array in merged)
    fixed = pl.BlockSpec(left.shape, lambda i: (0, 0))
    results = pl.pallas_call(
        functools.partial(pull_kernel, segments=segments, starts=starts),
        grid=(starts[-1],),
        in_specs=[fixed]
        + [chunk_spec(array.shape[0], array, at) for array, at in zip(merged, starts)]
        + [pl.BlockSpec(memory_space=pl.ANY)] * len(ahead),
        out_specs=[fixed] + [chunk_spec(RANK, array, at) for array, at in zip(merged, starts)],
        out_shape=[shape(left.shape, jnp.float32)]
        + [shape((RANK, array.shape[1]), jnp.bfloat16) for array in merged],
        compiler_params=limit(48),
        cost_estimate=cost(48 * total, 4 * total),
        name="pull",
    )(left, *merged, *ahead)
    return results[0], jnp.concatenate(results[1:], axis=1)


def new_errors_kernel(basis_ref, *refs, segments, starts):
    count = len(segments)
    factors, refs = refs[:count], refs[count:]
    step = pl.program_id(0)
    for at, (start, width) in enumerate(segments):
        merged, out = refs[at], refs[count + at]

        @pl.when((step >= starts[at]) & (step < starts[at + 1]))
        def _():
            basis_high, basis_low = halves(basis_ref[:, start : start + width])
            factor_high, factor_low = halves(factors[at][...])
            left = jnp.concatenate([basis_high, basis_low, basis_high], axis=0)
            right = jnp.concatenate([factor_high, factor_high, factor_low], axis=0)
            approx = lax.dot_general(
                left, right, (((0,), (0,)), ((), ())), preferred_element_type=jnp.float32
            )
            out[0] = merged[...] - approx


def new_errors_of(bases, factors, merged, segments):
    starts = chunk_starts(merged)
    total = sum(array.size for array in merged)
    places = [0]
    for array in merged:
        places.append(places[-1] + array.shape[1])
    return pl.pallas_call(
        functools.partial(new_errors_kernel, segments=segments, starts=starts),
        grid=(starts[-1],),
        in_specs=[pl.BlockSpec(bases.shape, lambda i: (0, 0))]
        + [
            chunk_spec(RANK, array, at, (), place)
            for array, at, place in zip(merged, starts, places)
        ]
        + [chunk_spec(array.shape[0], array, at) for array, at in zip(merged, starts)],
        out_specs=[
            chunk_spec(array.shape[0], array, at, (1,)) for array, at in zip(merged, starts)
        ],
        out_shape=[shape((1, *array.shape), jnp.float32) for array in merged],
        compiler_params=limit(48),
        cost_estimate=cost(48 * total, 8 * total),
        name="new_errors",
    )(bases, *[factors] * len(merged), *merged)


def compress(left, merged, segments, masters, moments, rates, rep, ahead=()):
    highest = lax.Precision.HIGHEST
    bases, pulled = pull(left, merged, segments, ahead)
    summed = plane_sum_half(pulled) / REPS
    errors = new_errors_of(bases, summed, merged, segments)
    results = []
    at = 0
    for (start, width), block, error, master, moment, rate in zip(
        segments, merged, errors, masters, moments, rates
    ):
        basis = bases[:, start : start + width]
        size = block.shape[1]
        factor = summed[:, at : at + size]
        col_count = master.shape[1]
        piece = lax.dynamic_slice_in_dim(summed, at + rep * col_count, col_count, 1)
        piece = lax.dot_general(basis, piece, (((0,), (0,)), ((), ())), precision=highest)
        moment_new = MOMENTUM * moment + piece
        results.append(
            (master - rate * moment_new, moment_new, error, basis.T, factor.T[None])
        )
        at += size
    return results


def fast_device(
    tokens,
    cotangent,
    lengths,
    w_qkv,
    w_out,
    w_gate_up,
    w_down,
    mom_qkv,
    mom_out,
    mom_gate_up,
    mom_down,
    err_qkv,
    err_out,
    err_gate_up,
    err_down,
    start_qkv,
    start_out,
    start_gate_up,
    start_down,
    layer_norm_gains,
    layer_norm_biases,
    norm_moments,
):
    f32 = jnp.float32
    bf16 = jnp.bfloat16
    rep = lax.axis_index("rep")
    shard = lax.axis_index("shard")
    core = rep % 2
    local_len, width = tokens.shape[1:]
    scale = HD ** (-0.5)

    stays = core == shard // 2

    def spread(values):
        parts = []
        for parity in (0, 1):
            sent = lax.dynamic_index_in_dim(values, (shard + parity) % 2, 0, keepdims=False)
            got = send(sent, spread_move(parity))
            parts.append(jnp.where(stays, sent, got) if parity == 0 else got)
        return parts

    def bring_back(rows):
        first = send(rows[:local_len], gather_move(0))
        first = jnp.where(stays, rows[:local_len], first)
        second = send(rows[local_len:], gather_move(1))
        even = shard % 2 == 0
        return jnp.stack([jnp.where(even, first, second), jnp.where(even, second, first)])

    side = jnp.concatenate(
        [
            w_gate_up.astype(bf16),
            w_down.astype(bf16).T,
            w_out.astype(bf16).T.reshape(24, width),
        ],
        axis=0,
    )
    gathered = lax.all_gather(side, "shard", axis=0)
    qkv_piece = jnp.concatenate(shard_gather(w_qkv.astype(bf16).T, shard), axis=1)
    qkv_near = plane_near(qkv_piece)
    rows_in = jnp.concatenate(spread(tokens), axis=0)
    qkv_far = plane_far(qkv_piece, qkv_near)
    both = jnp.stack([lengths, sibling(lengths)])
    group = shard // 2
    length = both[jnp.where(group == core, 0, 1), shard % 2]
    qkv_others = exchange(qkv_piece, qkv_near, qkv_far)
    inside = jnp.arange(local_len, dtype=jnp.int32)

    def starts_of(k):
        first = 2 * k + shard % 2
        second = 2 * k + 1 - shard % 2
        return [first * local_len, second * local_len]

    place = jnp.stack(
        starts_of(core) + starts_of(1 - core) + [length, jnp.zeros_like(length), local_len + 0 * length]
    ).astype(jnp.int32)
    qkv_t = plane_all(
        qkv_piece, qkv_near, qkv_far, qkv_others, rep, (gathered.reshape(-1, width), place)
    )
    qkv_t = qkv_t.reshape(3 * width, width)
    position = jnp.concatenate([place[0] + inside, place[1] + inside])
    inverse = jnp.exp(
        jnp.arange(HD // 2, dtype=jnp.int32).astype(f32) * (-2.0 * math.log(ROPE_BASE) / HD)
    )
    angle = position.astype(f32)[:, None] * inverse[None, :]
    cosine, sine = jnp.cos(angle), jnp.sin(angle)
    cos = jnp.concatenate([cosine] * 4, axis=1)
    sin = jnp.concatenate([-sine, sine] * 2, axis=1)

    kv = project(rows_in, qkv_t, cos, sin, 1, 2, 1, 1.0)
    kv_other = sibling(kv)
    q = project(rows_in, qkv_t, cos, sin, 0, 1, None, scale)
    out_piece = gathered[:, 288:].reshape(SHARDS, 96, 192).transpose(1, 0, 2)
    piece = jnp.concatenate(
        [
            gathered[:, :192].reshape(width, width),
            out_piece.reshape(96, width),
            gathered[:, 192:288].reshape(384, width),
        ],
        axis=0,
    )
    near = plane_near(piece)
    first = attend(place, q, kv, kv_other, 0, 2)
    second = attend(place, q, kv, kv_other, 2, 2, first)
    near = after(near, second[1])
    far = plane_far(piece, near)
    mix, qx = attend(place, q, kv, kv_other, 4, 2, second)
    others = [sibling(part) for part in (after(piece, second[1]), *near)]
    far = after(far, qx)
    others.append(sibling(jnp.concatenate(far, axis=0)))
    stacked = plane_all(piece, near, far, others, rep)
    cot_in = spread(after(cotangent, stacked))
    hat, rstd = out_norm(mix, stacked, rows_in)
    hidden, factor, normed_half, values = feed_forward(
        hat, layer_norm_gains, layer_norm_biases, stacked
    )
    mixed, grad_second, branch, vec_two = norm_back(
        place, values, layer_norm_gains, layer_norm_biases, cot_in
    )
    mixed_out = bring_back(mixed)

    other = 1 - core
    shard_own = jnp.where((shard == 0) | (shard == 3), 0, 1)
    kept = jnp.where(core == 0, shard_own, 3 - shard_own)
    index = jnp.stack([other, kept, 4 * core + 1 - kept, kept - 2 * core]).astype(jnp.int32)
    owner = core == shard // 2

    def kept_rows(values, at):
        parts = values.reshape(2, 2, -1, values.shape[2])
        return lax.dynamic_index_in_dim(parts, at, 1, keepdims=False).astype(f32)

    near = index[3]

    def core_sum(keep, got):
        mine = (kept_rows(keep, near) + kept_rows(got, near)).astype(bf16)
        theirs = (kept_rows(keep, 1 - near) + kept_rows(got, 1 - near)).astype(bf16)
        return mine, theirs

    def add(mine, pair):
        return (mine.astype(f32) + pair.astype(f32)).astype(bf16)

    branch_t = branch.T
    down_away = away_columns(index, branch_t, hidden, DIM)
    down_got = sibling(down_away)
    normed_t = normed_half.T
    away_1, keep_1, partial = feed_back(
        index, grad_second, branch, factor, stacked, normed_t, 0
    )
    got_1 = sibling(away_1)
    down_mine, down_theirs = keep_columns(index, branch_t, hidden, down_got, DIM)
    down_pair = pair_z(down_theirs)
    first_mine, first_theirs = core_sum(keep_1, got_1)
    first_pair = pair_z(first_theirs)
    away_2, keep_2, grad_attn, grad_attn_half, grad_mix, vec_one = feed_back(
        index, after(partial, down_mine, down_theirs, mixed_out), branch, factor,
        stacked, normed_t, 2, (hat, rstd, layer_norm_gains, stacked),
    )
    got_2 = sibling(away_2)
    mix_t = mix.T
    out_got = sibling(away_rows(index, mix_t, grad_attn_half, DIM))

    def back(grads, kv_set, at, first, count, more=(), skip=0):
        return attend_back(place, qx, kv_set, grads, mix, at, first, count, scale, more, skip)

    def join(pair, single):
        return jnp.concatenate([pair[0], pair[1], single], axis=1)

    vectors = jnp.concatenate([vec_one, vec_two], axis=0)
    second_mine, second_theirs = core_sum(keep_2, got_2)
    out_mine, out_theirs = keep_rows(index, mix_t, grad_attn_half, out_got, DIM)
    second_mine = join(second_mine, out_mine)
    second_theirs = join(second_theirs, out_theirs)
    second_pair = pair_z(second_theirs)
    grads = after(grad_mix, second_mine, second_theirs)
    dq_2, dk_2, dv_2 = back(grads, kv_other, 2, 4, 2)
    other_2 = sibling(dk_2), sibling(dv_2)
    down_sum = add(down_mine, after(down_pair, dq_2))
    down_far = to_owner(down_sum)
    vectors = vectors + pair_z(after(vectors, dq_2))
    grads = after(grads, down_sum)
    dq_1, dk_1, dv_1 = back(grads, kv_other, 2, 0, 4)
    other_1 = sibling(dk_1), sibling(dv_1)
    first_sum = add(first_mine, after(first_pair, dq_1))
    first_far = to_owner(first_sum)
    second_sum = add(second_mine, after(second_pair, dq_1))
    second_far = to_owner(second_sum)
    flag = owner.astype(jnp.int32).reshape(1)
    merged_down, left_down = merge_down(
        flag, (down_sum, after(down_far, dq_1)), err_down, start_down[0].T
    )
    tokens_t = rows_in.T

    def away_part(right):
        return away_rows(index, tokens_t, right, 256)

    def keep_part(right, got):
        return keep_rows(index, tokens_t, right, got, 256)

    grads = after(grads, first_sum, second_sum)
    grads_2 = back(grads, kv, 0, 4, 2, (dq_2, *other_2, cos, sin))
    away_2 = away_part(grads_2)
    got_2 = sibling(away_2)
    vectors = vectors + mirror_z(after(vectors, grads_2))
    grads = after(grads, away_2, down_far)
    grads_0 = back(grads, kv, 0, 0, 2, (dq_1, *other_1, cos, sin))
    away_0 = away_part(grads_0)
    got_0 = sibling(away_0)
    mine_2, theirs_2 = keep_part(grads_2, after(got_2, away_0))
    mine_0, theirs_0 = keep_part(grads_0, got_0)
    qkv_mine = jnp.concatenate([mine_0, mine_2], axis=1)
    qkv_theirs = jnp.concatenate([theirs_0, theirs_2], axis=1)
    qkv_pair = pair_z(qkv_theirs)
    grads = after(grads, qkv_mine, qkv_theirs, first_far, second_far)
    grads_1 = back(grads, kv, 0, 2, 2, (dq_1, *other_1, cos, sin), 2)
    away_1 = away_part(grads_1)
    got_1 = sibling(away_1)
    qkv_sum = add(qkv_mine, after(qkv_pair, away_1))
    qkv_far = to_owner(qkv_sum)
    input_rows = input_rows_of((grads_0, grads_1, grads_2), qkv_t, after(grad_attn, away_1))
    input_grad = bring_back(input_rows)
    merged_gate_up, merged_out, left_main = merge_main(
        flag, (first_sum, first_far), (second_sum, after(second_far, qkv_sum, input_rows)),
        err_gate_up, err_out, start_gate_up[0].T, start_out[0].T,
    )
    packed = jnp.concatenate([left_main, left_down, vectors.reshape(RANK, width // 2)], axis=1)
    packed = plane_sum(packed)
    mine_1, theirs_1 = keep_part(grads_1, after(got_1, left_main))
    pair_1 = pair_z(theirs_1)
    sum_1 = add(mine_1, pair_1)
    far_1 = to_owner(sum_1)

    norm_grad = packed[:, 1280:].reshape(4, width) / REPS
    params = jnp.stack(
        [layer_norm_gains[0], layer_norm_biases[0], layer_norm_gains[1], layer_norm_biases[1]]
    )
    norm_moment_new = MOMENTUM * norm_moments + norm_grad
    norm_new = params - NORM_RATE * norm_moment_new
    early = compress(
        packed[:, :1280],
        (merged_gate_up, merged_out, merged_down),
        ((0, 192), (256, 192), (512, 768)),
        (w_gate_up, w_out, w_down),
        (mom_gate_up, mom_out, mom_down),
        (LEARN_RATES[2], LEARN_RATES[1], LEARN_RATES[3]),
        rep,
    )
    merged_qkv, left_qkv = merge_qkv(
        flag, (qkv_sum, sum_1, qkv_sum), (qkv_far, far_1, qkv_far), err_qkv, start_qkv[0].T
    )
    late = compress(
        plane_sum(left_qkv), (merged_qkv,), ((0, 192),), (w_qkv,), (mom_qkv,),
        LEARN_RATES[:1], rep, (input_grad.reshape(-1, width),),
    )
    results = (late[0], early[1], early[0], early[2])
    new_weights, new_moments, new_errors, bases, factors = zip(*results)
    return (
        mixed_out,
        input_grad.astype(f32),
        *new_weights,
        *new_moments,
        *new_errors,
        *bases,
        *factors,
        norm_moment_new,
        norm_new,
    )


def choose(mesh):
    if mesh.shape["rep"] == REPS and mesh.shape["shard"] == SHARDS:
        return fast_device
    return general_device


def solution(mesh):
    placed = (
        P("rep", "shard", None),
        P("rep", "shard", None),
        P("rep"),
        P("shard", "rep"),
        P("shard", "rep"),
        P("shard", "rep"),
        P("shard", "rep"),
        P("shard", "rep"),
        P("shard", "rep"),
        P("shard", "rep"),
        P("shard", "rep"),
        P("rep", "shard", None),
        P("rep", "shard", None),
        P("rep", "shard", None),
        P("rep", "shard", None),
        P("shard", None, None),
        P("shard", None, None),
        P("shard", None, None),
        P("shard", None, None),
        P(),
        P(),
        P(),
    )
    return jax.shard_map(
        choose(mesh),
        mesh=mesh,
        in_specs=placed,
        out_specs=(
            P("rep", "shard", None),
            P("rep", "shard", None),
            P("shard", "rep"),
            P("shard", "rep"),
            P("shard", "rep"),
            P("shard", "rep"),
            P("shard", "rep"),
            P("shard", "rep"),
            P("shard", "rep"),
            P("shard", "rep"),
            P("rep", "shard", None),
            P("rep", "shard", None),
            P("rep", "shard", None),
            P("rep", "shard", None),
            P("shard", None),
            P("shard", None),
            P("shard", None),
            P("shard", None),
            P("shard", None, None),
            P("shard", None, None),
            P("shard", None, None),
            P("shard", None, None),
            P(),
            P(),
        ),
        check_vma=False,
    )
```
